32 devices in a mesh: groups: 2 (over y), aux: 16 (over z, x, core).
Axes of the slice: x: 2, y: 2, z: 4, core: 2. Of those that a mesh axis runs over, the one named last changes fastest.
Arguments:
- integrals: bfloat16 [8192, 5, 4096], P(('groups', 'aux')), parts along dimension 0, may hold values from -8 to 8
- block_list: int32 [32, 5], P(('groups', 'aux')), parts along dimension 0, may hold values from 0 to 255
- slot_counts: int32 [32], P(('groups', 'aux')), parts along dimension 0, may hold values from 1 to 5, as said below
- coefficients: bfloat16 [32768, 16], P(('groups', 'aux')), parts along dimension 0, may hold values from -0.3125 to 0.3125
- batch_index: int32 [32], P('groups'), parts along dimension 0, may hold values from 0 to 1023
- occ_energy: float32 [2048], P('groups'), parts along dimension 0, may hold values from -2 to -0.3
- vir_energy: float32 [128], P('groups'), parts along dimension 0, may hold values from 0.2 to 3
- owner_map: int32 [32], P('groups'), parts along dimension 0, may hold values from 0 to 15, as said below
Outputs:
- grad_coef: float32 [32768, 16], P(('groups', 'aux')), parts along dimension 0
- pair_energy: float32 [64], P(('groups', 'aux')), parts along dimension 0
The draws below stay inside these ranges and needn't reach their ends.
There are 2 independent parts, one for each index of `groups`. The reference program is written for one: setup_inputs(seed, part) draws one part's arguments, and reference() takes and returns one part's arrays. A program takes and returns all parts, laid end to end along the dimension named above; each array names one. Nothing has to cross between parts.
Inputs may be any that keep to these rules, and one draw needn't show every extreme that they name: `slot_counts`: some shard uses all 5 slots. `owner_map`: each device owns at most 2 batch orbitals, and some device owns 2.
All inputs are finite; a program needn't handle non-finite values.
Results may differ from the reference program's by a relative error of at most 0.0007.
Values may be sent and summed in bfloat16 or wider, within the bound.
No kernel may reach another device: no remote copies, remote signals or barrier semaphores. Data moves between devices by JAX's collectives and lax.ppermute only.
A program may use at most 128 MiB of HBM per device.

```python
import jax
import jax.numpy as jnp
from jax import lax

QD = 256
BW = 64
S = 5
BASIS = 16384
NOCC = 1024
CAP = 2
OB = 16
NAUX = 4096
NBLK = 256
N_AUX = 16


def draw_integrals(key, part):
    key = jax.random.fold_in(key, 11)
    first_key, second_key, third_key = jax.random.split(key, 3)
    full_shape = (NAUX, S, BW, BW)
    factors = jax.random.normal(first_key, (NAUX, S, BW, 8), jnp.float32)
    loading = 0.35 * jax.random.normal(third_key, (8, BW), jnp.float32)
    single = jax.random.normal(second_key, full_shape, jnp.float32)
    values = single
    for factor_id in range(8):
        values = values + factors[:, :, :, factor_id:factor_id + 1] * loading[factor_id][None, None, None, :]
    values = jnp.clip(values, -8.0, 8.0)
    return values.reshape(NAUX, S, BW * BW).astype(jnp.bfloat16)


def draw_slot_counts(key, part):
    key = jax.random.fold_in(key, 37)
    key_one, key_two = jax.random.split(key)
    counts = jax.random.randint(key_one, (N_AUX,), 1, S + 1)
    chosen = jax.random.randint(key_two, (), 0, N_AUX)
    return counts.at[chosen].set(S).astype(jnp.int32)


def draw_owner_map(key, part):
    key = jax.random.fold_in(key, 23)
    key_one, key_two = jax.random.split(key)
    devices_order = jax.random.permutation(key_one, N_AUX)
    quarter = N_AUX // 4
    owners = jnp.concatenate([devices_order[:quarter], devices_order[:quarter], devices_order[quarter:3 * quarter]])
    return jnp.take(owners, jax.random.permutation(key_two, N_AUX)).astype(jnp.int32)


def place_ends(entries, key, least, largest):
    spot = [jax.random.randint(jax.random.fold_in(key, axis), (), 0, length) for axis, length in enumerate(entries.shape)]
    longest = entries.shape.index(max(entries.shape))
    next_to = spot[:longest] + [(spot[longest] + 1) % entries.shape[longest]] + spot[longest + 1:]
    return entries.at[tuple(spot)].set(least).at[tuple(next_to)].set(largest)


def levels(rng, shape, cuts, smallest, largest):
    level = 1.0
    for axis_at, shards_of in cuts:
        draws = jax.random.uniform(jax.random.fold_in(jax.random.fold_in(rng, 6), axis_at), (shards_of,), jnp.float32, smallest / len(cuts), largest / len(cuts))
        level = level * jnp.repeat(jnp.exp(draws), shape[axis_at] // shards_of).reshape((-1,) + (1,) * (len(shape) - 1 - axis_at))
    return level


def centred(own_key, shape, width, reach, cuts=(), kind=jnp.bfloat16):
    gain = levels(own_key, shape, cuts, -0.22, 0.18) if cuts else 1.0
    drawn = jax.random.normal(own_key, shape, jnp.float32) * width * gain
    return jnp.minimum(jnp.maximum(drawn, -reach), reach).astype(kind)


def setup_inputs(seed: int = 0, part: int = 0) -> dict:
    splits = jax.random.split(jax.random.key(seed), 9)
    part_splits = jax.random.split(jax.random.fold_in(splits[8], part), 9)
    return {
        "integrals": draw_integrals(jax.random.fold_in(jax.random.fold_in(splits[8], part), 71), part),
        "block_list": place_ends(jax.random.randint(part_splits[1], (N_AUX, S), 0, NBLK), jax.random.fold_in(part_splits[1], 1), 0, NBLK - 1).astype(jnp.int32),
        "slot_counts": draw_slot_counts(jax.random.fold_in(jax.random.fold_in(splits[8], part), 71), part),
        "coefficients": centred(part_splits[3], (BASIS, OB), (BW * S) ** -0.5, 0.3125, ((0, 16),)),
        "batch_index": place_ends(jax.random.randint(part_splits[4], (OB,), 0, NOCC), jax.random.fold_in(part_splits[4], 1), 0, NOCC - 1).astype(jnp.int32),
        "occ_energy": jnp.clip(jax.random.uniform(part_splits[5], (NOCC,), jnp.float32, -2.0, -0.3), -2.0, -0.3),
        "vir_energy": jnp.clip(jax.random.uniform(part_splits[6], (BW,), jnp.float32, 0.2, 3.0), 0.2, 3.0),
        "owner_map": draw_owner_map(jax.random.fold_in(jax.random.fold_in(splits[8], part), 71), part),
    }


def half_transform(slab, blocks, used, coefficients):
    row_ids = blocks[:, None] * BW + jnp.arange(BW)[None, :]
    picked = jnp.take(coefficients, row_ids.reshape(-1), axis=0).reshape(S, BW, OB).astype(jnp.float32)
    usable = (jnp.arange(S) < used).astype(jnp.float32)
    picked = picked * usable[:, None, None]
    slab_wide = slab.reshape(QD, S, BW, BW).astype(jnp.float32)
    halfway = jnp.einsum('qsma,smi->qia', slab_wide, picked, precision=lax.Precision.HIGHEST)
    return halfway.astype(jnp.bfloat16)


def slot_table(owner_map):
    same_owner = owner_map[:, None] == owner_map[None, :]
    earlier = jnp.arange(OB)[None, :] < jnp.arange(OB)[:, None]
    owner_rank = jnp.sum((same_owner & earlier).astype(jnp.int32), axis=1)
    return (owner_map * CAP + owner_rank).astype(jnp.int32)


def reference(integrals, block_list, slot_counts, coefficients, batch_index, occ_energy, vir_energy, owner_map):
    shard_slabs = integrals.reshape(N_AUX, QD, S, BW * BW)

    def pair_step(total, pieces):
        slab, blocks, used = pieces
        halfway = half_transform(slab, blocks, used, coefficients).astype(jnp.float32)
        summed = jnp.einsum('qia,qib->iab', halfway, halfway, precision=lax.Precision.HIGHEST)
        return total + summed, None

    summed, _ = lax.scan(pair_step, jnp.zeros((OB, BW, BW), jnp.float32), (shard_slabs, block_list, slot_counts))
    pair_ints = summed * (0.125 / NAUX)
    occ_levels = jnp.take(occ_energy, batch_index)
    denominators = 2.0 * occ_levels[:, None, None] - vir_energy[None, :, None] - vir_energy[None, None, :]
    amplitudes = pair_ints / denominators
    energies = jnp.sum(pair_ints * amplitudes, axis=(1, 2))
    amps_half = lax.optimization_barrier(amplitudes.astype(jnp.bfloat16)).astype(jnp.float32)

    def grad_step(total, pieces):
        slab, blocks, used = pieces
        halfway = half_transform(slab, blocks, used, coefficients).astype(jnp.float32)
        weights = (0.5 / BW) * jnp.einsum('qia,iab->qib', halfway, amps_half, precision=lax.Precision.HIGHEST)
        weights = lax.optimization_barrier(weights.astype(jnp.bfloat16)).astype(jnp.float32)
        slab_wide = slab.reshape(QD, S, BW, BW).astype(jnp.float32)
        slot_terms = jnp.einsum('qsmn,qin->smi', slab_wide, weights, precision=lax.Precision.HIGHEST)
        usable = (jnp.arange(S) < used).astype(jnp.float32)
        slot_terms = slot_terms * usable[:, None, None]
        return total.at[blocks].add(slot_terms), None

    grad_blocks, _ = lax.scan(grad_step, jnp.zeros((NBLK, BW, OB), jnp.float32), (shard_slabs, block_list, slot_counts))
    grad_coef = grad_blocks.reshape(BASIS, OB)
    slot_ids = slot_table(owner_map)
    pair_energy = jnp.zeros((N_AUX * CAP,), jnp.float32).at[slot_ids].set(energies)
    return grad_coef, pair_energy
```

```python
import functools

import jax
import jax.numpy as jnp
from jax import lax
from jax.experimental import pallas as pl
from jax.experimental.pallas import tpu as pltpu
from jax.sharding import PartitionSpec as P

BW = 64
S = 5
CAP = 2
LANES = 128
HALVES = LANES // BW
TILES = BW * BW // LANES
ROWS = S * TILES
PARTS = 4
F32 = jnp.float32
BF16 = jnp.bfloat16
VMEM = pl.BlockSpec(memory_space=pltpu.VMEM)
SMEM = pl.BlockSpec(memory_space=pltpu.SMEM)


def iota(shape, dim):
    return lax.broadcasted_iota(jnp.int32, shape, dim)


def retile_kernel(part, x, out):
    count = out.shape[0]

    def step(g, carry):
        dst = pl.multiple_of(g * 16, 16)
        src = pl.multiple_of(part * count + g * 16, 16)
        for s in range(S):
            rows = x[s, pl.ds(src, 16), :].reshape(16, TILES, LANES)
            out[pl.ds(dst, 16), s * TILES : (s + 1) * TILES, :] = rows
        return carry

    lax.fori_loop(0, count // 16, step, 0)


def retile(x, part):
    q = x.shape[1] // PARTS
    return pl.pallas_call(
        functools.partial(retile_kernel, part),
        in_specs=[VMEM],
        out_specs=VMEM,
        out_shape=jax.ShapeDtypeStruct((q, ROWS, LANES), BF16),
        compiler_params=pltpu.CompilerParams(vmem_limit_bytes=28 * 2**20),
        cost_estimate=pl.CostEstimate(flops=0, bytes_accessed=4 * q * ROWS * LANES, transcendentals=0),
    )(x)


def gather_index(dev, me, masks):
    rel = lax.bitwise_xor(dev, me)
    place = 0
    for k, mask in enumerate(masks):
        place = place + jnp.where(lax.bitwise_and(rel, mask) != 0, 1 << k, 0)
    return place


def half_kernel(masks, blocks, counts, coef_a, coef_b, *refs):
    slabs, (half, keep, send, scr) = refs[:PARTS], refs[PARTS:]
    me = lax.axis_index("aux")
    orbs, width = coef_a.shape[1], coef_a.shape[2]
    per_dev = width // BW
    near = coef_a.shape[0]
    picked, perm = [], [[], []]
    src = iota((LANES, ROWS), 0)
    dst = iota((LANES, ROWS), 1)
    for s in range(S):
        block = blocks[0, s]
        dev = lax.div(block, per_dev)
        inner = lax.rem(block, per_dev)
        place = gather_index(dev, me, masks)
        col = pl.multiple_of(lax.div(inner, HALVES) * LANES, LANES)
        spot = lax.rem(place, near)
        ours = coef_a[spot, :, pl.ds(col, LANES)]
        theirs = coef_b[spot, :, pl.ds(col, LANES)]
        picked.append(jnp.where(place < near, ours, theirs))
        base = lax.rem(inner, HALVES) * BW
        used = jnp.where(s < counts[0], 1, 0)
        for h in range(HALVES):
            tile = dst - s * TILES
            hit = (src == base + HALVES * tile + h) & (tile >= 0) & (tile < TILES) & (used > 0)
            perm[h].append(jnp.where(hit, 1.0, 0.0).astype(BF16))
    picked = jnp.concatenate(picked, axis=1)
    coef = jnp.concatenate(
        [jnp.dot(picked, jnp.concatenate(perm[h], axis=0), preferred_element_type=F32) for h in range(HALVES)],
        axis=0,
    ).astype(BF16)
    low = iota((orbs, LANES), 1) < BW
    pairs = half.shape[1]
    for part in range(PARTS):
        slab = slabs[part]
        for p in range(slab.shape[0] // 2):
            both = jnp.concatenate([slab[2 * p], slab[2 * p + 1]], axis=1)
            r = jnp.dot(coef, both, preferred_element_type=F32)
            straight = jnp.where(low, r[:orbs, :LANES], r[orbs:, LANES:])
            crossed = jnp.where(low, r[:orbs, LANES:], r[orbs:, :LANES])
            row = straight + pltpu.roll(crossed, BW, 1)
            at = part * (slab.shape[0] // 2) + p
            for g in range(orbs // 8):
                scr[pl.ds(g * 8 * pairs + at, 8, stride=pairs), :] = row[g * 8 : g * 8 + 8]
    scale = 0.125 / (2 * pairs * lax.axis_size("aux"))
    lane = iota((BW, LANES), 1)
    left = lane < BW
    upper = iota((BW, LANES), 0) <= lax.rem(lane, BW)
    eye = iota((BW, LANES), 0) == lax.rem(lane, BW)

    def square(i):
        h = scr[i * pairs : (i + 1) * pairs, :].astype(BF16)
        half[i] = h
        t = lax.dot_general(h, h, (((0,), (0,)), ((), ())), preferred_element_type=F32) * scale
        return t[:BW], t[BW:]

    quads = orbs // 8
    cores = []
    for core in range(2):
        tiles, diags = [], []
        for k in range(quads):
            first = core * (orbs // 2) + 4 * k
            t = [square(first + j) for j in range(4)]
            lefts = [t[j][0] + pltpu.roll(t[j][1], BW, 1) for j in (0, 1)]
            rights = [pltpu.roll(t[j][0], BW, 1) + t[j][1] for j in (2, 3)]
            a = jnp.where(left, lefts[0], rights[0])
            b = jnp.where(left, lefts[1], rights[1])
            tiles.append(jnp.where(upper, a, b))
            diags.append(jnp.sum(jnp.where(eye, b, 0.0), axis=0, keepdims=True))
        spare = keep.shape[0] - quads * BW - quads
        if spare:
            diags.append(jnp.zeros((spare, LANES), F32))
        cores.append((tiles, jnp.concatenate(diags, axis=0)))
    own = lax.rem(me, 2) == 0
    for k in range(quads):
        keep[k * BW : (k + 1) * BW, :] = jnp.where(own, cores[0][0][k], cores[1][0][k])
        send[k * BW : (k + 1) * BW, :] = jnp.where(own, cores[1][0][k], cores[0][0][k])
    keep[quads * BW :, :] = jnp.where(own, cores[0][1], cores[1][1])
    send[quads * BW :, :] = jnp.where(own, cores[1][1], cores[0][1])


def half_transform(masks, block_list, slot_counts, coef_a, coef_b, slabs):
    orbs = coef_a.shape[1]
    pairs = sum(s.shape[0] for s in slabs) // 2
    quads = orbs // 8
    rows = quads * BW + -(-quads // 8) * 8
    packed = jax.ShapeDtypeStruct((rows, LANES), F32)
    return pl.pallas_call(
        functools.partial(half_kernel, masks),
        in_specs=[SMEM, SMEM, VMEM, VMEM] + [VMEM] * PARTS,
        out_specs=[VMEM] * 3,
        out_shape=[jax.ShapeDtypeStruct((orbs, pairs, LANES), BF16), packed, packed],
        scratch_shapes=[pltpu.VMEM((orbs * pairs, LANES), F32)],
        compiler_params=pltpu.CompilerParams(vmem_limit_bytes=44 * 2**20),
    )(block_list, slot_counts, coef_a, coef_b, *slabs)


def level_kernel(index, levels, out):
    lane = iota((1, LANES), 1)

    def step(i, carry):
        at = index[i]
        row = levels[pl.ds(lax.div(at, LANES), 1), :]
        value = jnp.sum(jnp.where(lane == lax.rem(at, LANES), row, 0.0), axis=1, keepdims=True)
        out[pl.ds(i, 1), :] = jnp.broadcast_to(2.0 * value, (1, LANES))
        return carry

    lax.fori_loop(0, out.shape[0], step, 0)


def level_rows(batch_index, occ_energy):
    return pl.pallas_call(
        level_kernel,
        in_specs=[SMEM, VMEM],
        out_specs=VMEM,
        out_shape=jax.ShapeDtypeStruct((batch_index.shape[0], LANES), F32),
    )(batch_index, occ_energy.reshape(-1, LANES))


def grad_kernel(blocks, counts, mine, other, levels, vir, half, *refs):
    slabs, (terms, energy, scr) = refs[:PARTS], refs[PARTS:]
    me = lax.axis_index("aux")
    orbs, pairs = half.shape[0], half.shape[1]
    quads = orbs // 8
    lane = iota((BW, LANES), 1)
    row = iota((BW, LANES), 0)
    left = lane < BW
    inner = lax.rem(lane, BW)
    vir_b = jnp.concatenate([vir[...], vir[...]], axis=1)
    vir_a = jnp.sum(jnp.where((row == inner) & left, vir_b, 0.0), axis=1, keepdims=True)
    even = lax.rem(me, 2) == 0
    zero = jnp.zeros((BW, LANES), F32)
    scale = 0.5 / BW
    for core in range(2):
        ours = even if core == 0 else jnp.logical_not(even)

        def packed(start, size, ours=ours):
            return jnp.where(ours, mine[start : start + size, :], other[start : start + size, :])

        for k in range(0, quads, 2):
            squares = [packed((k + j) * BW, BW) for j in range(2)]
            turned = jnp.concatenate(squares, axis=0).T
            top, bottom = turned[:BW], turned[BW:]
            flips = [
                jnp.where(left, top, pltpu.roll(bottom, BW, 1)),
                jnp.where(left, pltpu.roll(top, BW, 1), bottom),
            ]
            for j in range(2):
                first = core * (orbs // 2) + 4 * (k + j)
                diag = packed(quads * BW + k + j, 1)
                ints = [
                    jnp.where(row <= inner, squares[j], flips[j]),
                    jnp.where(row == inner, diag, jnp.where(row > inner, squares[j], flips[j])),
                ]
                for b in range(2):
                    one, two = first + b, first + 2 + b
                    level = jnp.where(left, levels[one : one + 1, :], levels[two : two + 1, :])
                    amps = ints[b] / ((level - vir_a) - vir_b)
                    sums = jnp.sum(ints[b] * amps, axis=0, keepdims=True)
                    energy[one : one + 1, :] = jnp.where(left[:1], sums, 0.0)
                    energy[two : two + 1, :] = jnp.where(left[:1], 0.0, sums)
                    turn = pltpu.roll(amps, BW, 1)
                    for i, lows, highs in ((one, amps, turn), (two, turn, amps)):
                        square = jnp.concatenate([jnp.where(left, lows, zero), jnp.where(left, zero, highs)], axis=0)
                        w = jnp.dot(half[i], square.astype(BF16), preferred_element_type=F32) * scale
                        scr[i * pairs : (i + 1) * pairs, :] = w.astype(BF16).astype(F32)
    low = iota((orbs, LANES), 1) < BW
    blank = jnp.zeros((orbs, LANES), F32)
    total = jnp.zeros((ROWS, HALVES * orbs), F32)
    for part in range(PARTS):
        slab = slabs[part]
        xs, ws = [], []
        for p in range(slab.shape[0] // 2):
            at = part * (slab.shape[0] // 2) + p
            w = jnp.concatenate(
                [scr[pl.ds(g * 8 * pairs + at, 8, stride=pairs), :] for g in range(orbs // 8)], axis=0
            )
            turn = pltpu.roll(w, BW, 1)
            ws.append(jnp.concatenate([jnp.where(low, w, blank), jnp.where(low, blank, turn)], axis=0).astype(BF16))
            ws.append(jnp.concatenate([jnp.where(low, turn, blank), jnp.where(low, blank, w)], axis=0).astype(BF16))
            xs += [slab[2 * p], slab[2 * p + 1]]
        total = total + lax.dot_general(
            jnp.concatenate(xs, axis=1),
            jnp.concatenate(ws, axis=1),
            (((1,), (1,)), ((), ())),
            preferred_element_type=F32,
        )
    flat = total.T
    width = terms.shape[1]
    src = iota((ROWS, width), 0)
    dst = iota((ROWS, width), 1)
    out = jnp.zeros((orbs, width), F32)
    for h in range(HALVES):
        spread = jnp.where(dst == lax.div(src, TILES) * BW + lax.rem(src, TILES) * HALVES + h, 1.0, 0.0)
        out = out + lax.dot_general(
            flat[h * orbs : (h + 1) * orbs],
            spread,
            (((1,), (0,)), ((), ())),
            precision=lax.Precision.HIGHEST,
            preferred_element_type=F32,
        )
    place = iota((orbs, width), 1) - S * BW
    for s in range(S):
        out = jnp.where(place == s, jnp.where(s < counts[0], blocks[0, s], -1).astype(F32), out)
    terms[...] = out


def gradient_terms(block_list, slot_counts, mine, other, levels, vir_energy, half, slabs):
    orbs, pairs = half.shape[0], half.shape[1]
    width = -(-(S * BW + S) // LANES) * LANES
    return pl.pallas_call(
        grad_kernel,
        in_specs=[SMEM, SMEM] + [VMEM] * 5 + [VMEM] * PARTS,
        out_specs=[VMEM] * 2,
        out_shape=[jax.ShapeDtypeStruct((orbs, width), F32), jax.ShapeDtypeStruct((orbs, LANES), F32)],
        scratch_shapes=[pltpu.VMEM((orbs * pairs, LANES), F32)],
        compiler_params=pltpu.CompilerParams(vmem_limit_bytes=44 * 2**20),
    )(block_list, slot_counts, mine, other, levels, vir_energy.reshape(1, -1), half, *slabs)


def place_kernel(near, far, out):
    me = lax.axis_index("aux")
    orbs, width = out.shape
    per_dev = width // BW
    lane = iota((orbs, LANES), 1)
    side = jnp.where(lane < BW, 0, 1)
    tiles = S * BW // LANES + 1
    for t in range(width // LANES):
        out[:, t * LANES : (t + 1) * LANES] = jnp.zeros((orbs, LANES), F32)

    def take(ref, d):
        ids = ref[d, :, (tiles - 1) * LANES : tiles * LANES]
        start = S * BW - (tiles - 1) * LANES
        ids = [ids[:, start + s : start + s + 1].astype(jnp.int32) - me * per_dev for s in range(S)]
        none = jnp.full_like(ids[0], -1)
        ids = ids + [none] * (2 * tiles - S)
        for k in range(tiles):
            value = ref[d, :, k * LANES : (k + 1) * LANES]
            one, two = ids[2 * k], ids[2 * k + 1]
            spot = jnp.where(side == 0, one, two)
            turn = pltpu.roll(value, BW, 1)
            turn_spot = jnp.where(side == 0, two, one)
            for t in range(width // LANES):
                here = HALVES * t + side
                cols = slice(t * LANES, (t + 1) * LANES)
                out[:, cols] += jnp.where(spot == here, value, 0.0) + jnp.where(turn_spot == here, turn, 0.0)

    def step(d, carry):
        take(near, d)
        take(far, d)
        return carry

    lax.fori_loop(0, near.shape[0], step, 0)


def place_terms(near, far, rows):
    return pl.pallas_call(
        place_kernel,
        in_specs=[VMEM, VMEM],
        out_specs=VMEM,
        out_shape=jax.ShapeDtypeStruct((near.shape[1], rows), F32),
        compiler_params=pltpu.CompilerParams(vmem_limit_bytes=44 * 2**20),
    )(near, far)


def swap(x, mask):
    size = lax.axis_size("aux")
    return lax.ppermute(x, "aux", [(i, i ^ mask) for i in range(size)])


def body(
    integrals, block_list, slot_counts, coefficients, batch_index, occ_energy, vir_energy, owner_map
):
    size = lax.axis_size("aux")
    me = lax.axis_index("aux")
    local_rows = coefficients.shape[0]
    masks = []
    while size >> (len(masks) + 1):
        masks.append(size >> (len(masks) + 1))
    x = jnp.transpose(integrals, (1, 0, 2))
    buf = coefficients.T[None]
    slabs = []
    for k, mask in enumerate(masks):
        far = swap(buf, mask)
        if k < PARTS:
            slabs.append(retile(x, k))
            if k == 0:
                levels = level_rows(batch_index, occ_energy)
        near, far = buf, far
        if k + 1 < len(masks):
            buf = jnp.concatenate([near, far], axis=0)
            if k + 1 < PARTS:
                buf, _ = lax.optimization_barrier((buf, slabs[-1]))
                x, _ = lax.optimization_barrier((x, far))
    while len(slabs) < PARTS:
        slabs.append(retile(x, len(slabs)))
    half, keep, send = half_transform(tuple(masks), block_list, slot_counts, near, far, slabs)
    keep = keep + swap(send, 1)
    for mask in reversed(masks[:-1]):
        keep = keep + swap(keep, mask)
    other = swap(keep, 1)
    terms, energy = gradient_terms(
        block_list, slot_counts, keep, other, levels, vir_energy, half, slabs
    )
    buf = terms[None]
    for mask in masks:
        near, far = buf, swap(buf, mask)
        buf = jnp.concatenate([near, far], axis=0)
    grad_coef = place_terms(near, far, local_rows).T
    energies = jnp.sum(energy, axis=1)
    orbs = owner_map.shape[0]
    same = owner_map[:, None] == owner_map[None, :]
    earlier = jnp.arange(orbs)[None, :] < jnp.arange(orbs)[:, None]
    rank = jnp.sum((same & earlier).astype(jnp.int32), axis=1)
    hit = (owner_map == me)[None, :] & (rank[None, :] == jnp.arange(CAP)[:, None])
    pair_energy = jnp.sum(jnp.where(hit, energies[None, :], 0.0), axis=1)
    return (grad_coef, pair_energy)


def solution(mesh):
    return jax.shard_map(
        body,
        mesh=mesh,
        in_specs=(
            P(("groups", "aux"), None, None),
            P(("groups", "aux"), None),
            P(("groups", "aux")),
            P(("groups", "aux"), None),
            P("groups"),
            P("groups"),
            P("groups"),
            P("groups"),
        ),
        out_specs=(P(("groups", "aux"), None), P(("groups", "aux"))),
        check_vma=False,
    )
```

```python
import functools

import jax
import jax.numpy as jnp
from jax import lax
from jax.experimental import pallas as pl
from jax.experimental.pallas import tpu as pltpu
from jax.sharding import PartitionSpec as P

BW = 64
S = 5
CAP = 2
LANES = 128
HALVES = LANES // BW
TILES = BW * BW // LANES
ROWS = S * TILES
PARTS = 3
F32 = jnp.float32
BF16 = jnp.bfloat16
VMEM = pl.BlockSpec(memory_space=pltpu.VMEM)
SMEM = pl.BlockSpec(memory_space=pltpu.SMEM)


def limit(orbs):
    return max(8, orbs // 4) * 2**20


def iota(shape, dim):
    return lax.broadcasted_iota(jnp.int32, shape, dim)


def split_rows(count):
    unit = count // 16
    return (3 * unit, 11 * unit, count - 14 * unit)


def retile_rows(x, out, at):
    for s in range(S):
        out[at : at + 16, s * TILES : (s + 1) * TILES, :] = x[s, at : at + 16, :].reshape(16, TILES, LANES)


def fetch(start, x, slab, sems):
    copies = []
    for c in range(slab.shape[1] // 16):
        src = x.at[:, pl.ds(start + c * 16, 16), :]
        copies.append(pltpu.make_async_copy(src, slab.at[:, pl.ds(c * 16, 16), :], sems.at[c]))
        copies[-1].start()
    return copies


def retile_kernel(start, x, out, slab, sems):
    for c, copy in enumerate(fetch(start, x, slab, sems)):
        copy.wait()
        retile_rows(slab, out, c * 16)


def retile(x, part):
    sizes = split_rows(x.shape[1])
    start, size = sum(sizes[:part]), sizes[part]
    return pl.pallas_call(
        functools.partial(retile_kernel, start),
        in_specs=[pl.BlockSpec(memory_space=pltpu.HBM)],
        out_specs=VMEM,
        out_shape=jax.ShapeDtypeStruct((size, ROWS, LANES), BF16),
        scratch_shapes=[pltpu.VMEM((S, size, TILES * LANES), BF16), pltpu.SemaphoreType.DMA((size // 16,))],
        compiler_params=pltpu.CompilerParams(vmem_limit_bytes=10 * 2**20),
        cost_estimate=pl.CostEstimate(flops=0, bytes_accessed=4 * size * ROWS * LANES, transcendentals=0),
    )(in_hbm(x))


def prepare_kernel(blocks, counts, index, levels, coef, x, *refs):
    rows, ids, held, out = refs[:4]
    sems, own_blocks, own_index, own_levels, slab, slab_sems = refs[4:]
    pairs = (blocks, own_blocks), (index, own_index), (levels, own_levels), (coef, held)
    copies = [pltpu.make_async_copy(src, dst, sems.at[k]) for k, (src, dst) in enumerate(pairs)]
    for copy in copies:
        copy.start()
    for c, copy in enumerate(fetch(0, x, slab, slab_sems)):
        copy.wait()
        retile_rows(slab, out, c * 16)
    for copy in copies:
        copy.wait()
    lane = iota((1, LANES), 1)

    def step(i, carry):
        at = own_index[i]
        row = own_levels[pl.ds(lax.div(at, LANES), 1), :]
        rows[pl.ds(i, 1), :] = jnp.where(lane == lax.rem(at, LANES), 2.0 * row, 0.0)
        return carry

    lax.fori_loop(0, rows.shape[0], step, 0)
    rows[...] = jnp.broadcast_to(jnp.sum(rows[...], axis=1, keepdims=True), rows.shape)
    total = jnp.full(ids.shape, -1, jnp.int32)
    for s in range(S):
        total = jnp.where((lane == s) & (s < counts[...]), own_blocks[0, s], total)
    ids[...] = total


def in_hbm(x):
    return pltpu.with_memory_space_constraint(x, pltpu.HBM)


def prepare(blocks, counts, index, levels, coef, x):
    far = pl.BlockSpec(memory_space=pltpu.HBM)
    size = split_rows(x.shape[1])[0]
    return pl.pallas_call(
        prepare_kernel,
        in_specs=[far, VMEM, far, far, far, far],
        out_specs=[VMEM] * 4,
        out_shape=[
            jax.ShapeDtypeStruct((index.shape[0], LANES), F32),
            jax.ShapeDtypeStruct((1, LANES), jnp.int32),
            jax.ShapeDtypeStruct(coef.shape, coef.dtype),
            jax.ShapeDtypeStruct((size, ROWS, LANES), BF16),
        ],
        scratch_shapes=[
            pltpu.SemaphoreType.DMA((4,)),
            pltpu.SMEM(blocks.shape, blocks.dtype),
            pltpu.SMEM(index.shape, index.dtype),
            pltpu.VMEM(levels.shape, levels.dtype),
            pltpu.VMEM((S, size, TILES * LANES), BF16),
            pltpu.SemaphoreType.DMA((size // 16,)),
        ],
        compiler_params=pltpu.CompilerParams(vmem_limit_bytes=8 * 2**20),
        cost_estimate=pl.CostEstimate(flops=0, bytes_accessed=4 * size * ROWS * LANES, transcendentals=0),
    )(in_hbm(blocks), counts, in_hbm(index), in_hbm(levels), in_hbm(coef), in_hbm(x))


def stages(size):
    bits = []
    while size > 2:
        size //= 2
        bits.append(size)
    steps = [(bits.pop(0),)] if len(bits) % 2 else []
    for high, low in zip(bits[::2], bits[1::2]):
        steps.append((low, high ^ low, high))
    return tuple(steps)


def gather_index(dev, me, steps):
    rel = lax.bitwise_xor(dev, me)
    place, count = 0, 1
    for step in steps:
        low = lax.bitwise_and(rel, step[0]) != 0
        if len(step) == 1:
            place = place + jnp.where(low, count, 0)
        else:
            high = lax.bitwise_and(rel, step[2]) != 0
            place = place + jnp.where(high, jnp.where(low, 2, 3), jnp.where(low, 1, 0)) * count
        count *= len(step) + 1
    return place


def half_kernel(steps, ids, coef_a, coef_b, *refs):
    slabs, (half, send, scr) = refs[:PARTS], refs[PARTS:]
    me = lax.axis_index("aux")
    orbs, width = coef_a.shape[1], coef_a.shape[2]
    per_dev = width // BW
    near = coef_a.shape[0]
    src = iota((LANES, LANES), 0)
    dst = iota((LANES, LANES), 1)
    wanted = (dst & BW) // BW + (dst & (TILES - 1)) * 2 + (dst & TILES) // TILES * BW
    spread = jnp.where(src == wanted, 1.0, 0.0).astype(BF16)
    picked = []
    for s in range(S):
        block = jnp.maximum(ids[0, s], 0)
        dev = lax.div(block, per_dev)
        inner = lax.rem(block, per_dev)
        place = gather_index(dev, me, steps)
        col = pl.multiple_of(lax.div(inner, HALVES) * LANES, LANES)
        spot = lax.rem(place, near)
        ours = coef_a[spot, :, pl.ds(col, LANES)]
        theirs = coef_b[spot, :, pl.ds(col, LANES)]
        picked.append(jnp.where(place < near, ours, theirs))
    apart = jnp.dot(jnp.concatenate(picked, axis=0), spread, preferred_element_type=F32)
    group = iota((orbs, LANES), 1) // TILES
    coef = [[jnp.zeros((orbs, LANES), F32) for _ in range(2)] for _ in range(HALVES)]
    for s in range(S):
        second = lax.rem(ids[0, s], HALVES) == 1
        value = apart[s * orbs : (s + 1) * orbs]
        value = jnp.where(second, pltpu.roll(value, LANES - TILES, 1), value)
        for h in range(HALVES):
            shift = (s * TILES - h * BW) % LANES
            there = pltpu.roll(value, shift, 1) if shift else value
            tile = s * TILES // LANES
            hit = (group == s % (LANES // TILES)) & (ids[0, s] >= 0)
            coef[h][tile] = jnp.where(hit, there, coef[h][tile])
    coef = jnp.concatenate([jnp.concatenate(coef[h], axis=1)[:, :ROWS] for h in range(HALVES)], axis=0).astype(BF16)
    low = iota((orbs, LANES), 1) < BW
    pairs = half.shape[1]
    base = 0
    for slab in slabs:
        for p in range(slab.shape[0] // 2):
            both = jnp.concatenate([slab[2 * p], slab[2 * p + 1]], axis=1)
            r = jnp.dot(coef, both, preferred_element_type=F32)
            straight = jnp.where(low, r[:orbs, :LANES], r[orbs:, LANES:])
            crossed = jnp.where(low, r[:orbs, LANES:], r[orbs:, :LANES])
            row = straight + pltpu.roll(crossed, BW, 1)
            for g in range(orbs // 8):
                scr[pl.ds(g * 8 * pairs + base + p, 8, stride=pairs), :] = row[g * 8 : g * 8 + 8]
        base += slab.shape[0] // 2
    for i in range(orbs):
        half[i] = scr[i * pairs : (i + 1) * pairs, :].astype(BF16)
    pair_squares(half, 1 - lax.rem(me, 2), send)


def pair_squares(half, core, out):
    orbs, pairs = half.shape[0], half.shape[1]
    scale = 0.125 / (2 * pairs * lax.axis_size("aux"))
    lane = iota((BW, LANES), 1)
    left = lane < BW
    upper = iota((BW, LANES), 0) <= lax.rem(lane, BW)
    eye = iota((BW, LANES), 0) == lax.rem(lane, BW)
    quads = orbs // 8
    diags = []
    for k in range(quads):
        t = []
        for j in range(4):
            h = half[core * (orbs // 2) + 4 * k + j]
            t.append(lax.dot_general(h, h, (((0,), (0,)), ((), ())), preferred_element_type=F32) * scale)
        lefts = [t[j][:BW] + pltpu.roll(t[j][BW:], BW, 1) for j in (0, 1)]
        rights = [pltpu.roll(t[j][:BW], BW, 1) + t[j][BW:] for j in (2, 3)]
        a = jnp.where(left, lefts[0], rights[0])
        b = jnp.where(left, lefts[1], rights[1])
        out[k * BW : (k + 1) * BW, :] = jnp.where(upper, a, b)
        diags.append(jnp.sum(jnp.where(eye, b, 0.0), axis=0, keepdims=True))
    spare = out.shape[0] - quads * BW - quads
    if spare:
        diags.append(jnp.zeros((spare, LANES), F32))
    out[quads * BW :, :] = jnp.concatenate(diags, axis=0)


def own_kernel(half, out):
    pair_squares(half, lax.rem(lax.axis_index("aux"), 2), out)


def own_squares(half, like):
    return pl.pallas_call(
        own_kernel,
        in_specs=[VMEM],
        out_specs=VMEM,
        out_shape=jax.ShapeDtypeStruct(like.shape, F32),
        compiler_params=pltpu.CompilerParams(vmem_limit_bytes=4 * 2**20),
        cost_estimate=pl.CostEstimate(flops=0, bytes_accessed=2 * 2**20, transcendentals=0),
    )(half)


def half_transform(steps, ids, coef_a, coef_b, slabs):
    orbs = coef_a.shape[1]
    pairs = sum(s.shape[0] for s in slabs) // 2
    quads = orbs // 8
    rows = quads * BW + -(-quads // 8) * 8
    packed = jax.ShapeDtypeStruct((rows, LANES), F32)
    return pl.pallas_call(
        functools.partial(half_kernel, steps),
        in_specs=[SMEM, VMEM, VMEM] + [VMEM] * PARTS,
        out_specs=[VMEM] * 2,
        out_shape=[jax.ShapeDtypeStruct((orbs, pairs, LANES), BF16), packed],
        scratch_shapes=[pltpu.VMEM((orbs * pairs, LANES), F32)],
        compiler_params=pltpu.CompilerParams(vmem_limit_bytes=limit(orbs)),
    )(ids, coef_a, coef_b, *slabs)


def weight_rows(packed, core, levels, vir, half, energy, weights):
    orbs, pairs = half.shape[0], half.shape[1]
    quads = orbs // 8
    lane = iota((BW, LANES), 1)
    row = iota((BW, LANES), 0)
    left = lane < BW
    inner = lax.rem(lane, BW)
    vir_b = jnp.concatenate([vir[...], vir[...]], axis=1)
    vir_a = jnp.sum(jnp.where((row == inner) & left, vir_b, 0.0), axis=1, keepdims=True)
    zero = jnp.zeros((BW, LANES), F32)
    scale = 0.5 / BW
    start = core * (orbs // 2)
    for k in range(0, quads, 2):
        squares = [packed[(k + j) * BW : (k + j + 1) * BW, :] for j in range(2)]
        turned = jnp.concatenate(squares, axis=0).T
        top, bottom = turned[:BW], turned[BW:]
        flips = [
            jnp.where(left, top, pltpu.roll(bottom, BW, 1)),
            jnp.where(left, pltpu.roll(top, BW, 1), bottom),
        ]
        for j in range(2):
            first = 4 * (k + j)
            diag = packed[quads * BW + k + j : quads * BW + k + j + 1, :]
            ints = [
                jnp.where(row <= inner, squares[j], flips[j]),
                jnp.where(row == inner, diag, jnp.where(row > inner, squares[j], flips[j])),
            ]
            for b in range(2):
                one, two = first + b, first + 2 + b
                level = jnp.where(left[:1], levels[pl.ds(start + one, 1), :], levels[pl.ds(start + two, 1), :])
                amps = ints[b] / ((level - vir_a) - vir_b)
                sums = jnp.sum(ints[b] * amps, axis=0, keepdims=True)
                energy[one : one + 1, :] = jnp.where(left[:1], sums, 0.0)
                energy[two : two + 1, :] = jnp.where(left[:1], 0.0, sums)
                turn = pltpu.roll(amps, BW, 1)
                for i, lows, highs in ((one, amps, turn), (two, turn, amps)):
                    square = jnp.concatenate([jnp.where(left, lows, zero), jnp.where(left, zero, highs)], axis=0)
                    w = jnp.dot(half[start + i], square.astype(BF16), preferred_element_type=F32) * scale
                    weights[i * pairs : (i + 1) * pairs, :] = w.astype(BF16).astype(F32)


def weight_kernel(packed, levels, vir, half, energy, weights):
    weight_rows(packed, lax.rem(lax.axis_index("aux"), 2), levels, vir, half, energy, weights)


def own_weights(packed, levels, vir, half):
    orbs, pairs = half.shape[0], half.shape[1]
    return pl.pallas_call(
        weight_kernel,
        in_specs=[VMEM] * 4,
        out_specs=[VMEM] * 2,
        out_shape=[
            jax.ShapeDtypeStruct((orbs // 2, LANES), F32),
            jax.ShapeDtypeStruct((orbs // 2 * pairs, LANES), F32),
        ],
        compiler_params=pltpu.CompilerParams(vmem_limit_bytes=4 * 2**20),
        cost_estimate=pl.CostEstimate(flops=0, bytes_accessed=3 * 2**20, transcendentals=0),
    )(packed, levels, vir, half)


def grad_kernel(ids, packed, levels, vir, half, own_energy, own, *refs):
    slabs, (terms, energy, other_energy, other, mixed) = refs[:PARTS], refs[PARTS:]
    core = lax.rem(lax.axis_index("aux"), 2)
    orbs, pairs = half.shape[0], half.shape[1]
    mid = orbs // 2
    weight_rows(packed, 1 - core, levels, vir, half, other_energy, other)

    def ordered(ours, theirs):
        return jnp.concatenate([jnp.where(core == 0, ours, theirs), jnp.where(core == 0, theirs, ours)], axis=0)

    energy[...] = ordered(own_energy[...], other_energy[...])
    low = iota((orbs, LANES), 1) < BW
    blank = jnp.zeros((orbs, LANES), F32)
    total = jnp.zeros((ROWS, HALVES * orbs), F32)
    base = 0
    for slab in slabs:
        for start in range(0, slab.shape[0] // 2, 32):
            xs, ws = [], []
            for p in range(start, min(start + 32, slab.shape[0] // 2)):
                w = jnp.concatenate(
                    [
                        ref[pl.ds(g * 8 * pairs + base + p, 8, stride=pairs), :]
                        for ref in (own, other)
                        for g in range(mid // 8)
                    ],
                    axis=0,
                )
                turn = pltpu.roll(w, BW, 1)
                ws.append(jnp.concatenate([jnp.where(low, w, blank), jnp.where(low, blank, turn)], axis=0).astype(BF16))
                ws.append(jnp.concatenate([jnp.where(low, turn, blank), jnp.where(low, blank, w)], axis=0).astype(BF16))
                xs += [slab[2 * p], slab[2 * p + 1]]
            total = total + lax.dot_general(
                jnp.concatenate(xs, axis=1),
                jnp.concatenate(ws, axis=1),
                (((1,), (1,)), ((), ())),
                preferred_element_type=F32,
            )
        base += slab.shape[0] // 2
    width = terms.shape[1]
    turn = total if HALVES * orbs > LANES else jnp.pad(total, ((0, 0), (0, LANES - HALVES * orbs)))
    for h in range(HALVES):
        rows = turn[:, h * orbs : h * orbs + LANES]
        if rows.shape[1] < LANES:
            rows = pltpu.roll(turn, LANES - h * orbs, 1)
        mixed[pl.ds(h, ROWS, stride=HALVES), :] = rows
    mixed[HALVES * ROWS :, :] = jnp.zeros((width - HALVES * ROWS, LANES), F32)
    for t in range(width // LANES):
        out = mixed[t * LANES : (t + 1) * LANES, :].T[:orbs]
        out = ordered(out[:mid], out[mid:])
        place = iota((orbs, LANES), 1) + (t * LANES - S * BW)
        for s in range(S):
            if t * LANES <= S * BW + s < (t + 1) * LANES:
                out = jnp.where(place == s, ids[0, s].astype(F32), out)
        terms[:, t * LANES : (t + 1) * LANES] = out


def gradient_terms(ids, packed, levels, vir, half, own_energy, own, slabs):
    orbs, pairs = half.shape[0], half.shape[1]
    width = -(-(S * BW + S) // LANES) * LANES
    return pl.pallas_call(
        grad_kernel,
        in_specs=[SMEM] + [VMEM] * 6 + [VMEM] * PARTS,
        out_specs=[VMEM] * 2,
        out_shape=[jax.ShapeDtypeStruct((orbs, width), F32), jax.ShapeDtypeStruct((orbs, LANES), F32)],
        scratch_shapes=[
            pltpu.VMEM(own_energy.shape, F32),
            pltpu.VMEM(own.shape, F32),
            pltpu.VMEM((width, LANES), F32),
        ],
        compiler_params=pltpu.CompilerParams(vmem_limit_bytes=limit(orbs)),
    )(ids, packed, levels, vir, half, own_energy, own, *slabs)


def place_kernel(*refs):
    piece, out = refs[0], refs[-1]
    me = lax.axis_index("aux")
    orbs, width = out.shape
    per_dev = width // BW
    step_tiles = range(width // LANES)
    lane = iota((8, LANES), 1)
    side = jnp.where(lane < BW, 0, 1)
    tiles = S * BW // LANES + 1
    start = S * BW - (tiles - 1) * LANES
    groups = [slice(g, min(g + 16, orbs)) for g in range(0, orbs, 16)]
    for rows in groups:
        parts = [slice(r, r + 8) for r in range(rows.start, rows.stop, 8)]
        if len(refs) == 3:
            total = [[refs[1][r, t * LANES : (t + 1) * LANES] for t in step_tiles] for r in parts]
        else:
            total = [[jnp.zeros((8, LANES), F32) for _ in step_tiles] for _ in parts]

        def step(d, total, parts=parts):
            total = [list(row) for row in total]
            tail = piece[d, 0:8, (tiles - 1) * LANES : tiles * LANES]
            ids = [jnp.broadcast_to(tail[:, start + s : start + s + 1], (8, LANES)) for s in range(S)]
            ids = [i.astype(jnp.int32) - me * per_dev for i in ids]
            ids = ids + [jnp.full((8, LANES), -1, jnp.int32)] * (2 * tiles - S)
            for k in range(tiles):
                spot = jnp.where(side == 0, ids[2 * k], ids[2 * k + 1]) - side
                turn_spot = jnp.where(side == 0, ids[2 * k + 1], ids[2 * k]) - side
                values = [piece[d, r, k * LANES : (k + 1) * LANES] for r in parts]
                turns = [pltpu.roll(v, BW, 1) for v in values]
                for t in step_tiles:
                    here, there = spot == HALVES * t, turn_spot == HALVES * t
                    for r in range(len(parts)):
                        added = jnp.where(here, values[r], 0.0) + jnp.where(there, turns[r], 0.0)
                        total[r][t] = total[r][t] + added
            return total

        if piece.shape[0] <= 8:
            for d in range(piece.shape[0]):
                total = step(d, total)
        else:
            total = lax.fori_loop(0, piece.shape[0], step, total)
        for r, part in enumerate(parts):
            for t in step_tiles:
                out[part, t * LANES : (t + 1) * LANES] = total[r][t]


def place_terms(piece, total, rows):
    args = (piece,) if total is None else (piece, total)
    return pl.pallas_call(
        place_kernel,
        in_specs=[VMEM] * len(args),
        out_specs=VMEM,
        out_shape=jax.ShapeDtypeStruct((piece.shape[1], rows), F32),
        compiler_params=pltpu.CompilerParams(vmem_limit_bytes=8 * 2**20),
        cost_estimate=pl.CostEstimate(flops=0, bytes_accessed=4 * piece.size, transcendentals=0),
    )(*args)


def pair_kernel(owner, energy, out, held, sem):
    copy = pltpu.make_async_copy(owner, held, sem)
    copy.start()
    copy.wait()
    me = lax.axis_index("aux")

    def step(i, carry):
        rank, rows = carry
        mine = held[i] == me
        row = energy[pl.ds(i, 1), :]
        rows = [jnp.where(mine & (rank == k), row, rows[k]) for k in range(CAP)]
        return rank + jnp.where(mine, 1, 0), rows

    blank = jnp.zeros((1, LANES), F32)
    _, rows = lax.fori_loop(0, energy.shape[0], step, (jnp.int32(0), [blank] * CAP))
    for k in range(CAP):
        out[k] = jnp.sum(rows[k])


def pair_slots(owner_map, energy):
    return pl.pallas_call(
        pair_kernel,
        in_specs=[pl.BlockSpec(memory_space=pltpu.HBM), VMEM],
        out_specs=SMEM,
        out_shape=jax.ShapeDtypeStruct((CAP,), F32),
        scratch_shapes=[pltpu.SMEM(owner_map.shape, owner_map.dtype), pltpu.SemaphoreType.DMA],
        compiler_params=pltpu.CompilerParams(vmem_limit_bytes=2**20),
        cost_estimate=pl.CostEstimate(flops=0, bytes_accessed=2**20, transcendentals=0),
    )(in_hbm(owner_map), energy)


def swap(x, mask):
    size = lax.axis_size("aux")
    return lax.ppermute(x, "aux", [(i, i ^ mask) for i in range(size)])


def body(
    integrals, block_list, slot_counts, coefficients, batch_index, occ_energy, vir_energy, owner_map
):
    local_rows = coefficients.shape[0]
    steps = stages(lax.axis_size("aux"))
    x = jnp.transpose(integrals, (1, 0, 2))
    buf = coefficients.T[None]
    slabs = []
    for k, step in enumerate(steps):
        far = [swap(buf, mask) for mask in step]
        if k == 0:
            levels, ids, buf, slab = prepare(
                block_list, slot_counts.reshape(1, 1), batch_index, occ_energy.reshape(-1, LANES), buf, x
            )
            slabs.append(slab)
        if k + 1 == len(steps):
            slabs.append(retile(x, 1))
        buf = jnp.concatenate([buf] + far, axis=0)
        buf, _ = lax.optimization_barrier((buf, slabs[-1]))
        x, _ = lax.optimization_barrier((x, far[0]))
    far = swap(buf, 1)
    slabs.append(retile(x, 2))
    half, send = half_transform(steps + ((1,),), ids, buf, far, slabs)
    keep = own_squares(half, send) + swap(send, 1)
    for step in reversed(steps):
        keep = sum([swap(keep, mask) for mask in step], keep)
    other = swap(keep, 1)
    vir = vir_energy.reshape(1, -1)
    own_energy, own = own_weights(keep, levels, vir, half)
    terms, energy = gradient_terms(ids, other, levels, vir, half, own_energy, own, slabs)
    buf, total, done = terms[None], None, 0
    for k, step in enumerate(steps):
        far = [swap(buf, mask) for mask in step]
        if k == 0:
            pair_energy = pair_slots(owner_map, energy)
        total = place_terms(buf[done:], total, local_rows)
        done = buf.shape[0]
        buf = jnp.concatenate([buf] + far, axis=0)
        buf, total, pair_energy = lax.optimization_barrier((buf, total, pair_energy))
    far = swap(buf, 1)
    total = place_terms(buf[done:], total, local_rows)
    grad_coef = place_terms(far, total, local_rows).T
    return (grad_coef, pair_energy)


def solution(mesh):
    return jax.shard_map(
        body,
        mesh=mesh,
        in_specs=(
            P(("groups", "aux"), None, None),
            P(("groups", "aux"), None),
            P(("groups", "aux")),
            P(("groups", "aux"), None),
            P("groups"),
            P("groups"),
            P("groups"),
            P("groups"),
        ),
        out_specs=(P(("groups", "aux"), None), P(("groups", "aux"))),
        check_vma=False,
    )
```

```python
import functools

import jax
import jax.numpy as jnp
from jax import lax
from jax.experimental import pallas as pl
from jax.experimental.pallas import tpu as pltpu
from jax.sharding import PartitionSpec as P

BW = 64
S = 5
CAP = 2
LANES = 128
HALVES = LANES // BW
TILES = BW * BW // LANES
ROWS = S * TILES
PARTS = 3
SEAT = 8
SEATS = LANES // SEAT
TERM_TILES = -(-S * BW // LANES)
F32 = jnp.float32
BF16 = jnp.bfloat16
VMEM = pl.BlockSpec(memory_space=pltpu.VMEM)
SMEM = pl.BlockSpec(memory_space=pltpu.SMEM)


def limit(orbs):
    return max(8, orbs // 4) * 2**20


def iota(shape, dim):
    return lax.broadcasted_iota(jnp.int32, shape, dim)


def split_rows(count):
    unit = count // 16
    return (unit, 13 * unit, count - 14 * unit)


def retile_rows(x, out, at):
    for s in range(S):
        out[at : at + 16, s * TILES : (s + 1) * TILES, :] = x[s, at : at + 16, :].reshape(16, TILES, LANES)


def fetch(start, x, slab, sems):
    copies = []
    for c in range(slab.shape[1] // 16):
        src = x.at[:, pl.ds(start + c * 16, 16), :]
        copies.append(pltpu.make_async_copy(src, slab.at[:, pl.ds(c * 16, 16), :], sems.at[c]))
        copies[-1].start()
    return copies


def retile_kernel(start, x, out, slab, sems):
    for c, copy in enumerate(fetch(start, x, slab, sems)):
        copy.wait()
        retile_rows(slab, out, c * 16)


def retile(x, part):
    sizes = split_rows(x.shape[1])
    start, size = sum(sizes[:part]), sizes[part]
    return pl.pallas_call(
        functools.partial(retile_kernel, start),
        in_specs=[pl.BlockSpec(memory_space=pltpu.HBM)],
        out_specs=VMEM,
        out_shape=jax.ShapeDtypeStruct((size, ROWS, LANES), BF16),
        scratch_shapes=[pltpu.VMEM((S, size, TILES * LANES), BF16), pltpu.SemaphoreType.DMA((size // 16,))],
        compiler_params=pltpu.CompilerParams(vmem_limit_bytes=10 * 2**20),
        cost_estimate=pl.CostEstimate(flops=0, bytes_accessed=4 * size * ROWS * LANES, transcendentals=0),
    )(in_hbm(x))


def prepare_kernel(blocks, counts, index, levels, coef, x, *refs):
    rows, ids, held, out = refs[:4]
    sems, own_blocks, own_index, own_levels, slab, slab_sems = refs[4:]
    pairs = (blocks, own_blocks), (index, own_index), (levels, own_levels), (coef, held)
    copies = [pltpu.make_async_copy(src, dst, sems.at[k]) for k, (src, dst) in enumerate(pairs)]
    for copy in copies:
        copy.start()
    for c, copy in enumerate(fetch(0, x, slab, slab_sems)):
        copy.wait()
        retile_rows(slab, out, c * 16)
    for copy in copies:
        copy.wait()
    lane = iota((1, LANES), 1)

    def step(i, carry):
        at = own_index[i]
        row = own_levels[pl.ds(lax.div(at, LANES), 1), :]
        rows[pl.ds(i, 1), :] = jnp.where(lane == lax.rem(at, LANES), 2.0 * row, 0.0)
        return carry

    lax.fori_loop(0, rows.shape[0], step, 0)
    rows[...] = jnp.broadcast_to(jnp.sum(rows[...], axis=1, keepdims=True), rows.shape)
    total = jnp.full(ids.shape, -1, jnp.int32)
    for s in range(S):
        total = jnp.where((lane == s) & (s < counts[...]), own_blocks[0, s], total)
    ids[...] = total


def in_hbm(x):
    return pltpu.with_memory_space_constraint(x, pltpu.HBM)


def prepare(blocks, counts, index, levels, coef, x):
    far = pl.BlockSpec(memory_space=pltpu.HBM)
    size = split_rows(x.shape[1])[0]
    return pl.pallas_call(
        prepare_kernel,
        in_specs=[far, VMEM, far, far, far, far],
        out_specs=[VMEM] * 4,
        out_shape=[
            jax.ShapeDtypeStruct((index.shape[0], LANES), F32),
            jax.ShapeDtypeStruct((1, LANES), jnp.int32),
            jax.ShapeDtypeStruct(coef.shape, coef.dtype),
            jax.ShapeDtypeStruct((size, ROWS, LANES), BF16),
        ],
        scratch_shapes=[
            pltpu.SemaphoreType.DMA((4,)),
            pltpu.SMEM(blocks.shape, blocks.dtype),
            pltpu.SMEM(index.shape, index.dtype),
            pltpu.VMEM(levels.shape, levels.dtype),
            pltpu.VMEM((S, size, TILES * LANES), BF16),
            pltpu.SemaphoreType.DMA((size // 16,)),
        ],
        compiler_params=pltpu.CompilerParams(vmem_limit_bytes=8 * 2**20),
        cost_estimate=pl.CostEstimate(flops=0, bytes_accessed=4 * size * ROWS * LANES, transcendentals=0),
    )(in_hbm(blocks), counts, in_hbm(index), in_hbm(levels), in_hbm(coef), in_hbm(x))


def stages(size):
    bits = []
    while size > 2:
        size //= 2
        bits.append(size)
    steps = [(bits.pop(0),)] if len(bits) % 2 else []
    for high, low in zip(bits[::2], bits[1::2]):
        steps.append((low, high ^ low, high))
    return tuple(steps)


def gather_index(dev, me, steps):
    rel = lax.bitwise_xor(dev, me)
    place, count = 0, 1
    for step in steps:
        low = lax.bitwise_and(rel, step[0]) != 0
        if len(step) == 1:
            place = place + jnp.where(low, count, 0)
        else:
            high = lax.bitwise_and(rel, step[2]) != 0
            place = place + jnp.where(high, jnp.where(low, 2, 3), jnp.where(low, 1, 0)) * count
        count *= len(step) + 1
    return place


def half_kernel(steps, ids, id_row, coef_a, coef_b, *refs):
    slabs, (half, send) = refs[:PARTS], refs[PARTS:]
    me = lax.axis_index("aux")
    orbs, width = coef_a.shape[1], coef_a.shape[2]
    per_dev = width // BW
    near = coef_a.shape[0]
    src = iota((LANES, LANES), 0)
    dst = iota((LANES, LANES), 1)
    wanted = (dst & BW) // BW + (dst & (TILES - 1)) * 2 + (dst & TILES) // TILES * BW
    spread = jnp.where(src == wanted, 1.0, 0.0).astype(BF16)
    picked = []
    for s in range(S):
        block = jnp.maximum(ids[0, s], 0)
        dev = lax.div(block, per_dev)
        inner = lax.rem(block, per_dev)
        place = gather_index(dev, me, steps)
        col = pl.multiple_of(lax.div(inner, HALVES) * LANES, LANES)
        spot = lax.rem(place, near)
        ours = coef_a[spot, :, pl.ds(col, LANES)]
        theirs = coef_b[spot, :, pl.ds(col, LANES)]
        picked.append(jnp.where(place < near, ours, theirs))
    apart = jnp.dot(jnp.concatenate(picked, axis=0), spread, preferred_element_type=F32)
    group = iota((orbs, LANES), 1) // TILES
    coef = [[jnp.zeros((orbs, LANES), F32) for _ in range(2)] for _ in range(HALVES)]
    for s in range(S):
        second = lax.rem(ids[0, s], HALVES) == 1
        value = apart[s * orbs : (s + 1) * orbs]
        value = jnp.where(second, pltpu.roll(value, LANES - TILES, 1), value)
        for h in range(HALVES):
            shift = (s * TILES - h * BW) % LANES
            there = pltpu.roll(value, shift, 1) if shift else value
            tile = s * TILES // LANES
            hit = (group == s % (LANES // TILES)) & (ids[0, s] >= 0)
            coef[h][tile] = jnp.where(hit, there, coef[h][tile])
    coef = jnp.concatenate([jnp.concatenate(coef[h], axis=1)[:, :ROWS] for h in range(HALVES)], axis=0).astype(BF16)
    low = iota((orbs, LANES), 1) < BW
    base = 0
    rows = []
    for slab in slabs:
        for p in range(slab.shape[0] // 2):
            both = jnp.concatenate([slab[2 * p], slab[2 * p + 1]], axis=1)
            r = jnp.dot(coef, both, preferred_element_type=F32)
            straight = jnp.where(low, r[:orbs, :LANES], r[orbs:, LANES:])
            crossed = jnp.where(low, r[:orbs, LANES:], r[orbs:, :LANES])
            rows.append(straight + pltpu.roll(crossed, BW, 1))
            if len(rows) == 16:
                half[:, base : base + 16, :] = jnp.swapaxes(jnp.stack(rows), 0, 1).astype(BF16)
                base, rows = base + 16, []
    pair_squares(half, 1 - lax.rem(me, 2), id_row, send)


def pair_squares(half, core, id_row, out):
    orbs, pairs = half.shape[0], half.shape[1]
    scale = 0.125 / (2 * pairs * lax.axis_size("aux"))
    lane = iota((BW, LANES), 1)
    left = lane < BW
    upper = iota((BW, LANES), 0) <= lax.rem(lane, BW)
    eye = iota((BW, LANES), 0) == lax.rem(lane, BW)
    quads = orbs // 8
    diags = []
    for k in range(quads):
        t = []
        for j in range(4):
            h = half[core * (orbs // 2) + 4 * k + j]
            t.append(lax.dot_general(h, h, (((0,), (0,)), ((), ())), preferred_element_type=F32) * scale)
        lefts = [t[j][:BW] + pltpu.roll(t[j][BW:], BW, 1) for j in (0, 1)]
        rights = [pltpu.roll(t[j][:BW], BW, 1) + t[j][BW:] for j in (2, 3)]
        a = jnp.where(left, lefts[0], rights[0])
        b = jnp.where(left, lefts[1], rights[1])
        out[k * BW : (k + 1) * BW, :] = jnp.where(upper, a, b)
        diags.append(jnp.sum(jnp.where(eye, b, 0.0), axis=0, keepdims=True))
    me = lax.axis_index("aux")
    spare = out.shape[0] - quads * BW - quads
    own = pltpu.roll((id_row[...] + 1).astype(F32), lax.rem(me, SEATS) * SEAT, 1)
    diags.append(jnp.where(iota((spare, LANES), 0) == lax.div(me, SEATS), own, 0.0))
    out[quads * BW :, :] = jnp.concatenate(diags, axis=0)


def own_kernel(half, id_row, out):
    pair_squares(half, lax.rem(lax.axis_index("aux"), 2), id_row, out)


def own_squares(half, ids, like):
    return pl.pallas_call(
        own_kernel,
        in_specs=[VMEM] * 2,
        out_specs=VMEM,
        out_shape=jax.ShapeDtypeStruct(like.shape, F32),
        compiler_params=pltpu.CompilerParams(vmem_limit_bytes=4 * 2**20),
        cost_estimate=pl.CostEstimate(flops=0, bytes_accessed=2 * 2**20, transcendentals=0),
    )(half, ids)


def half_transform(steps, ids, coef_a, coef_b, slabs):
    orbs = coef_a.shape[1]
    pairs = sum(s.shape[0] for s in slabs) // 2
    quads = orbs // 8
    rows = quads * BW + -(-(quads + -(-lax.axis_size("aux") // SEATS)) // 8) * 8
    packed = jax.ShapeDtypeStruct((rows, LANES), F32)
    return pl.pallas_call(
        functools.partial(half_kernel, steps),
        in_specs=[SMEM] + [VMEM] * (3 + PARTS),
        out_specs=[VMEM] * 2,
        out_shape=[jax.ShapeDtypeStruct((orbs, pairs, LANES), BF16), packed],
        compiler_params=pltpu.CompilerParams(vmem_limit_bytes=limit(orbs)),
    )(ids, ids, coef_a, coef_b, *slabs)


def weight_rows(packed, core, levels, vir, half, energy, weights):
    orbs, pairs = half.shape[0], half.shape[1]
    quads = orbs // 8
    lane = iota((BW, LANES), 1)
    row = iota((BW, LANES), 0)
    left = lane < BW
    inner = lax.rem(lane, BW)
    vir_b = jnp.concatenate([vir[...], vir[...]], axis=1)
    vir_a = jnp.sum(jnp.where((row == inner) & left, vir_b, 0.0), axis=1, keepdims=True)
    zero = jnp.zeros((BW, LANES), F32)
    scale = 0.5 / BW
    start = core * (orbs // 2)
    for k in range(0, quads, 2):
        squares = [packed[(k + j) * BW : (k + j + 1) * BW, :] for j in range(2)]
        turned = jnp.concatenate(squares, axis=0).T
        top, bottom = turned[:BW], turned[BW:]
        flips = [
            jnp.where(left, top, pltpu.roll(bottom, BW, 1)),
            jnp.where(left, pltpu.roll(top, BW, 1), bottom),
        ]
        for j in range(2):
            first = 4 * (k + j)
            diag = packed[quads * BW + k + j : quads * BW + k + j + 1, :]
            ints = [
                jnp.where(row <= inner, squares[j], flips[j]),
                jnp.where(row == inner, diag, jnp.where(row > inner, squares[j], flips[j])),
            ]
            for b in range(2):
                one, two = first + b, first + 2 + b
                level = jnp.where(left[:1], levels[pl.ds(start + one, 1), :], levels[pl.ds(start + two, 1), :])
                amps = ints[b] / ((level - vir_a) - vir_b)
                sums = jnp.sum(ints[b] * amps, axis=0, keepdims=True)
                energy[one : one + 1, :] = jnp.where(left[:1], sums, 0.0)
                energy[two : two + 1, :] = jnp.where(left[:1], 0.0, sums)
                turn = pltpu.roll(amps, BW, 1)
                for i, lows, highs in ((one, amps, turn), (two, turn, amps)):
                    square = jnp.concatenate([jnp.where(left, lows, zero), jnp.where(left, zero, highs)], axis=0)
                    w = jnp.dot(half[start + i], square.astype(BF16), preferred_element_type=F32) * scale
                    weights[i * pairs : (i + 1) * pairs, :] = w.astype(BF16).astype(F32)


def weight_kernel(packed, levels, vir, half, energy, weights):
    weight_rows(packed, lax.rem(lax.axis_index("aux"), 2), levels, vir, half, energy, weights)


def own_weights(packed, levels, vir, half):
    orbs, pairs = half.shape[0], half.shape[1]
    return pl.pallas_call(
        weight_kernel,
        in_specs=[VMEM] * 4,
        out_specs=[VMEM] * 2,
        out_shape=[
            jax.ShapeDtypeStruct((orbs // 2, LANES), F32),
            jax.ShapeDtypeStruct((orbs // 2 * pairs, LANES), F32),
        ],
        compiler_params=pltpu.CompilerParams(vmem_limit_bytes=4 * 2**20),
        cost_estimate=pl.CostEstimate(flops=0, bytes_accessed=3 * 2**20, transcendentals=0),
    )(packed, levels, vir, half)


def grad_kernel(packed, levels, vir, half, own_energy, own, *refs):
    slabs, (terms, energy, other_energy, other, mixed) = refs[:PARTS], refs[PARTS:]
    core = lax.rem(lax.axis_index("aux"), 2)
    orbs, pairs = half.shape[0], half.shape[1]
    mid = orbs // 2
    weight_rows(packed, 1 - core, levels, vir, half, other_energy, other)

    def ordered(ours, theirs):
        return jnp.concatenate([jnp.where(core == 0, ours, theirs), jnp.where(core == 0, theirs, ours)], axis=0)

    energy[...] = ordered(own_energy[...], other_energy[...])
    low = iota((orbs, LANES), 1) < BW
    blank = jnp.zeros((orbs, LANES), F32)
    total = jnp.zeros((ROWS, HALVES * orbs), F32)
    base = 0
    for slab in slabs:
        for start in range(0, slab.shape[0] // 2, 32):
            xs, ws = [], []
            for p in range(start, min(start + 32, slab.shape[0] // 2)):
                w = jnp.concatenate(
                    [
                        ref[pl.ds(g * 8 * pairs + base + p, 8, stride=pairs), :]
                        for ref in (own, other)
                        for g in range(mid // 8)
                    ],
                    axis=0,
                )
                turn = pltpu.roll(w, BW, 1)
                ws.append(jnp.concatenate([jnp.where(low, w, blank), jnp.where(low, blank, turn)], axis=0).astype(BF16))
                ws.append(jnp.concatenate([jnp.where(low, turn, blank), jnp.where(low, blank, w)], axis=0).astype(BF16))
                xs += [slab[2 * p], slab[2 * p + 1]]
            total = total + lax.dot_general(
                jnp.concatenate(xs, axis=1),
                jnp.concatenate(ws, axis=1),
                (((1,), (1,)), ((), ())),
                preferred_element_type=F32,
            )
        base += slab.shape[0] // 2
    width = mixed.shape[0]
    turn = total if HALVES * orbs > LANES else jnp.pad(total, ((0, 0), (0, LANES - HALVES * orbs)))
    for h in range(HALVES):
        rows = turn[:, h * orbs : h * orbs + LANES]
        if rows.shape[1] < LANES:
            rows = pltpu.roll(turn, LANES - h * orbs, 1)
        mixed[pl.ds(h, ROWS, stride=HALVES), :] = rows
    mixed[HALVES * ROWS :, :] = jnp.zeros((width - HALVES * ROWS, LANES), F32)
    for t in range(width // LANES):
        out = mixed[t * LANES : (t + 1) * LANES, :].T[:orbs]
        out = ordered(out[:mid], out[mid:])
        if (t + 1) * LANES > S * BW:
            out = jnp.where(low[:mid], out[:mid], pltpu.roll(out[mid:], BW, 1))
        terms[t * orbs : t * orbs + out.shape[0], :] = out


def gradient_terms(packed, levels, vir, half, own_energy, own, slabs):
    orbs, pairs = half.shape[0], half.shape[1]
    width = -(-S * BW // LANES) * LANES
    return pl.pallas_call(
        grad_kernel,
        in_specs=[VMEM] * (6 + PARTS),
        out_specs=[VMEM] * 2,
        out_shape=[jax.ShapeDtypeStruct((orbs * S * BW // LANES, LANES), F32), jax.ShapeDtypeStruct((orbs, LANES), F32)],
        scratch_shapes=[
            pltpu.VMEM(own_energy.shape, F32),
            pltpu.VMEM(own.shape, F32),
            pltpu.VMEM((width, LANES), F32),
        ],
        compiler_params=pltpu.CompilerParams(vmem_limit_bytes=limit(orbs)),
    )(packed, levels, vir, half, own_energy, own, *slabs)


def seat_kernel(start, per_dev, rels, packed, out):
    me = lax.axis_index("aux")
    side = jnp.where(iota((1, LANES), 1) < BW, 0, 1)
    for d, rel in enumerate(rels):
        dev = lax.bitwise_xor(me, rel)
        row = packed[pl.ds(start + lax.div(dev, SEATS), 1), :]
        row = pltpu.roll(row, lax.rem(SEATS - lax.rem(dev, SEATS), SEATS) * SEAT, 1)
        row = row.astype(jnp.int32) - (1 + me * per_dev)
        ids = [jnp.broadcast_to(row[:, s : s + 1], (1, LANES)) for s in range(2 * TERM_TILES)]
        for k in range(TERM_TILES):
            one, two = ids[2 * k], ids[2 * k + 1]
            out[d * SEAT + 2 * k : d * SEAT + 2 * k + 1, :] = jnp.where(side == 0, one, two) - side
            out[d * SEAT + 2 * k + 1 : d * SEAT + 2 * k + 2, :] = jnp.where(side == 0, two, one) - side


def seats(packed, orbs, rows, rels):
    start = orbs // 8 * (BW + 1)
    return pl.pallas_call(
        functools.partial(seat_kernel, start, rows // BW, rels),
        in_specs=[VMEM],
        out_specs=VMEM,
        out_shape=jax.ShapeDtypeStruct((len(rels) * SEAT, LANES), jnp.int32),
        compiler_params=pltpu.CompilerParams(vmem_limit_bytes=2 * 2**20),
        cost_estimate=pl.CostEstimate(flops=0, bytes_accessed=2**20, transcendentals=0),
    )(packed)


def place_kernel(base, piece, spots, *refs):
    out = refs[-1]
    orbs, width = out.shape
    mid = orbs // 2
    step_tiles = range(width // LANES)
    for first in range(0, orbs, 16):
        parts = [slice(r, r + 8) for r in range(first, min(first + 16, orbs), 8)]
        if len(refs) == 2:
            total = [[refs[0][r, t * LANES : (t + 1) * LANES] for t in step_tiles] for r in parts]
        else:
            total = [[jnp.zeros((8, LANES), F32) for _ in step_tiles] for _ in parts]

        def step(d, total, parts=parts):
            total = [list(row) for row in total]
            for k in range(TERM_TILES):
                at = (base + d) * SEAT + 2 * k
                spot = jnp.broadcast_to(spots[pl.ds(at, 1), :], (8, LANES))
                turn_spot = jnp.broadcast_to(spots[pl.ds(at + 1, 1), :], (8, LANES))
                values, turns = [], []
                for r in parts:
                    half = (k + 1) * LANES > S * BW
                    swapped = half and r.start >= mid
                    start = k * orbs + r.start - (mid if swapped else 0)
                    value = piece[d, start : start + 8, :]
                    turn = pltpu.roll(value, BW, 1)
                    values.append(turn if swapped else value)
                    turns.append(value if swapped else turn)
                for t in step_tiles:
                    here, there = spot == HALVES * t, turn_spot == HALVES * t
                    for r in range(len(parts)):
                        added = jnp.where(here, values[r], 0.0) + jnp.where(there, turns[r], 0.0)
                        total[r][t] = total[r][t] + added
            return total

        if piece.shape[0] <= 8:
            for d in range(piece.shape[0]):
                total = step(d, total)
        else:
            total = lax.fori_loop(0, piece.shape[0], step, total)
        for r, part in enumerate(parts):
            for t in step_tiles:
                out[part, t * LANES : (t + 1) * LANES] = total[r][t]


def place_terms(base, piece, spots, total, orbs, rows):
    args = (piece, spots) if total is None else (piece, spots, total)
    return pl.pallas_call(
        functools.partial(place_kernel, base),
        in_specs=[VMEM] * len(args),
        out_specs=VMEM,
        out_shape=jax.ShapeDtypeStruct((orbs, rows), F32),
        compiler_params=pltpu.CompilerParams(vmem_limit_bytes=8 * 2**20),
        cost_estimate=pl.CostEstimate(flops=0, bytes_accessed=4 * piece.size, transcendentals=0),
    )(*args)


def pair_kernel(owner, energy, out, held, sem):
    copy = pltpu.make_async_copy(owner, held, sem)
    copy.start()
    copy.wait()
    me = lax.axis_index("aux")

    def step(i, carry):
        rank, rows = carry
        mine = held[i] == me
        row = energy[pl.ds(i, 1), :]
        rows = [jnp.where(mine & (rank == k), row, rows[k]) for k in range(CAP)]
        return rank + jnp.where(mine, 1, 0), rows

    blank = jnp.zeros((1, LANES), F32)
    _, rows = lax.fori_loop(0, energy.shape[0], step, (jnp.int32(0), [blank] * CAP))
    for k in range(CAP):
        out[k] = jnp.sum(rows[k])


def pair_slots(owner_map, energy):
    return pl.pallas_call(
        pair_kernel,
        in_specs=[pl.BlockSpec(memory_space=pltpu.HBM), VMEM],
        out_specs=SMEM,
        out_shape=jax.ShapeDtypeStruct((CAP,), F32),
        scratch_shapes=[pltpu.SMEM(owner_map.shape, owner_map.dtype), pltpu.SemaphoreType.DMA],
        compiler_params=pltpu.CompilerParams(vmem_limit_bytes=2**20),
        cost_estimate=pl.CostEstimate(flops=0, bytes_accessed=2**20, transcendentals=0),
    )(in_hbm(owner_map), energy)


def swap(x, mask):
    size = lax.axis_size("aux")
    return lax.ppermute(x, "aux", [(i, i ^ mask) for i in range(size)])


def body(
    integrals, block_list, slot_counts, coefficients, batch_index, occ_energy, vir_energy, owner_map
):
    local_rows = coefficients.shape[0]
    steps = stages(lax.axis_size("aux"))
    x = jnp.transpose(integrals, (1, 0, 2))
    buf = coefficients.T[None]
    slabs = []
    for k, step in enumerate(steps):
        far = [swap(buf, mask) for mask in step]
        if k == 0:
            levels, ids, buf, slab = prepare(
                block_list, slot_counts.reshape(1, 1), batch_index, occ_energy.reshape(-1, LANES), buf, x
            )
            slabs.append(slab)
        if k + 1 == len(steps):
            slabs.append(retile(x, 1))
        buf = jnp.concatenate([buf] + far, axis=0)
        buf, _ = lax.optimization_barrier((buf, slabs[-1]))
        x, _ = lax.optimization_barrier((x, far[0]))
    far = swap(buf, 1)
    slabs.append(retile(x, 2))
    half, send = half_transform(steps + ((1,),), ids, buf, far, slabs)
    keep = own_squares(half, ids, send) + swap(send, 1)
    for step in reversed(steps):
        keep = sum([swap(keep, mask) for mask in step], keep)
    other = swap(keep, 1)
    vir = vir_energy.reshape(1, -1)
    own_energy, own = own_weights(keep, levels, vir, half)
    rels = [0]
    for step in steps + ((1,),):
        rels = rels + [rel ^ mask for mask in step for rel in rels]
    orbs = owner_map.shape[0]
    spots = seats(keep, orbs, local_rows, tuple(rels))
    other, spots = lax.optimization_barrier((other, spots))
    terms, energy = gradient_terms(other, levels, vir, half, own_energy, own, slabs)
    buf, total, done = terms[None], None, 0
    for k, step in enumerate(steps):
        far = [swap(buf, mask) for mask in step]
        total = place_terms(done, buf[done:], spots, total, orbs, local_rows)
        if k + 1 == len(steps):
            pair_energy = pair_slots(owner_map, energy)
            total, pair_energy = lax.optimization_barrier((total, pair_energy))
        done = buf.shape[0]
        buf = jnp.concatenate([buf] + far, axis=0)
        buf, total = lax.optimization_barrier((buf, total))
    far = swap(buf, 1)
    total = place_terms(done, buf[done:], spots, total, orbs, local_rows)
    grad_coef = place_terms(buf.shape[0], far, spots, total, orbs, local_rows).T
    return (grad_coef, pair_energy)


def solution(mesh):
    return jax.shard_map(
        body,
        mesh=mesh,
        in_specs=(
            P(("groups", "aux"), None, None),
            P(("groups", "aux"), None),
            P(("groups", "aux")),
            P(("groups", "aux"), None),
            P("groups"),
            P("groups"),
            P("groups"),
            P("groups"),
        ),
        out_specs=(P(("groups", "aux"), None), P(("groups", "aux"))),
        check_vma=False,
    )
```

```python
import functools

import jax
import jax.numpy as jnp
from jax import lax
from jax.experimental import pallas as pl
from jax.experimental.pallas import tpu as pltpu
from jax.sharding import PartitionSpec as P

BW = 64
S = 5
CAP = 2
LANES = 128
HALVES = LANES // BW
TILES = BW * BW // LANES
ROWS = S * TILES
PARTS = 3
GATHER_COEF = (1, 2, 0)
SUM_INTS = (2, 0, 1)
GATHER_TERMS = (0, 2, 1)
SEAT = 8
SEATS = LANES // SEAT
TERM_TILES = -(-S * BW // LANES)
F32 = jnp.float32
BF16 = jnp.bfloat16
VMEM = pl.BlockSpec(memory_space=pltpu.VMEM)
SMEM = pl.BlockSpec(memory_space=pltpu.SMEM)


def limit(orbs):
    return max(8, orbs // 4) * 2**20


def iota(shape, dim):
    return lax.broadcasted_iota(jnp.int32, shape, dim)


def split_rows(count):
    unit = count // 16
    return (unit, 13 * unit, count - 14 * unit), (2 * unit, unit, 0)


def retile_rows(x, at, out, to):
    for s in range(S):
        out[to : to + 16, s * TILES : (s + 1) * TILES, :] = x[s, at : at + 16, :].reshape(16, TILES, LANES)


def fetch(start, x, slab, sems, first):
    copies = []
    for c in range(slab.shape[1] // 16):
        src = x.at[:, pl.ds(start + c * 16, 16), :]
        copies.append(pltpu.make_async_copy(src, slab.at[:, pl.ds(c * 16, 16), :], sems.at[first + c]))
        copies[-1].start()
    return copies


def retile_part(start, x, raw, out, ahead, slab, sems):
    have = 0 if raw is None else raw.shape[1]
    copies = fetch(start + have, x, slab, sems, 0)
    later = [] if ahead is None else fetch(start + out.shape[0], x, ahead, sems, len(copies))
    for c in range(have // 16):
        retile_rows(raw, c * 16, out, c * 16)
    for c, copy in enumerate(copies):
        copy.wait()
        retile_rows(slab, c * 16, out, have + c * 16)
    return later


def retile_kernel(start, x, raw, out, *refs):
    ahead = refs[0] if len(refs) == 3 else None
    slab, sems = refs[-2:]
    for copy in retile_part(start, x, raw, out, ahead, slab, sems):
        copy.wait()


def retile_shapes(count, part):
    sizes, ahead = split_rows(count)
    width = TILES * LANES
    have = ahead[part - 1] if part else 0
    out = [jax.ShapeDtypeStruct((sizes[part], ROWS, LANES), BF16)]
    if ahead[part]:
        out.append(jax.ShapeDtypeStruct((S, ahead[part], width), BF16))
    scratch = [
        pltpu.VMEM((S, sizes[part] - have, width), BF16),
        pltpu.SemaphoreType.DMA(((sizes[part] - have + ahead[part]) // 16,)),
    ]
    return sum(sizes[:part]), out, scratch


def retile(x, part, raw):
    start, out, scratch = retile_shapes(x.shape[1], part)
    return pl.pallas_call(
        functools.partial(retile_kernel, start),
        in_specs=[pl.BlockSpec(memory_space=pltpu.HBM), VMEM],
        out_specs=[VMEM] * len(out),
        out_shape=out,
        scratch_shapes=scratch,
        compiler_params=pltpu.CompilerParams(vmem_limit_bytes=10 * 2**20),
        cost_estimate=pl.CostEstimate(flops=0, bytes_accessed=4 * out[0].size, transcendentals=0),
    )(in_hbm(x), raw)


def prepare_kernel(blocks, counts, coef, x, ids, held, out, ahead, sems, own_blocks, slab, slab_sems):
    pairs = (blocks, own_blocks), (coef, held)
    copies = [pltpu.make_async_copy(src, dst, sems.at[k]) for k, (src, dst) in enumerate(pairs)]
    for copy in copies:
        copy.start()
    later = retile_part(0, x, None, out, ahead, slab, slab_sems)
    for copy in copies:
        copy.wait()
    lane = iota((1, LANES), 1)
    total = jnp.full(ids.shape, -1, jnp.int32)
    for s in range(S):
        total = jnp.where((lane == s) & (s < counts[...]), own_blocks[0, s], total)
    ids[...] = total
    for copy in later:
        copy.wait()


def in_hbm(x):
    return pltpu.with_memory_space_constraint(x, pltpu.HBM)


def prepare(blocks, counts, coef, x):
    far = pl.BlockSpec(memory_space=pltpu.HBM)
    _, out, scratch = retile_shapes(x.shape[1], 0)
    return pl.pallas_call(
        prepare_kernel,
        in_specs=[far, VMEM, far, far],
        out_specs=[VMEM] * 4,
        out_shape=[
            jax.ShapeDtypeStruct((1, LANES), jnp.int32),
            jax.ShapeDtypeStruct(coef.shape, coef.dtype),
        ]
        + out,
        scratch_shapes=[pltpu.SemaphoreType.DMA((2,)), pltpu.SMEM(blocks.shape, blocks.dtype)] + scratch,
        compiler_params=pltpu.CompilerParams(vmem_limit_bytes=8 * 2**20),
        cost_estimate=pl.CostEstimate(flops=0, bytes_accessed=4 * out[0].size, transcendentals=0),
    )(in_hbm(blocks), counts, in_hbm(coef), in_hbm(x))


def level_kernel(index, levels, rows, own_index, own_levels, sems):
    pairs = (index, own_index), (levels, own_levels)
    copies = [pltpu.make_async_copy(src, dst, sems.at[k]) for k, (src, dst) in enumerate(pairs)]
    for copy in copies:
        copy.start()
    for copy in copies:
        copy.wait()
    lane = iota((1, LANES), 1)

    def step(i, carry):
        at = own_index[i]
        row = own_levels[pl.ds(lax.div(at, LANES), 1), :]
        rows[pl.ds(i, 1), :] = jnp.where(lane == lax.rem(at, LANES), 2.0 * row, 0.0)
        return carry

    lax.fori_loop(0, rows.shape[0], step, 0)
    rows[...] = jnp.broadcast_to(jnp.sum(rows[...], axis=1, keepdims=True), rows.shape)


def level_rows(index, levels):
    far = pl.BlockSpec(memory_space=pltpu.HBM)
    return pl.pallas_call(
        level_kernel,
        in_specs=[far, far],
        out_specs=VMEM,
        out_shape=jax.ShapeDtypeStruct((index.shape[0], LANES), F32),
        scratch_shapes=[
            pltpu.SMEM(index.shape, index.dtype),
            pltpu.VMEM(levels.shape, levels.dtype),
            pltpu.SemaphoreType.DMA((2,)),
        ],
        compiler_params=pltpu.CompilerParams(vmem_limit_bytes=2**20),
        cost_estimate=pl.CostEstimate(flops=0, bytes_accessed=2**20, transcendentals=0),
    )(in_hbm(index), in_hbm(levels))


def stages(size, order):
    bits = []
    while size > 2:
        size //= 2
        bits.append(size)
    steps = [(bits.pop(0),)] if len(bits) % 2 else []
    for high, low in zip(bits[::2], bits[1::2]):
        both = (low, high, high ^ low)
        steps.append(tuple(both[k] for k in order))
    return tuple(steps)


def gather_index(dev, me, steps):
    rel = lax.bitwise_xor(dev, me)
    place, count = 0, 1
    for step in steps:
        bits = lax.bitwise_and(rel, functools.reduce(int.__or__, step))
        for k, mask in enumerate(step):
            place = place + jnp.where(bits == mask, (k + 1) * count, 0)
        count *= len(step) + 1
    return place


def half_kernel(steps, ids, id_row, coef_a, coef_b, *refs):
    slabs, (half, send) = refs[:PARTS], refs[PARTS:]
    me = lax.axis_index("aux")
    orbs, width = coef_a.shape[1], coef_a.shape[2]
    per_dev = width // BW
    near = coef_a.shape[0]
    src = iota((LANES, LANES), 0)
    dst = iota((LANES, LANES), 1)
    wanted = (dst & BW) // BW + (dst & (TILES - 1)) * 2 + (dst & TILES) // TILES * BW
    spread = jnp.where(src == wanted, 1.0, 0.0).astype(BF16)
    picked = []
    for s in range(S):
        block = jnp.maximum(ids[0, s], 0)
        dev = lax.div(block, per_dev)
        inner = lax.rem(block, per_dev)
        place = gather_index(dev, me, steps)
        col = pl.multiple_of(lax.div(inner, HALVES) * LANES, LANES)
        spot = lax.rem(place, near)
        ours = coef_a[spot, :, pl.ds(col, LANES)]
        theirs = coef_b[spot, :, pl.ds(col, LANES)]
        picked.append(jnp.where(place < near, ours, theirs))
    apart = jnp.dot(jnp.concatenate(picked, axis=0), spread, preferred_element_type=F32)
    group = iota((orbs, LANES), 1) // TILES
    coef = [[jnp.zeros((orbs, LANES), F32) for _ in range(2)] for _ in range(HALVES)]
    for s in range(S):
        second = lax.rem(ids[0, s], HALVES) == 1
        value = apart[s * orbs : (s + 1) * orbs]
        value = jnp.where(second, pltpu.roll(value, LANES - TILES, 1), value)
        for h in range(HALVES):
            shift = (s * TILES - h * BW) % LANES
            there = pltpu.roll(value, shift, 1) if shift else value
            tile = s * TILES // LANES
            hit = (group == s % (LANES // TILES)) & (ids[0, s] >= 0)
            coef[h][tile] = jnp.where(hit, there, coef[h][tile])
    coef = jnp.concatenate([jnp.concatenate(coef[h], axis=1)[:, :ROWS] for h in range(HALVES)], axis=0).astype(BF16)
    low = iota((orbs, LANES), 1) < BW
    base = 0
    rows = []
    for slab in slabs:
        for p in range(slab.shape[0] // 2):
            both = jnp.concatenate([slab[2 * p], slab[2 * p + 1]], axis=1)
            r = jnp.dot(coef, both, preferred_element_type=F32)
            straight = jnp.where(low, r[:orbs, :LANES], r[orbs:, LANES:])
            crossed = jnp.where(low, r[:orbs, LANES:], r[orbs:, :LANES])
            rows.append(straight + pltpu.roll(crossed, BW, 1))
            if len(rows) == 16:
                half[:, base : base + 16, :] = jnp.swapaxes(jnp.stack(rows), 0, 1).astype(BF16)
                base, rows = base + 16, []
    pair_squares(half, 1 - lax.rem(me, 2), id_row, send)


def pair_squares(half, core, id_row, out):
    orbs, pairs = half.shape[0], half.shape[1]
    scale = 0.125 / (2 * pairs * lax.axis_size("aux"))
    lane = iota((BW, LANES), 1)
    left = lane < BW
    upper = iota((BW, LANES), 0) <= lax.rem(lane, BW)
    eye = iota((BW, LANES), 0) == lax.rem(lane, BW)
    quads = orbs // 8
    diags = []
    for k in range(quads):
        t = []
        for j in range(4):
            h = half[core * (orbs // 2) + 4 * k + j]
            t.append(lax.dot_general(h, h, (((0,), (0,)), ((), ())), preferred_element_type=F32) * scale)
        lefts = [t[j][:BW] + pltpu.roll(t[j][BW:], BW, 1) for j in (0, 1)]
        rights = [pltpu.roll(t[j][:BW], BW, 1) + t[j][BW:] for j in (2, 3)]
        a = jnp.where(left, lefts[0], rights[0])
        b = jnp.where(left, lefts[1], rights[1])
        out[k * BW : (k + 1) * BW, :] = jnp.where(upper, a, b)
        diags.append(jnp.sum(jnp.where(eye, b, 0.0), axis=0, keepdims=True))
    me = lax.axis_index("aux")
    spare = out.shape[0] - quads * BW - quads
    own = pltpu.roll((id_row[...] + 1).astype(F32), lax.rem(me, SEATS) * SEAT, 1)
    diags.append(jnp.where(iota((spare, LANES), 0) == lax.div(me, SEATS), own, 0.0))
    out[quads * BW :, :] = jnp.concatenate(diags, axis=0)


def own_kernel(half, id_row, out):
    pair_squares(half, lax.rem(lax.axis_index("aux"), 2), id_row, out)


def own_squares(half, ids, like):
    return pl.pallas_call(
        own_kernel,
        in_specs=[VMEM] * 2,
        out_specs=VMEM,
        out_shape=jax.ShapeDtypeStruct(like.shape, F32),
        compiler_params=pltpu.CompilerParams(vmem_limit_bytes=4 * 2**20),
        cost_estimate=pl.CostEstimate(flops=0, bytes_accessed=2 * 2**20, transcendentals=0),
    )(half, ids)


def half_transform(steps, ids, coef_a, coef_b, slabs):
    orbs = coef_a.shape[1]
    pairs = sum(s.shape[0] for s in slabs) // 2
    quads = orbs // 8
    rows = quads * BW + -(-(quads + -(-lax.axis_size("aux") // SEATS)) // 8) * 8
    packed = jax.ShapeDtypeStruct((rows, LANES), F32)
    return pl.pallas_call(
        functools.partial(half_kernel, steps),
        in_specs=[SMEM] + [VMEM] * (3 + PARTS),
        out_specs=[VMEM] * 2,
        out_shape=[jax.ShapeDtypeStruct((orbs, pairs, LANES), BF16), packed],
        compiler_params=pltpu.CompilerParams(vmem_limit_bytes=limit(orbs)),
    )(ids, ids, coef_a, coef_b, *slabs)


def weight_rows(packed, core, levels, vir, half, energy, weights):
    orbs, pairs = half.shape[0], half.shape[1]
    quads = orbs // 8
    lane = iota((BW, LANES), 1)
    row = iota((BW, LANES), 0)
    left = lane < BW
    inner = lax.rem(lane, BW)
    vir_b = jnp.concatenate([vir[...], vir[...]], axis=1)
    vir_a = jnp.sum(jnp.where((row == inner) & left, vir_b, 0.0), axis=1, keepdims=True)
    zero = jnp.zeros((BW, LANES), F32)
    scale = 0.5 / BW
    start = core * (orbs // 2)
    for k in range(0, quads, 2):
        squares = [packed[(k + j) * BW : (k + j + 1) * BW, :] for j in range(2)]
        turned = jnp.concatenate(squares, axis=0).T
        top, bottom = turned[:BW], turned[BW:]
        flips = [
            jnp.where(left, top, pltpu.roll(bottom, BW, 1)),
            jnp.where(left, pltpu.roll(top, BW, 1), bottom),
        ]
        for j in range(2):
            first = 4 * (k + j)
            diag = packed[quads * BW + k + j : quads * BW + k + j + 1, :]
            ints = [
                jnp.where(row <= inner, squares[j], flips[j]),
                jnp.where(row == inner, diag, jnp.where(row > inner, squares[j], flips[j])),
            ]
            for b in range(2):
                one, two = first + b, first + 2 + b
                level = jnp.where(left[:1], levels[pl.ds(start + one, 1), :], levels[pl.ds(start + two, 1), :])
                amps = ints[b] / ((level - vir_a) - vir_b)
                sums = jnp.sum(ints[b] * amps, axis=0, keepdims=True)
                energy[one : one + 1, :] = jnp.where(left[:1], sums, 0.0)
                energy[two : two + 1, :] = jnp.where(left[:1], 0.0, sums)
                turn = pltpu.roll(amps, BW, 1)
                for i, lows, highs in ((one, amps, turn), (two, turn, amps)):
                    square = jnp.concatenate([jnp.where(left, lows, zero), jnp.where(left, zero, highs)], axis=0)
                    w = jnp.dot(half[start + i], square.astype(BF16), preferred_element_type=F32) * scale
                    weights[i * pairs : (i + 1) * pairs, :] = w.astype(BF16).astype(F32)


def weight_kernel(packed, levels, vir, half, energy, weights):
    weight_rows(packed, lax.rem(lax.axis_index("aux"), 2), levels, vir, half, energy, weights)


def own_weights(packed, levels, vir, half):
    orbs, pairs = half.shape[0], half.shape[1]
    return pl.pallas_call(
        weight_kernel,
        in_specs=[VMEM] * 4,
        out_specs=[VMEM] * 2,
        out_shape=[
            jax.ShapeDtypeStruct((orbs // 2, LANES), F32),
            jax.ShapeDtypeStruct((orbs // 2 * pairs, LANES), F32),
        ],
        compiler_params=pltpu.CompilerParams(vmem_limit_bytes=4 * 2**20),
        cost_estimate=pl.CostEstimate(flops=0, bytes_accessed=3 * 2**20, transcendentals=0),
    )(packed, levels, vir, half)


def grad_kernel(packed, levels, vir, half, own_energy, own, *refs):
    slabs, (terms, energy, other_energy, other, mixed) = refs[:PARTS], refs[PARTS:]
    core = lax.rem(lax.axis_index("aux"), 2)
    orbs, pairs = half.shape[0], half.shape[1]
    mid = orbs // 2
    weight_rows(packed, 1 - core, levels, vir, half, other_energy, other)

    def ordered(ours, theirs):
        return jnp.concatenate([jnp.where(core == 0, ours, theirs), jnp.where(core == 0, theirs, ours)], axis=0)

    energy[...] = ordered(own_energy[...], other_energy[...])
    low = iota((orbs, LANES), 1) < BW
    blank = jnp.zeros((orbs, LANES), F32)
    total = jnp.zeros((ROWS, HALVES * orbs), F32)
    base = 0
    for slab in slabs:
        for start in range(0, slab.shape[0] // 2, 32):
            xs, ws = [], []
            for p in range(start, min(start + 32, slab.shape[0] // 2)):
                w = jnp.concatenate(
                    [
                        ref[pl.ds(g * 8 * pairs + base + p, 8, stride=pairs), :]
                        for ref in (own, other)
                        for g in range(mid // 8)
                    ],
                    axis=0,
                )
                turn = pltpu.roll(w, BW, 1)
                ws.append(jnp.concatenate([jnp.where(low, w, blank), jnp.where(low, blank, turn)], axis=0).astype(BF16))
                ws.append(jnp.concatenate([jnp.where(low, turn, blank), jnp.where(low, blank, w)], axis=0).astype(BF16))
                xs += [slab[2 * p], slab[2 * p + 1]]
            total = total + lax.dot_general(
                jnp.concatenate(xs, axis=1),
                jnp.concatenate(ws, axis=1),
                (((1,), (1,)), ((), ())),
                preferred_element_type=F32,
            )
        base += slab.shape[0] // 2
    width = mixed.shape[0]
    turn = total if HALVES * orbs > LANES else jnp.pad(total, ((0, 0), (0, LANES - HALVES * orbs)))
    for h in range(HALVES):
        rows = turn[:, h * orbs : h * orbs + LANES]
        if rows.shape[1] < LANES:
            rows = pltpu.roll(turn, LANES - h * orbs, 1)
        mixed[pl.ds(h, ROWS, stride=HALVES), :] = rows
    mixed[HALVES * ROWS :, :] = jnp.zeros((width - HALVES * ROWS, LANES), F32)
    for t in range(width // LANES):
        out = mixed[t * LANES : (t + 1) * LANES, :].T[:orbs]
        out = ordered(out[:mid], out[mid:])
        if (t + 1) * LANES > S * BW:
            out = jnp.where(low[:mid], out[:mid], pltpu.roll(out[mid:], BW, 1))
        terms[t * orbs : t * orbs + out.shape[0], :] = out


def gradient_terms(packed, levels, vir, half, own_energy, own, slabs):
    orbs, pairs = half.shape[0], half.shape[1]
    width = -(-S * BW // LANES) * LANES
    return pl.pallas_call(
        grad_kernel,
        in_specs=[VMEM] * (6 + PARTS),
        out_specs=[VMEM] * 2,
        out_shape=[jax.ShapeDtypeStruct((orbs * S * BW // LANES, LANES), F32), jax.ShapeDtypeStruct((orbs, LANES), F32)],
        scratch_shapes=[
            pltpu.VMEM(own_energy.shape, F32),
            pltpu.VMEM(own.shape, F32),
            pltpu.VMEM((width, LANES), F32),
        ],
        compiler_params=pltpu.CompilerParams(vmem_limit_bytes=limit(orbs)),
    )(packed, levels, vir, half, own_energy, own, *slabs)


def seat_kernel(start, per_dev, rels, packed, out):
    me = lax.axis_index("aux")
    side = jnp.where(iota((1, LANES), 1) < BW, 0, 1)
    for d, rel in enumerate(rels):
        dev = lax.bitwise_xor(me, rel)
        row = packed[pl.ds(start + lax.div(dev, SEATS), 1), :]
        row = pltpu.roll(row, lax.rem(SEATS - lax.rem(dev, SEATS), SEATS) * SEAT, 1)
        row = row.astype(jnp.int32) - (1 + me * per_dev)
        ids = [jnp.broadcast_to(row[:, s : s + 1], (1, LANES)) for s in range(2 * TERM_TILES)]
        for k in range(TERM_TILES):
            one, two = ids[2 * k], ids[2 * k + 1]
            out[d * SEAT + 2 * k : d * SEAT + 2 * k + 1, :] = jnp.where(side == 0, one, two) - side
            out[d * SEAT + 2 * k + 1 : d * SEAT + 2 * k + 2, :] = jnp.where(side == 0, two, one) - side


def seats(packed, orbs, rows, rels):
    start = orbs // 8 * (BW + 1)
    return pl.pallas_call(
        functools.partial(seat_kernel, start, rows // BW, rels),
        in_specs=[VMEM],
        out_specs=VMEM,
        out_shape=jax.ShapeDtypeStruct((len(rels) * SEAT, LANES), jnp.int32),
        compiler_params=pltpu.CompilerParams(vmem_limit_bytes=2 * 2**20),
        cost_estimate=pl.CostEstimate(flops=0, bytes_accessed=2**20, transcendentals=0),
    )(packed)


def place_kernel(base, other, piece, spots, *refs):
    out = refs[-1]
    orbs, width = out.shape
    shift = 0
    if other:
        shift = jnp.where(lax.rem(lax.axis_index("aux"), 2) == 0, 1, -1) * (width // BW)
    mid = orbs // 2
    step_tiles = range(width // LANES)
    for first in range(0, orbs, 16):
        parts = [slice(r, r + 8) for r in range(first, min(first + 16, orbs), 8)]
        if len(refs) == 2:
            total = [[refs[0][r, t * LANES : (t + 1) * LANES] for t in step_tiles] for r in parts]
        else:
            total = [[jnp.zeros((8, LANES), F32) for _ in step_tiles] for _ in parts]

        def step(d, total, parts=parts):
            total = [list(row) for row in total]
            for k in range(TERM_TILES):
                at = (base + d) * SEAT + 2 * k
                spot = jnp.broadcast_to(spots[pl.ds(at, 1), :] - shift, (8, LANES))
                turn_spot = jnp.broadcast_to(spots[pl.ds(at + 1, 1), :] - shift, (8, LANES))
                values, turns = [], []
                for r in parts:
                    half = (k + 1) * LANES > S * BW
                    swapped = half and r.start >= mid
                    start = k * orbs + r.start - (mid if swapped else 0)
                    value = piece[d, start : start + 8, :]
                    turn = pltpu.roll(value, BW, 1)
                    values.append(turn if swapped else value)
                    turns.append(value if swapped else turn)
                for t in step_tiles:
                    here, there = spot == HALVES * t, turn_spot == HALVES * t
                    for r in range(len(parts)):
                        added = jnp.where(here, values[r], 0.0) + jnp.where(there, turns[r], 0.0)
                        total[r][t] = total[r][t] + added
            return total

        if piece.shape[0] <= 8:
            for d in range(piece.shape[0]):
                total = step(d, total)
        else:
            total = lax.fori_loop(0, piece.shape[0], step, total)
        for r, part in enumerate(parts):
            for t in step_tiles:
                out[part, t * LANES : (t + 1) * LANES] = total[r][t]


def place_terms(base, other, piece, spots, total, orbs, rows):
    args = (piece, spots) if total is None else (piece, spots, total)
    return pl.pallas_call(
        functools.partial(place_kernel, base, other),
        in_specs=[VMEM] * len(args),
        out_specs=VMEM,
        out_shape=jax.ShapeDtypeStruct((orbs, rows), F32),
        compiler_params=pltpu.CompilerParams(vmem_limit_bytes=8 * 2**20),
        cost_estimate=pl.CostEstimate(flops=0, bytes_accessed=4 * piece.size, transcendentals=0),
    )(*args)


def pair_kernel(owner, energy, out, held, sem):
    copy = pltpu.make_async_copy(owner, held, sem)
    copy.start()
    copy.wait()
    me = lax.axis_index("aux")

    def step(i, carry):
        rank, rows = carry
        mine = held[i] == me
        row = energy[pl.ds(i, 1), :]
        rows = [jnp.where(mine & (rank == k), row, rows[k]) for k in range(CAP)]
        return rank + jnp.where(mine, 1, 0), rows

    blank = jnp.zeros((1, LANES), F32)
    _, rows = lax.fori_loop(0, energy.shape[0], step, (jnp.int32(0), [blank] * CAP))
    for k in range(CAP):
        out[k] = jnp.sum(rows[k])


def pair_slots(owner_map, energy):
    return pl.pallas_call(
        pair_kernel,
        in_specs=[pl.BlockSpec(memory_space=pltpu.HBM), VMEM],
        out_specs=SMEM,
        out_shape=jax.ShapeDtypeStruct((CAP,), F32),
        scratch_shapes=[pltpu.SMEM(owner_map.shape, owner_map.dtype), pltpu.SemaphoreType.DMA],
        compiler_params=pltpu.CompilerParams(vmem_limit_bytes=2**20),
        cost_estimate=pl.CostEstimate(flops=0, bytes_accessed=2**20, transcendentals=0),
    )(in_hbm(owner_map), energy)


def swap(x, mask):
    size = lax.axis_size("aux")
    return lax.ppermute(x, "aux", [(i, i ^ mask) for i in range(size)])


def body(
    integrals, block_list, slot_counts, coefficients, batch_index, occ_energy, vir_energy, owner_map
):
    local_rows = coefficients.shape[0]
    size = lax.axis_size("aux")
    steps = stages(size, GATHER_COEF)
    x = jnp.transpose(integrals, (1, 0, 2))
    buf = coefficients.T[None]
    slabs, raw = [], None
    for k, step in enumerate(steps):
        far = [swap(buf, mask) for mask in step]
        if k == 0:
            ids, buf, slab, raw = prepare(block_list, slot_counts.reshape(1, 1), buf, x)
            slabs.append(slab)
        if k + 1 == len(steps):
            slab, raw = retile(x, 1, raw)
            slabs.append(slab)
        buf = jnp.concatenate([buf] + far, axis=0)
        buf, _ = lax.optimization_barrier((buf, slabs[-1]))
        x, raw, _ = lax.optimization_barrier((x, raw, far[0]))
    far = swap(buf, 1)
    slabs += retile(x, 2, raw)
    half, send = half_transform(steps + ((1,),), ids, buf, far, slabs)
    keep = own_squares(half, ids, send) + swap(send, 1)
    for k, step in enumerate(reversed(stages(size, SUM_INTS))):
        far = [swap(keep, mask) for mask in step]
        if k == 0:
            levels = level_rows(batch_index, occ_energy.reshape(-1, LANES))
        keep = sum(far, keep)
        keep, levels = lax.optimization_barrier((keep, levels))
    other = swap(keep, 1)
    vir = vir_energy.reshape(1, -1)
    own_energy, own = own_weights(keep, levels, vir, half)
    steps = stages(size, GATHER_TERMS)
    rels = [0]
    for step in steps:
        rels = rels + [rel ^ mask for mask in step for rel in rels]
    orbs = owner_map.shape[0]
    spots = seats(keep, orbs, local_rows, tuple(rels))
    other, spots = lax.optimization_barrier((other, spots))
    terms, energy = gradient_terms(other, levels, vir, half, own_energy, own, slabs)
    buf, done, ours, theirs = terms[None], 0, None, None
    for k, step in enumerate(steps):
        far = [swap(buf, mask) for mask in step]
        piece = buf[done:]
        theirs = place_terms(done, True, piece, spots, theirs, orbs, local_rows)
        ours = place_terms(done, False, piece, spots, ours, orbs, local_rows)
        done = buf.shape[0]
        if k + 1 < len(steps):
            buf = jnp.concatenate([buf] + far, axis=0)
            buf, ours, theirs = lax.optimization_barrier((buf, ours, theirs))
    pair_energy = pair_slots(owner_map, energy)
    ours, theirs, pair_energy = lax.optimization_barrier((ours, theirs, pair_energy))
    for k, piece in enumerate(far):
        theirs = place_terms(done + k * piece.shape[0], True, piece, spots, theirs, orbs, local_rows)
    last = swap(theirs, 1)
    ours = place_terms(done, False, jnp.concatenate(far, axis=0), spots, ours, orbs, local_rows)
    grad_coef = (ours + last).T
    return (grad_coef, pair_energy)


def solution(mesh):
    return jax.shard_map(
        body,
        mesh=mesh,
        in_specs=(
            P(("groups", "aux"), None, None),
            P(("groups", "aux"), None),
            P(("groups", "aux")),
            P(("groups", "aux"), None),
            P("groups"),
            P("groups"),
            P("groups"),
            P("groups"),
        ),
        out_specs=(P(("groups", "aux"), None), P(("groups", "aux"))),
        check_vma=False,
    )
```

```python
import functools

import jax
import jax.numpy as jnp
from jax import lax
from jax.experimental import pallas as pl
from jax.experimental.pallas import tpu as pltpu
from jax.sharding import PartitionSpec as P

BW = 64
S = 5
CAP = 2
LANES = 128
HALVES = LANES // BW
TILES = BW * BW // LANES
ROWS = S * TILES
PARTS = 3
GATHER_COEF = (1, 2, 0)
SUM_INTS = (2, 0, 1)
GATHER_TERMS = (0, 2, 1)
SEAT = 8
SEATS = LANES // SEAT
TERM_TILES = -(-S * BW // LANES)
F32 = jnp.float32
BF16 = jnp.bfloat16
VMEM = pl.BlockSpec(memory_space=pltpu.VMEM)
SMEM = pl.BlockSpec(memory_space=pltpu.SMEM)


def limit(orbs):
    return max(8, orbs // 4) * 2**20


def iota(shape, dim):
    return lax.broadcasted_iota(jnp.int32, shape, dim)


def split_rows(count):
    unit = count // 16
    return (unit, 13 * unit, count - 14 * unit), (2 * unit, unit, 0)


def retile_rows(x, at, out, to):
    for s in range(S):
        out[to : to + 16, s * TILES : (s + 1) * TILES, :] = x[s, at : at + 16, :].reshape(16, TILES, LANES)


def fetch(start, x, slab, sems, first):
    copies = []
    for c in range(slab.shape[1] // 16):
        src = x.at[:, pl.ds(start + c * 16, 16), :]
        copies.append(pltpu.make_async_copy(src, slab.at[:, pl.ds(c * 16, 16), :], sems.at[first + c]))
        copies[-1].start()
    return copies


def retile_part(start, x, raw, out, ahead, slab, sems):
    have = 0 if raw is None else raw.shape[1]
    copies = fetch(start + have, x, slab, sems, 0)
    later = [] if ahead is None else fetch(start + out.shape[0], x, ahead, sems, len(copies))
    for c in range(have // 16):
        retile_rows(raw, c * 16, out, c * 16)
    for c, copy in enumerate(copies):
        copy.wait()
        retile_rows(slab, c * 16, out, have + c * 16)
    return later


def retile_kernel(start, x, raw, out, *refs):
    ahead = refs[0] if len(refs) == 3 else None
    slab, sems = refs[-2:]
    for copy in retile_part(start, x, raw, out, ahead, slab, sems):
        copy.wait()


def retile_shapes(count, part):
    sizes, ahead = split_rows(count)
    width = TILES * LANES
    have = ahead[part - 1] if part else 0
    out = [jax.ShapeDtypeStruct((sizes[part], ROWS, LANES), BF16)]
    if ahead[part]:
        out.append(jax.ShapeDtypeStruct((S, ahead[part], width), BF16))
    scratch = [
        pltpu.VMEM((S, sizes[part] - have, width), BF16),
        pltpu.SemaphoreType.DMA(((sizes[part] - have + ahead[part]) // 16,)),
    ]
    return sum(sizes[:part]), out, scratch


def retile(x, part, raw):
    start, out, scratch = retile_shapes(x.shape[1], part)
    return pl.pallas_call(
        functools.partial(retile_kernel, start),
        in_specs=[pl.BlockSpec(memory_space=pltpu.HBM), VMEM],
        out_specs=[VMEM] * len(out),
        out_shape=out,
        scratch_shapes=scratch,
        compiler_params=pltpu.CompilerParams(vmem_limit_bytes=10 * 2**20),
        cost_estimate=pl.CostEstimate(flops=0, bytes_accessed=4 * out[0].size, transcendentals=0),
    )(in_hbm(x), raw)


def prepare_kernel(blocks, counts, coef, x, ids, held, out, ahead, sems, own_blocks, slab, slab_sems):
    pairs = (blocks, own_blocks), (coef, held)
    copies = [pltpu.make_async_copy(src, dst, sems.at[k]) for k, (src, dst) in enumerate(pairs)]
    for copy in copies:
        copy.start()
    later = retile_part(0, x, None, out, ahead, slab, slab_sems)
    for copy in copies:
        copy.wait()
    lane = iota((1, LANES), 1)
    total = jnp.full(ids.shape, -1, jnp.int32)
    for s in range(S):
        total = jnp.where((lane == s) & (s < counts[...]), own_blocks[0, s], total)
    ids[...] = total
    for copy in later:
        copy.wait()


def in_hbm(x):
    return pltpu.with_memory_space_constraint(x, pltpu.HBM)


def prepare(blocks, counts, coef, x):
    far = pl.BlockSpec(memory_space=pltpu.HBM)
    _, out, scratch = retile_shapes(x.shape[1], 0)
    return pl.pallas_call(
        prepare_kernel,
        in_specs=[far, VMEM, far, far],
        out_specs=[VMEM] * 4,
        out_shape=[
            jax.ShapeDtypeStruct((1, LANES), jnp.int32),
            jax.ShapeDtypeStruct(coef.shape, coef.dtype),
        ]
        + out,
        scratch_shapes=[pltpu.SemaphoreType.DMA((2,)), pltpu.SMEM(blocks.shape, blocks.dtype)] + scratch,
        compiler_params=pltpu.CompilerParams(vmem_limit_bytes=8 * 2**20),
        cost_estimate=pl.CostEstimate(flops=0, bytes_accessed=4 * out[0].size, transcendentals=0),
    )(in_hbm(blocks), counts, in_hbm(coef), in_hbm(x))


def level_kernel(index, levels, rows, own_index, own_levels, sems):
    pairs = (index, own_index), (levels, own_levels)
    copies = [pltpu.make_async_copy(src, dst, sems.at[k]) for k, (src, dst) in enumerate(pairs)]
    for copy in copies:
        copy.start()
    for copy in copies:
        copy.wait()
    lane = iota((1, LANES), 1)

    def step(i, carry):
        at = own_index[i]
        row = own_levels[pl.ds(lax.div(at, LANES), 1), :]
        rows[pl.ds(i, 1), :] = jnp.where(lane == lax.rem(at, LANES), 2.0 * row, 0.0)
        return carry

    lax.fori_loop(0, rows.shape[0], step, 0)
    rows[...] = jnp.broadcast_to(jnp.sum(rows[...], axis=1, keepdims=True), rows.shape)


def level_rows(index, levels):
    far = pl.BlockSpec(memory_space=pltpu.HBM)
    return pl.pallas_call(
        level_kernel,
        in_specs=[far, far],
        out_specs=VMEM,
        out_shape=jax.ShapeDtypeStruct((index.shape[0], LANES), F32),
        scratch_shapes=[
            pltpu.SMEM(index.shape, index.dtype),
            pltpu.VMEM(levels.shape, levels.dtype),
            pltpu.SemaphoreType.DMA((2,)),
        ],
        compiler_params=pltpu.CompilerParams(vmem_limit_bytes=2**20),
        cost_estimate=pl.CostEstimate(flops=0, bytes_accessed=2**20, transcendentals=0),
    )(in_hbm(index), in_hbm(levels))


def stages(size, order):
    bits = []
    while size > 2:
        size //= 2
        bits.append(size)
    steps = [(bits.pop(0),)] if len(bits) % 2 else []
    for high, low in zip(bits[::2], bits[1::2]):
        both = (low, high, high ^ low)
        steps.append(tuple(both[k] for k in order))
    return tuple(steps)


def gather_index(dev, me, steps):
    rel = lax.bitwise_xor(dev, me)
    place, count = 0, 1
    for step in steps:
        bits = lax.bitwise_and(rel, functools.reduce(int.__or__, step))
        for k, mask in enumerate(step):
            place = place + jnp.where(bits == mask, (k + 1) * count, 0)
        count *= len(step) + 1
    return place


def half_kernel(steps, id_row, coef_a, coef_b, *refs):
    slabs, (half, send) = refs[:PARTS], refs[PARTS:]
    me = lax.axis_index("aux")
    orbs, width = coef_a.shape[1], coef_a.shape[2]
    per_dev = width // BW
    near = coef_a.shape[0]
    src = iota((LANES, LANES), 0)
    dst = iota((LANES, LANES), 1)
    wanted = (dst & BW) // BW + (dst & (TILES - 1)) * 2 + (dst & TILES) // TILES * BW
    spread = jnp.where(src == wanted, 1.0, 0.0).astype(BF16)
    ids = [id_row[0, s] for s in range(S)]
    picked = []
    for s in range(S):
        block = jnp.maximum(ids[s], 0)
        dev = lax.div(block, per_dev)
        inner = lax.rem(block, per_dev)
        place = gather_index(dev, me, steps)
        col = pl.multiple_of(lax.div(inner, HALVES) * LANES, LANES)
        spot = lax.rem(place, near)
        ours = coef_a[spot, :, pl.ds(col, LANES)]
        theirs = coef_b[spot, :, pl.ds(col, LANES)]
        picked.append(jnp.where(place < near, ours, theirs))
    apart = jnp.dot(jnp.concatenate(picked, axis=0), spread, preferred_element_type=F32)
    group = iota((orbs, LANES), 1) // TILES
    coef = [[jnp.zeros((orbs, LANES), F32) for _ in range(2)] for _ in range(HALVES)]
    for s in range(S):
        second = lax.rem(ids[s], HALVES) == 1
        value = apart[s * orbs : (s + 1) * orbs]
        value = jnp.where(second, pltpu.roll(value, LANES - TILES, 1), value)
        for h in range(HALVES):
            shift = (s * TILES - h * BW) % LANES
            there = pltpu.roll(value, shift, 1) if shift else value
            tile = s * TILES // LANES
            hit = (group == s % (LANES // TILES)) & (ids[s] >= 0)
            coef[h][tile] = jnp.where(hit, there, coef[h][tile])
    coef = jnp.concatenate([jnp.concatenate(coef[h], axis=1)[:, :ROWS] for h in range(HALVES)], axis=0).astype(BF16)
    low = iota((orbs, LANES), 1) < BW
    base = 0
    rows = []
    for slab in slabs:
        for p in range(slab.shape[0] // 2):
            both = jnp.concatenate([slab[2 * p], slab[2 * p + 1]], axis=1)
            r = jnp.dot(coef, both, preferred_element_type=F32)
            straight = jnp.where(low, r[:orbs, :LANES], r[orbs:, LANES:])
            crossed = jnp.where(low, r[:orbs, LANES:], r[orbs:, :LANES])
            rows.append(straight + pltpu.roll(crossed, BW, 1))
            if len(rows) == 16:
                half[:, base : base + 16, :] = jnp.swapaxes(jnp.stack(rows), 0, 1).astype(BF16)
                base, rows = base + 16, []
    pair_squares(half, 1 - lax.rem(me, 2), id_row, send)


def pair_squares(half, core, id_row, out):
    orbs, pairs = half.shape[0], half.shape[1]
    scale = 0.125 / (2 * pairs * lax.axis_size("aux"))
    lane = iota((BW, LANES), 1)
    left = lane < BW
    upper = iota((BW, LANES), 0) <= lax.rem(lane, BW)
    eye = iota((BW, LANES), 0) == lax.rem(lane, BW)
    quads = orbs // 8
    diags = []
    for k in range(quads):
        t = []
        for j in range(4):
            h = half[core * (orbs // 2) + 4 * k + j]
            t.append(lax.dot_general(h, h, (((0,), (0,)), ((), ())), preferred_element_type=F32) * scale)
        lefts = [t[j][:BW] + pltpu.roll(t[j][BW:], BW, 1) for j in (0, 1)]
        rights = [pltpu.roll(t[j][:BW], BW, 1) + t[j][BW:] for j in (2, 3)]
        a = jnp.where(left, lefts[0], rights[0])
        b = jnp.where(left, lefts[1], rights[1])
        out[k * BW : (k + 1) * BW, :] = jnp.where(upper, a, b)
        diags.append(jnp.sum(jnp.where(eye, b, 0.0), axis=0, keepdims=True))
    me = lax.axis_index("aux")
    spare = out.shape[0] - quads * BW - quads
    own = pltpu.roll((id_row[...] + 1).astype(F32), lax.rem(me, SEATS) * SEAT, 1)
    diags.append(jnp.where(iota((spare, LANES), 0) == lax.div(me, SEATS), own, 0.0))
    out[quads * BW :, :] = jnp.concatenate(diags, axis=0)


def own_kernel(half, id_row, out):
    pair_squares(half, lax.rem(lax.axis_index("aux"), 2), id_row, out)


def own_squares(half, ids, like):
    return pl.pallas_call(
        own_kernel,
        in_specs=[VMEM] * 2,
        out_specs=VMEM,
        out_shape=jax.ShapeDtypeStruct(like.shape, F32),
        compiler_params=pltpu.CompilerParams(vmem_limit_bytes=4 * 2**20),
        cost_estimate=pl.CostEstimate(flops=0, bytes_accessed=2 * 2**20, transcendentals=0),
    )(half, ids)


def half_transform(steps, ids, coef_a, coef_b, slabs):
    orbs = coef_a.shape[1]
    pairs = sum(s.shape[0] for s in slabs) // 2
    quads = orbs // 8
    rows = quads * BW + -(-(quads + -(-lax.axis_size("aux") // SEATS)) // 8) * 8
    packed = jax.ShapeDtypeStruct((rows, LANES), F32)
    return pl.pallas_call(
        functools.partial(half_kernel, steps),
        in_specs=[VMEM] * (3 + PARTS),
        out_specs=[VMEM] * 2,
        out_shape=[jax.ShapeDtypeStruct((orbs, pairs, LANES), BF16), packed],
        compiler_params=pltpu.CompilerParams(vmem_limit_bytes=limit(orbs)),
    )(ids, coef_a, coef_b, *slabs)


def weight_rows(packed, core, levels, vir, half, energy, weights):
    orbs, pairs = half.shape[0], half.shape[1]
    quads = orbs // 8
    lane = iota((BW, LANES), 1)
    row = iota((BW, LANES), 0)
    left = lane < BW
    inner = lax.rem(lane, BW)
    vir_b = jnp.concatenate([vir[...], vir[...]], axis=1)
    vir_a = jnp.sum(jnp.where((row == inner) & left, vir_b, 0.0), axis=1, keepdims=True)
    zero = jnp.zeros((BW, LANES), F32)
    scale = 0.5 / BW
    start = core * (orbs // 2)
    for k in range(0, quads, 2):
        squares = [packed[(k + j) * BW : (k + j + 1) * BW, :] for j in range(2)]
        turned = jnp.concatenate(squares, axis=0).T
        top, bottom = turned[:BW], turned[BW:]
        flips = [
            jnp.where(left, top, pltpu.roll(bottom, BW, 1)),
            jnp.where(left, pltpu.roll(top, BW, 1), bottom),
        ]
        for j in range(2):
            first = 4 * (k + j)
            diag = packed[quads * BW + k + j : quads * BW + k + j + 1, :]
            ints = [
                jnp.where(row <= inner, squares[j], flips[j]),
                jnp.where(row == inner, diag, jnp.where(row > inner, squares[j], flips[j])),
            ]
            for b in range(2):
                one, two = first + b, first + 2 + b
                level = jnp.where(left[:1], levels[pl.ds(start + one, 1), :], levels[pl.ds(start + two, 1), :])
                amps = ints[b] / ((level - vir_a) - vir_b)
                sums = jnp.sum(ints[b] * amps, axis=0, keepdims=True)
                energy[one : one + 1, :] = jnp.where(left[:1], sums, 0.0)
                energy[two : two + 1, :] = jnp.where(left[:1], 0.0, sums)
                turn = pltpu.roll(amps, BW, 1)
                for i, lows, highs in ((one, amps, turn), (two, turn, amps)):
                    square = jnp.concatenate([jnp.where(left, lows, zero), jnp.where(left, zero, highs)], axis=0)
                    w = jnp.dot(half[start + i], square.astype(BF16), preferred_element_type=F32) * scale
                    weights[i * pairs : (i + 1) * pairs, :] = w.astype(BF16).astype(F32)


def weight_kernel(other, packed, levels, vir, half, energy, weights):
    core = lax.rem(lax.axis_index("aux"), 2)
    weight_rows(packed, 1 - core if other else core, levels, vir, half, energy, weights)


def core_weights(other, packed, levels, vir, half):
    orbs, pairs = half.shape[0], half.shape[1]
    return pl.pallas_call(
        functools.partial(weight_kernel, other),
        in_specs=[VMEM] * 4,
        out_specs=[VMEM] * 2,
        out_shape=[
            jax.ShapeDtypeStruct((orbs // 2, LANES), F32),
            jax.ShapeDtypeStruct((orbs // 2 * pairs, LANES), F32),
        ],
        compiler_params=pltpu.CompilerParams(vmem_limit_bytes=4 * 2**20),
        cost_estimate=pl.CostEstimate(flops=0, bytes_accessed=3 * 2**20, transcendentals=0),
    )(packed, levels, vir, half)


def grad_kernel(own_energy, own, other_energy, other, *refs):
    slabs, (terms, energy, mixed) = refs[:PARTS], refs[PARTS:]
    core = lax.rem(lax.axis_index("aux"), 2)
    mid = own_energy.shape[0]
    orbs, pairs = 2 * mid, own.shape[0] // mid

    def ordered(ours, theirs):
        return jnp.concatenate([jnp.where(core == 0, ours, theirs), jnp.where(core == 0, theirs, ours)], axis=0)

    energy[...] = ordered(own_energy[...], other_energy[...])
    low = iota((orbs, LANES), 1) < BW
    blank = jnp.zeros((orbs, LANES), F32)
    total = jnp.zeros((ROWS, HALVES * orbs), F32)
    base = 0
    for slab in slabs:
        for start in range(0, slab.shape[0] // 2, 32):
            xs, ws = [], []
            for p in range(start, min(start + 32, slab.shape[0] // 2)):
                w = jnp.concatenate(
                    [
                        ref[pl.ds(g * 8 * pairs + base + p, 8, stride=pairs), :]
                        for ref in (own, other)
                        for g in range(mid // 8)
                    ],
                    axis=0,
                )
                turn = pltpu.roll(w, BW, 1)
                ws.append(jnp.concatenate([jnp.where(low, w, blank), jnp.where(low, blank, turn)], axis=0).astype(BF16))
                ws.append(jnp.concatenate([jnp.where(low, turn, blank), jnp.where(low, blank, w)], axis=0).astype(BF16))
                xs += [slab[2 * p], slab[2 * p + 1]]
            total = total + lax.dot_general(
                jnp.concatenate(xs, axis=1),
                jnp.concatenate(ws, axis=1),
                (((1,), (1,)), ((), ())),
                preferred_element_type=F32,
            )
        base += slab.shape[0] // 2
    width = mixed.shape[0]
    turn = total if HALVES * orbs > LANES else jnp.pad(total, ((0, 0), (0, LANES - HALVES * orbs)))
    for h in range(HALVES):
        rows = turn[:, h * orbs : h * orbs + LANES]
        if rows.shape[1] < LANES:
            rows = pltpu.roll(turn, LANES - h * orbs, 1)
        mixed[pl.ds(h, ROWS, stride=HALVES), :] = rows
    mixed[HALVES * ROWS :, :] = jnp.zeros((width - HALVES * ROWS, LANES), F32)
    for t in range(width // LANES):
        out = mixed[t * LANES : (t + 1) * LANES, :].T[:orbs]
        out = ordered(out[:mid], out[mid:])
        if (t + 1) * LANES > S * BW:
            out = jnp.where(low[:mid], out[:mid], pltpu.roll(out[mid:], BW, 1))
        terms[t * orbs : t * orbs + out.shape[0], :] = out


def gradient_terms(own_energy, own, other_energy, other, slabs):
    orbs = 2 * own_energy.shape[0]
    width = -(-S * BW // LANES) * LANES
    return pl.pallas_call(
        grad_kernel,
        in_specs=[VMEM] * (4 + PARTS),
        out_specs=[VMEM] * 2,
        out_shape=[jax.ShapeDtypeStruct((orbs * S * BW // LANES, LANES), F32), jax.ShapeDtypeStruct((orbs, LANES), F32)],
        scratch_shapes=[pltpu.VMEM((width, LANES), F32)],
        compiler_params=pltpu.CompilerParams(vmem_limit_bytes=limit(orbs)),
    )(own_energy, own, other_energy, other, *slabs)


def seat_kernel(start, per_dev, rels, packed, out):
    me = lax.axis_index("aux")
    side = jnp.where(iota((1, LANES), 1) < BW, 0, 1)
    for d, rel in enumerate(rels):
        dev = lax.bitwise_xor(me, rel)
        row = packed[pl.ds(start + lax.div(dev, SEATS), 1), :]
        row = pltpu.roll(row, lax.rem(SEATS - lax.rem(dev, SEATS), SEATS) * SEAT, 1)
        row = row.astype(jnp.int32) - (1 + me * per_dev)
        ids = [jnp.broadcast_to(row[:, s : s + 1], (1, LANES)) for s in range(2 * TERM_TILES)]
        for k in range(TERM_TILES):
            one, two = ids[2 * k], ids[2 * k + 1]
            out[d * SEAT + 2 * k : d * SEAT + 2 * k + 1, :] = jnp.where(side == 0, one, two) - side
            out[d * SEAT + 2 * k + 1 : d * SEAT + 2 * k + 2, :] = jnp.where(side == 0, two, one) - side


def seats(packed, orbs, rows, rels):
    start = orbs // 8 * (BW + 1)
    return pl.pallas_call(
        functools.partial(seat_kernel, start, rows // BW, rels),
        in_specs=[VMEM],
        out_specs=VMEM,
        out_shape=jax.ShapeDtypeStruct((len(rels) * SEAT, LANES), jnp.int32),
        compiler_params=pltpu.CompilerParams(vmem_limit_bytes=2 * 2**20),
        cost_estimate=pl.CostEstimate(flops=0, bytes_accessed=2**20, transcendentals=0),
    )(packed)


def place_kernel(base, other, piece, spots, *refs):
    out = refs[-1]
    orbs, width = out.shape
    shift = 0
    if other:
        shift = jnp.where(lax.rem(lax.axis_index("aux"), 2) == 0, 1, -1) * (width // BW)
    mid = orbs // 2
    step_tiles = range(width // LANES)
    for first in range(0, orbs, 16):
        parts = [slice(r, r + 8) for r in range(first, min(first + 16, orbs), 8)]
        if len(refs) == 2:
            total = [[refs[0][r, t * LANES : (t + 1) * LANES] for t in step_tiles] for r in parts]
        else:
            total = [[jnp.zeros((8, LANES), F32) for _ in step_tiles] for _ in parts]

        def step(d, total, parts=parts):
            total = [list(row) for row in total]
            for k in range(TERM_TILES):
                at = (base + d) * SEAT + 2 * k
                spot = jnp.broadcast_to(spots[pl.ds(at, 1), :] - shift, (8, LANES))
                turn_spot = jnp.broadcast_to(spots[pl.ds(at + 1, 1), :] - shift, (8, LANES))
                values, turns = [], []
                for r in parts:
                    half = (k + 1) * LANES > S * BW
                    swapped = half and r.start >= mid
                    start = k * orbs + r.start - (mid if swapped else 0)
                    value = piece[d, start : start + 8, :]
                    turn = pltpu.roll(value, BW, 1)
                    values.append(turn if swapped else value)
                    turns.append(value if swapped else turn)
                for t in step_tiles:
                    here, there = spot == HALVES * t, turn_spot == HALVES * t
                    for r in range(len(parts)):
                        added = jnp.where(here, values[r], 0.0) + jnp.where(there, turns[r], 0.0)
                        total[r][t] = total[r][t] + added
            return total

        if piece.shape[0] <= 8:
            for d in range(piece.shape[0]):
                total = step(d, total)
        else:
            total = lax.fori_loop(0, piece.shape[0], step, total)
        for r, part in enumerate(parts):
            for t in step_tiles:
                out[part, t * LANES : (t + 1) * LANES] = total[r][t]


def place_terms(base, other, piece, spots, total, orbs, rows):
    args = (piece, spots) if total is None else (piece, spots, total)
    return pl.pallas_call(
        functools.partial(place_kernel, base, other),
        in_specs=[VMEM] * len(args),
        out_specs=VMEM,
        out_shape=jax.ShapeDtypeStruct((orbs, rows), F32),
        compiler_params=pltpu.CompilerParams(vmem_limit_bytes=8 * 2**20),
        cost_estimate=pl.CostEstimate(flops=0, bytes_accessed=4 * piece.size, transcendentals=0),
    )(*args)


def pair_kernel(owner, energy, out, held, sem):
    copy = pltpu.make_async_copy(owner, held, sem)
    copy.start()
    copy.wait()
    me = lax.axis_index("aux")

    def step(i, carry):
        rank, rows = carry
        mine = held[i] == me
        row = energy[pl.ds(i, 1), :]
        rows = [jnp.where(mine & (rank == k), row, rows[k]) for k in range(CAP)]
        return rank + jnp.where(mine, 1, 0), rows

    blank = jnp.zeros((1, LANES), F32)
    _, rows = lax.fori_loop(0, energy.shape[0], step, (jnp.int32(0), [blank] * CAP))
    for k in range(CAP):
        out[k] = jnp.sum(rows[k])


def pair_slots(owner_map, energy):
    return pl.pallas_call(
        pair_kernel,
        in_specs=[pl.BlockSpec(memory_space=pltpu.HBM), VMEM],
        out_specs=SMEM,
        out_shape=jax.ShapeDtypeStruct((CAP,), F32),
        scratch_shapes=[pltpu.SMEM(owner_map.shape, owner_map.dtype), pltpu.SemaphoreType.DMA],
        compiler_params=pltpu.CompilerParams(vmem_limit_bytes=2**20),
        cost_estimate=pl.CostEstimate(flops=0, bytes_accessed=2**20, transcendentals=0),
    )(in_hbm(owner_map), energy)


def swap(x, mask):
    size = lax.axis_size("aux")
    return lax.ppermute(x, "aux", [(i, i ^ mask) for i in range(size)])


def body(
    integrals, block_list, slot_counts, coefficients, batch_index, occ_energy, vir_energy, owner_map
):
    local_rows = coefficients.shape[0]
    size = lax.axis_size("aux")
    steps = stages(size, GATHER_COEF)
    x = jnp.transpose(integrals, (1, 0, 2))
    buf = coefficients.T[None]
    slabs, raw = [], None
    for k, step in enumerate(steps):
        far = [swap(buf, mask) for mask in step]
        if k == 0:
            ids, buf, slab, raw = prepare(block_list, slot_counts.reshape(1, 1), buf, x)
            slabs.append(slab)
        if k + 1 == len(steps):
            slab, raw = retile(x, 1, raw)
            slabs.append(slab)
        buf = jnp.concatenate([buf] + far, axis=0)
        buf, _ = lax.optimization_barrier((buf, slabs[-1]))
        x, raw, _ = lax.optimization_barrier((x, raw, far[0]))
    far = swap(buf, 1)
    slabs += retile(x, 2, raw)
    half, send = half_transform(steps + ((1,),), ids, buf, far, slabs)
    keep = own_squares(half, ids, send) + swap(send, 1)
    for k, step in enumerate(reversed(stages(size, SUM_INTS))):
        far = [swap(keep, mask) for mask in step]
        if k == 0:
            levels = level_rows(batch_index, occ_energy.reshape(-1, LANES))
        keep = sum(far, keep)
        keep, levels = lax.optimization_barrier((keep, levels))
    other = swap(keep, 1)
    vir = vir_energy.reshape(1, -1)
    own_energy, own = core_weights(False, keep, levels, vir, half)
    steps = stages(size, GATHER_TERMS)
    rels = [0]
    for step in steps:
        rels = rels + [rel ^ mask for mask in step for rel in rels]
    orbs = owner_map.shape[0]
    spots = seats(keep, orbs, local_rows, tuple(rels))
    other, spots = lax.optimization_barrier((other, spots))
    other_energy, other = core_weights(True, other, levels, vir, half)
    terms, energy = gradient_terms(own_energy, own, other_energy, other, slabs)
    buf, done, ours, theirs = terms[None], 0, None, None
    for k, step in enumerate(steps):
        far = [swap(buf, mask) for mask in step]
        piece = buf[done:]
        theirs = place_terms(done, True, piece, spots, theirs, orbs, local_rows)
        ours = place_terms(done, False, piece, spots, ours, orbs, local_rows)
        done = buf.shape[0]
        if k + 1 < len(steps):
            buf = jnp.concatenate([buf] + far, axis=0)
            buf, ours, theirs = lax.optimization_barrier((buf, ours, theirs))
    pair_energy = pair_slots(owner_map, energy)
    ours, theirs, pair_energy = lax.optimization_barrier((ours, theirs, pair_energy))
    for k, piece in enumerate(far):
        theirs = place_terms(done + k * piece.shape[0], True, piece, spots, theirs, orbs, local_rows)
    last = swap(theirs, 1)
    ours = place_terms(done, False, jnp.concatenate(far, axis=0), spots, ours, orbs, local_rows)
    grad_coef = (ours + last).T
    return (grad_coef, pair_energy)


def solution(mesh):
    return jax.shard_map(
        body,
        mesh=mesh,
        in_specs=(
            P(("groups", "aux"), None, None),
            P(("groups", "aux"), None),
            P(("groups", "aux")),
            P(("groups", "aux"), None),
            P("groups"),
            P("groups"),
            P("groups"),
            P("groups"),
        ),
        out_specs=(P(("groups", "aux"), None), P(("groups", "aux"))),
        check_vma=False,
    )
```

```python
import functools

import jax
import jax.numpy as jnp
from jax import lax
from jax.experimental import pallas as pl
from jax.experimental.pallas import tpu as pltpu
from jax.sharding import PartitionSpec as P

BW = 64
S = 5
CAP = 2
LANES = 128
HALVES = LANES // BW
TILES = BW * BW // LANES
ROWS = S * TILES
PARTS = 3
GATHER_COEF = (1, 2, 0)
SUM_INTS = (2, 0, 1)
GATHER_TERMS = (2, 0, 1)
SEAT = 8
SEATS = LANES // SEAT
TERM_TILES = -(-S * BW // LANES)
F32 = jnp.float32
BF16 = jnp.bfloat16
VMEM = pl.BlockSpec(memory_space=pltpu.VMEM)
SMEM = pl.BlockSpec(memory_space=pltpu.SMEM)


def limit(orbs):
    return max(8, orbs // 4) * 2**20


def iota(shape, dim):
    return lax.broadcasted_iota(jnp.int32, shape, dim)


def split_rows(count):
    unit = count // 16
    return (unit, 13 * unit, count - 14 * unit), (2 * unit, unit, 0)


def retile_rows(x, at, out, to):
    for s in range(S):
        out[to : to + 16, s * TILES : (s + 1) * TILES, :] = x[s, at : at + 16, :].reshape(16, TILES, LANES)


def fetch(start, x, slab, sems, first):
    copies = []
    for c in range(slab.shape[1] // 16):
        src = x.at[:, pl.ds(start + c * 16, 16), :]
        copies.append(pltpu.make_async_copy(src, slab.at[:, pl.ds(c * 16, 16), :], sems.at[first + c]))
        copies[-1].start()
    return copies


def retile_part(start, x, raw, out, ahead, slab, sems):
    have = 0 if raw is None else raw.shape[1]
    copies = fetch(start + have, x, slab, sems, 0)
    later = [] if ahead is None else fetch(start + out.shape[0], x, ahead, sems, len(copies))
    for c in range(have // 16):
        retile_rows(raw, c * 16, out, c * 16)
    for c, copy in enumerate(copies):
        copy.wait()
        retile_rows(slab, c * 16, out, have + c * 16)
    return later


def retile_kernel(start, x, raw, out, *refs):
    ahead = refs[0] if len(refs) == 3 else None
    slab, sems = refs[-2:]
    for copy in retile_part(start, x, raw, out, ahead, slab, sems):
        copy.wait()


def retile_shapes(count, part):
    sizes, ahead = split_rows(count)
    width = TILES * LANES
    have = ahead[part - 1] if part else 0
    out = [jax.ShapeDtypeStruct((sizes[part], ROWS, LANES), BF16)]
    if ahead[part]:
        out.append(jax.ShapeDtypeStruct((S, ahead[part], width), BF16))
    scratch = [
        pltpu.VMEM((S, sizes[part] - have, width), BF16),
        pltpu.SemaphoreType.DMA(((sizes[part] - have + ahead[part]) // 16,)),
    ]
    return sum(sizes[:part]), out, scratch


def retile(x, part, raw):
    start, out, scratch = retile_shapes(x.shape[1], part)
    return pl.pallas_call(
        functools.partial(retile_kernel, start),
        in_specs=[pl.BlockSpec(memory_space=pltpu.HBM), VMEM],
        out_specs=[VMEM] * len(out),
        out_shape=out,
        scratch_shapes=scratch,
        compiler_params=pltpu.CompilerParams(vmem_limit_bytes=10 * 2**20),
        cost_estimate=pl.CostEstimate(flops=0, bytes_accessed=4 * out[0].size, transcendentals=0),
    )(in_hbm(x), raw)


def prepare_kernel(blocks, counts, coef, x, ids, held, out, ahead, sems, own_blocks, slab, slab_sems):
    pairs = (blocks, own_blocks), (coef, held)
    copies = [pltpu.make_async_copy(src, dst, sems.at[k]) for k, (src, dst) in enumerate(pairs)]
    for copy in copies:
        copy.start()
    later = retile_part(0, x, None, out, ahead, slab, slab_sems)
    for copy in copies:
        copy.wait()
    lane = iota((1, LANES), 1)
    total = jnp.full(ids.shape, -1, jnp.int32)
    for s in range(S):
        total = jnp.where((lane == s) & (s < counts[...]), own_blocks[0, s], total)
    ids[...] = total
    for copy in later:
        copy.wait()


def in_hbm(x):
    return pltpu.with_memory_space_constraint(x, pltpu.HBM)


def prepare(blocks, counts, coef, x):
    far = pl.BlockSpec(memory_space=pltpu.HBM)
    _, out, scratch = retile_shapes(x.shape[1], 0)
    return pl.pallas_call(
        prepare_kernel,
        in_specs=[far, VMEM, far, far],
        out_specs=[VMEM] * 4,
        out_shape=[
            jax.ShapeDtypeStruct((1, LANES), jnp.int32),
            jax.ShapeDtypeStruct(coef.shape, coef.dtype),
        ]
        + out,
        scratch_shapes=[pltpu.SemaphoreType.DMA((2,)), pltpu.SMEM(blocks.shape, blocks.dtype)] + scratch,
        compiler_params=pltpu.CompilerParams(vmem_limit_bytes=8 * 2**20),
        cost_estimate=pl.CostEstimate(flops=0, bytes_accessed=4 * out[0].size, transcendentals=0),
    )(in_hbm(blocks), counts, in_hbm(coef), in_hbm(x))


def level_kernel(index, levels, rows, own_index, own_levels, sems):
    pairs = (index, own_index), (levels, own_levels)
    copies = [pltpu.make_async_copy(src, dst, sems.at[k]) for k, (src, dst) in enumerate(pairs)]
    for copy in copies:
        copy.start()
    for copy in copies:
        copy.wait()
    lane = iota((1, LANES), 1)

    def step(i, carry):
        at = own_index[i]
        row = own_levels[pl.ds(lax.div(at, LANES), 1), :]
        rows[pl.ds(i, 1), :] = jnp.where(lane == lax.rem(at, LANES), 2.0 * row, 0.0)
        return carry

    lax.fori_loop(0, rows.shape[0], step, 0)
    rows[...] = jnp.broadcast_to(jnp.sum(rows[...], axis=1, keepdims=True), rows.shape)


def level_rows(index, levels):
    far = pl.BlockSpec(memory_space=pltpu.HBM)
    return pl.pallas_call(
        level_kernel,
        in_specs=[far, far],
        out_specs=VMEM,
        out_shape=jax.ShapeDtypeStruct((index.shape[0], LANES), F32),
        scratch_shapes=[
            pltpu.SMEM(index.shape, index.dtype),
            pltpu.VMEM(levels.shape, levels.dtype),
            pltpu.SemaphoreType.DMA((2,)),
        ],
        compiler_params=pltpu.CompilerParams(vmem_limit_bytes=2**20),
        cost_estimate=pl.CostEstimate(flops=0, bytes_accessed=2**20, transcendentals=0),
    )(in_hbm(index), in_hbm(levels))


def stages(size, order):
    bits = []
    while size > 2:
        size //= 2
        bits.append(size)
    steps = [(bits.pop(0),)] if len(bits) % 2 else []
    for high, low in zip(bits[::2], bits[1::2]):
        both = (low, high, high ^ low)
        steps.append(tuple(both[k] for k in order))
    return tuple(steps)


def gather_index(dev, me, steps):
    rel = lax.bitwise_xor(dev, me)
    place, count = 0, 1
    for step in steps:
        bits = lax.bitwise_and(rel, functools.reduce(int.__or__, step))
        for k, mask in enumerate(step):
            place = place + jnp.where(bits == mask, (k + 1) * count, 0)
        count *= len(step) + 1
    return place


def half_kernel(steps, id_row, coef_a, coef_b, *refs):
    slabs, (half, send) = refs[:PARTS], refs[PARTS:]
    me = lax.axis_index("aux")
    orbs, width = coef_a.shape[1], coef_a.shape[2]
    per_dev = width // BW
    near = coef_a.shape[0]
    src = iota((LANES, LANES), 0)
    dst = iota((LANES, LANES), 1)
    wanted = (dst & BW) // BW + (dst & (TILES - 1)) * 2 + (dst & TILES) // TILES * BW
    spread = jnp.where(src == wanted, 1.0, 0.0).astype(BF16)
    ids = [id_row[0, s] for s in range(S)]
    picked = []
    for s in range(S):
        block = jnp.maximum(ids[s], 0)
        dev = lax.div(block, per_dev)
        inner = lax.rem(block, per_dev)
        place = gather_index(dev, me, steps)
        col = pl.multiple_of(lax.div(inner, HALVES) * LANES, LANES)
        spot = lax.rem(place, near)
        ours = coef_a[spot, :, pl.ds(col, LANES)]
        theirs = coef_b[spot, :, pl.ds(col, LANES)]
        picked.append(jnp.where(place < near, ours, theirs))
    apart = jnp.dot(jnp.concatenate(picked, axis=0), spread, preferred_element_type=F32)
    group = iota((orbs, LANES), 1) // TILES
    coef = [[jnp.zeros((orbs, LANES), F32) for _ in range(2)] for _ in range(HALVES)]
    for s in range(S):
        second = lax.rem(ids[s], HALVES) == 1
        value = apart[s * orbs : (s + 1) * orbs]
        value = jnp.where(second, pltpu.roll(value, LANES - TILES, 1), value)
        for h in range(HALVES):
            shift = (s * TILES - h * BW) % LANES
            there = pltpu.roll(value, shift, 1) if shift else value
            tile = s * TILES // LANES
            hit = (group == s % (LANES // TILES)) & (ids[s] >= 0)
            coef[h][tile] = jnp.where(hit, there, coef[h][tile])
    coef = jnp.concatenate([jnp.concatenate(coef[h], axis=1)[:, :ROWS] for h in range(HALVES)], axis=0).astype(BF16)
    low = iota((orbs, LANES), 1) < BW
    base = 0
    rows = []
    for slab in slabs:
        for p in range(slab.shape[0] // 2):
            both = jnp.concatenate([slab[2 * p], slab[2 * p + 1]], axis=1)
            r = jnp.dot(coef, both, preferred_element_type=F32)
            straight = jnp.where(low, r[:orbs, :LANES], r[orbs:, LANES:])
            crossed = jnp.where(low, r[:orbs, LANES:], r[orbs:, :LANES])
            rows.append(straight + pltpu.roll(crossed, BW, 1))
            if len(rows) == 16:
                half[:, base : base + 16, :] = jnp.swapaxes(jnp.stack(rows), 0, 1).astype(BF16)
                base, rows = base + 16, []
    pair_squares(half, 1 - lax.rem(me, 2), id_row, send)


def pair_squares(half, core, id_row, out):
    orbs, pairs = half.shape[0], half.shape[1]
    scale = 0.125 / (2 * pairs * lax.axis_size("aux"))
    lane = iota((BW, LANES), 1)
    left = lane < BW
    upper = iota((BW, LANES), 0) <= lax.rem(lane, BW)
    eye = iota((BW, LANES), 0) == lax.rem(lane, BW)
    quads = orbs // 8
    diags = []
    for k in range(quads):
        t = []
        for j in range(4):
            h = half[core * (orbs // 2) + 4 * k + j]
            t.append(lax.dot_general(h, h, (((0,), (0,)), ((), ())), preferred_element_type=F32) * scale)
        lefts = [t[j][:BW] + pltpu.roll(t[j][BW:], BW, 1) for j in (0, 1)]
        rights = [pltpu.roll(t[j][:BW], BW, 1) + t[j][BW:] for j in (2, 3)]
        a = jnp.where(left, lefts[0], rights[0])
        b = jnp.where(left, lefts[1], rights[1])
        out[k * BW : (k + 1) * BW, :] = jnp.where(upper, a, b)
        diags.append(jnp.sum(jnp.where(eye, b, 0.0), axis=0, keepdims=True))
    me = lax.axis_index("aux")
    spare = out.shape[0] - quads * BW - quads
    own = pltpu.roll((id_row[...] + 1).astype(F32), lax.rem(me, SEATS) * SEAT, 1)
    diags.append(jnp.where(iota((spare, LANES), 0) == lax.div(me, SEATS), own, 0.0))
    out[quads * BW :, :] = jnp.concatenate(diags, axis=0)


def own_kernel(half, id_row, out):
    pair_squares(half, lax.rem(lax.axis_index("aux"), 2), id_row, out)


def own_squares(half, ids, like):
    return pl.pallas_call(
        own_kernel,
        in_specs=[VMEM] * 2,
        out_specs=VMEM,
        out_shape=jax.ShapeDtypeStruct(like.shape, F32),
        compiler_params=pltpu.CompilerParams(vmem_limit_bytes=4 * 2**20),
        cost_estimate=pl.CostEstimate(flops=0, bytes_accessed=2 * 2**20, transcendentals=0),
    )(half, ids)


def half_transform(steps, ids, coef_a, coef_b, slabs):
    orbs = coef_a.shape[1]
    pairs = sum(s.shape[0] for s in slabs) // 2
    quads = orbs // 8
    rows = quads * BW + -(-(quads + -(-lax.axis_size("aux") // SEATS)) // 8) * 8
    packed = jax.ShapeDtypeStruct((rows, LANES), F32)
    return pl.pallas_call(
        functools.partial(half_kernel, steps),
        in_specs=[VMEM] * (3 + PARTS),
        out_specs=[VMEM] * 2,
        out_shape=[jax.ShapeDtypeStruct((orbs, pairs, LANES), BF16), packed],
        compiler_params=pltpu.CompilerParams(vmem_limit_bytes=limit(orbs)),
    )(ids, coef_a, coef_b, *slabs)


def weight_rows(packed, core, levels, vir, half, energy, weights):
    orbs, pairs = half.shape[0], half.shape[1]
    quads = orbs // 8
    lane = iota((BW, LANES), 1)
    row = iota((BW, LANES), 0)
    left = lane < BW
    inner = lax.rem(lane, BW)
    vir_b = jnp.concatenate([vir[...], vir[...]], axis=1)
    vir_a = jnp.sum(jnp.where((row == inner) & left, vir_b, 0.0), axis=1, keepdims=True)
    zero = jnp.zeros((BW, LANES), F32)
    scale = 0.5 / BW
    start = core * (orbs // 2)
    for k in range(0, quads, 2):
        squares = [packed[(k + j) * BW : (k + j + 1) * BW, :] for j in range(2)]
        turned = jnp.concatenate(squares, axis=0).T
        top, bottom = turned[:BW], turned[BW:]
        flips = [
            jnp.where(left, top, pltpu.roll(bottom, BW, 1)),
            jnp.where(left, pltpu.roll(top, BW, 1), bottom),
        ]
        for j in range(2):
            first = 4 * (k + j)
            diag = packed[quads * BW + k + j : quads * BW + k + j + 1, :]
            ints = [
                jnp.where(row <= inner, squares[j], flips[j]),
                jnp.where(row == inner, diag, jnp.where(row > inner, squares[j], flips[j])),
            ]
            for b in range(2):
                one, two = first + b, first + 2 + b
                level = jnp.where(left[:1], levels[pl.ds(start + one, 1), :], levels[pl.ds(start + two, 1), :])
                amps = ints[b] / ((level - vir_a) - vir_b)
                sums = jnp.sum(ints[b] * amps, axis=0, keepdims=True)
                energy[one : one + 1, :] = jnp.where(left[:1], sums, 0.0)
                energy[two : two + 1, :] = jnp.where(left[:1], 0.0, sums)
                turn = pltpu.roll(amps, BW, 1)
                for i, lows, highs in ((one, amps, turn), (two, turn, amps)):
                    square = jnp.concatenate([jnp.where(left, lows, zero), jnp.where(left, zero, highs)], axis=0)
                    w = jnp.dot(half[start + i], square.astype(BF16), preferred_element_type=F32) * scale
                    weights[i * pairs : (i + 1) * pairs, :] = w.astype(BF16).astype(F32)


def weight_kernel(other, packed, levels, vir, half, energy, weights):
    core = lax.rem(lax.axis_index("aux"), 2)
    weight_rows(packed, 1 - core if other else core, levels, vir, half, energy, weights)


def core_weights(other, packed, levels, vir, half):
    orbs, pairs = half.shape[0], half.shape[1]
    return pl.pallas_call(
        functools.partial(weight_kernel, other),
        in_specs=[VMEM] * 4,
        out_specs=[VMEM] * 2,
        out_shape=[
            jax.ShapeDtypeStruct((orbs // 2, LANES), F32),
            jax.ShapeDtypeStruct((orbs // 2 * pairs, LANES), F32),
        ],
        compiler_params=pltpu.CompilerParams(vmem_limit_bytes=4 * 2**20),
        cost_estimate=pl.CostEstimate(flops=0, bytes_accessed=3 * 2**20, transcendentals=0),
    )(packed, levels, vir, half)


def grad_kernel(own_energy, own, other_energy, other, *refs):
    slabs, (terms, energy, mixed) = refs[:PARTS], refs[PARTS:]
    core = lax.rem(lax.axis_index("aux"), 2)
    mid = own_energy.shape[0]
    orbs, pairs = 2 * mid, own.shape[0] // mid

    def ordered(ours, theirs):
        return jnp.concatenate([jnp.where(core == 0, ours, theirs), jnp.where(core == 0, theirs, ours)], axis=0)

    energy[...] = ordered(own_energy[...], other_energy[...])
    low = iota((orbs, LANES), 1) < BW
    blank = jnp.zeros((orbs, LANES), F32)
    total = jnp.zeros((ROWS, HALVES * orbs), F32)
    base = 0
    for slab in slabs:
        for start in range(0, slab.shape[0] // 2, 32):
            xs, ws = [], []
            for p in range(start, min(start + 32, slab.shape[0] // 2)):
                w = jnp.concatenate(
                    [
                        ref[pl.ds(g * 8 * pairs + base + p, 8, stride=pairs), :]
                        for ref in (own, other)
                        for g in range(mid // 8)
                    ],
                    axis=0,
                )
                turn = pltpu.roll(w, BW, 1)
                ws.append(jnp.concatenate([jnp.where(low, w, blank), jnp.where(low, blank, turn)], axis=0).astype(BF16))
                ws.append(jnp.concatenate([jnp.where(low, turn, blank), jnp.where(low, blank, w)], axis=0).astype(BF16))
                xs += [slab[2 * p], slab[2 * p + 1]]
            total = total + lax.dot_general(
                jnp.concatenate(xs, axis=1),
                jnp.concatenate(ws, axis=1),
                (((1,), (1,)), ((), ())),
                preferred_element_type=F32,
            )
        base += slab.shape[0] // 2
    width = mixed.shape[0]
    turn = total if HALVES * orbs > LANES else jnp.pad(total, ((0, 0), (0, LANES - HALVES * orbs)))
    for h in range(HALVES):
        rows = turn[:, h * orbs : h * orbs + LANES]
        if rows.shape[1] < LANES:
            rows = pltpu.roll(turn, LANES - h * orbs, 1)
        mixed[pl.ds(h, ROWS, stride=HALVES), :] = rows
    mixed[HALVES * ROWS :, :] = jnp.zeros((width - HALVES * ROWS, LANES), F32)
    for t in range(width // LANES):
        out = mixed[t * LANES : (t + 1) * LANES, :].T[:orbs]
        out = ordered(out[:mid], out[mid:])
        if (t + 1) * LANES > S * BW:
            out = jnp.where(low[:mid], out[:mid], pltpu.roll(out[mid:], BW, 1))
        terms[t * orbs : t * orbs + out.shape[0], :] = out


def gradient_terms(own_energy, own, other_energy, other, slabs):
    orbs = 2 * own_energy.shape[0]
    width = -(-S * BW // LANES) * LANES
    return pl.pallas_call(
        grad_kernel,
        in_specs=[VMEM] * (4 + PARTS),
        out_specs=[VMEM] * 2,
        out_shape=[jax.ShapeDtypeStruct((orbs * S * BW // LANES, LANES), F32), jax.ShapeDtypeStruct((orbs, LANES), F32)],
        scratch_shapes=[pltpu.VMEM((width, LANES), F32)],
        compiler_params=pltpu.CompilerParams(vmem_limit_bytes=limit(orbs)),
    )(own_energy, own, other_energy, other, *slabs)


def seat_kernel(start, per_dev, rels, packed, out):
    me = lax.axis_index("aux")
    side = jnp.where(iota((1, LANES), 1) < BW, 0, 1)
    for d, rel in enumerate(rels):
        dev = lax.bitwise_xor(me, rel)
        row = packed[pl.ds(start + lax.div(dev, SEATS), 1), :]
        row = pltpu.roll(row, lax.rem(SEATS - lax.rem(dev, SEATS), SEATS) * SEAT, 1)
        row = row.astype(jnp.int32) - (1 + me * per_dev)
        ids = [jnp.broadcast_to(row[:, s : s + 1], (1, LANES)) for s in range(2 * TERM_TILES)]
        for k in range(TERM_TILES):
            one, two = ids[2 * k], ids[2 * k + 1]
            out[d * SEAT + 2 * k : d * SEAT + 2 * k + 1, :] = jnp.where(side == 0, one, two) - side
            out[d * SEAT + 2 * k + 1 : d * SEAT + 2 * k + 2, :] = jnp.where(side == 0, two, one) - side


def seats(packed, orbs, rows, rels):
    start = orbs // 8 * (BW + 1)
    return pl.pallas_call(
        functools.partial(seat_kernel, start, rows // BW, rels),
        in_specs=[VMEM],
        out_specs=VMEM,
        out_shape=jax.ShapeDtypeStruct((len(rels) * SEAT, LANES), jnp.int32),
        compiler_params=pltpu.CompilerParams(vmem_limit_bytes=2 * 2**20),
        cost_estimate=pl.CostEstimate(flops=0, bytes_accessed=2**20, transcendentals=0),
    )(packed)


def place_kernel(base, other, piece, spots, *refs):
    out = refs[-1]
    orbs, width = out.shape
    shift = 0
    if other:
        shift = jnp.where(lax.rem(lax.axis_index("aux"), 2) == 0, 1, -1) * (width // BW)
    mid = orbs // 2
    step_tiles = range(width // LANES)
    for first in range(0, orbs, 16):
        parts = [slice(r, r + 8) for r in range(first, min(first + 16, orbs), 8)]
        if len(refs) == 2:
            total = [[refs[0][r, t * LANES : (t + 1) * LANES] for t in step_tiles] for r in parts]
        else:
            total = [[jnp.zeros((8, LANES), F32) for _ in step_tiles] for _ in parts]

        def step(d, total, parts=parts):
            total = [list(row) for row in total]
            for k in range(TERM_TILES):
                at = (base + d) * SEAT + 2 * k
                spot = jnp.broadcast_to(spots[pl.ds(at, 1), :] - shift, (8, LANES))
                turn_spot = jnp.broadcast_to(spots[pl.ds(at + 1, 1), :] - shift, (8, LANES))
                values, turns = [], []
                for r in parts:
                    half = (k + 1) * LANES > S * BW
                    swapped = half and r.start >= mid
                    start = k * orbs + r.start - (mid if swapped else 0)
                    value = piece[d, start : start + 8, :]
                    turn = pltpu.roll(value, BW, 1)
                    values.append(turn if swapped else value)
                    turns.append(value if swapped else turn)
                for t in step_tiles:
                    here, there = spot == HALVES * t, turn_spot == HALVES * t
                    for r in range(len(parts)):
                        added = jnp.where(here, values[r], 0.0) + jnp.where(there, turns[r], 0.0)
                        total[r][t] = total[r][t] + added
            return total

        if piece.shape[0] <= 8:
            for d in range(piece.shape[0]):
                total = step(d, total)
        else:
            total = lax.fori_loop(0, piece.shape[0], step, total)
        for r, part in enumerate(parts):
            for t in step_tiles:
                out[part, t * LANES : (t + 1) * LANES] = total[r][t]


def place_terms(base, other, piece, spots, total, orbs, rows):
    args = (piece, spots) if total is None else (piece, spots, total)
    return pl.pallas_call(
        functools.partial(place_kernel, base, other),
        in_specs=[VMEM] * len(args),
        out_specs=VMEM,
        out_shape=jax.ShapeDtypeStruct((orbs, rows), F32),
        compiler_params=pltpu.CompilerParams(vmem_limit_bytes=8 * 2**20),
        cost_estimate=pl.CostEstimate(flops=0, bytes_accessed=4 * piece.size, transcendentals=0),
    )(*args)


def pair_kernel(owner, energy, out, held, sem):
    copy = pltpu.make_async_copy(owner, held, sem)
    copy.start()
    copy.wait()
    me = lax.axis_index("aux")

    def step(i, carry):
        rank, rows = carry
        mine = held[i] == me
        row = energy[pl.ds(i, 1), :]
        rows = [jnp.where(mine & (rank == k), row, rows[k]) for k in range(CAP)]
        return rank + jnp.where(mine, 1, 0), rows

    blank = jnp.zeros((1, LANES), F32)
    _, rows = lax.fori_loop(0, energy.shape[0], step, (jnp.int32(0), [blank] * CAP))
    for k in range(CAP):
        out[k] = jnp.sum(rows[k])


def pair_slots(owner_map, energy):
    return pl.pallas_call(
        pair_kernel,
        in_specs=[pl.BlockSpec(memory_space=pltpu.HBM), VMEM],
        out_specs=SMEM,
        out_shape=jax.ShapeDtypeStruct((CAP,), F32),
        scratch_shapes=[pltpu.SMEM(owner_map.shape, owner_map.dtype), pltpu.SemaphoreType.DMA],
        compiler_params=pltpu.CompilerParams(vmem_limit_bytes=2**20),
        cost_estimate=pl.CostEstimate(flops=0, bytes_accessed=2**20, transcendentals=0),
    )(in_hbm(owner_map), energy)


def swap(x, mask):
    size = lax.axis_size("aux")
    return lax.ppermute(x, "aux", [(i, i ^ mask) for i in range(size)])


def body(
    integrals, block_list, slot_counts, coefficients, batch_index, occ_energy, vir_energy, owner_map
):
    local_rows = coefficients.shape[0]
    size = lax.axis_size("aux")
    steps = stages(size, GATHER_COEF)
    x = jnp.transpose(integrals, (1, 0, 2))
    buf = coefficients.T[None]
    slabs, raw = [], None
    for k, step in enumerate(steps):
        far = [swap(buf, mask) for mask in step]
        if k == 0:
            ids, buf, slab, raw = prepare(block_list, slot_counts.reshape(1, 1), buf, x)
            slabs.append(slab)
        if k + 1 == len(steps):
            slab, raw = retile(x, 1, raw)
            slabs.append(slab)
        buf = jnp.concatenate([buf] + far, axis=0)
        buf, _ = lax.optimization_barrier((buf, slabs[-1]))
        x, raw, _ = lax.optimization_barrier((x, raw, far[0]))
    far = swap(buf, 1)
    slabs += retile(x, 2, raw)
    half, send = half_transform(steps + ((1,),), ids, buf, far, slabs)
    keep = own_squares(half, ids, send) + swap(send, 1)
    for k, step in enumerate(reversed(stages(size, SUM_INTS))):
        far = [swap(keep, mask) for mask in step]
        if k == 0:
            levels = level_rows(batch_index, occ_energy.reshape(-1, LANES))
        keep = sum(far, keep)
        keep, levels = lax.optimization_barrier((keep, levels))
    other = swap(keep, 1)
    vir = vir_energy.reshape(1, -1)
    own_energy, own = core_weights(False, keep, levels, vir, half)
    steps = stages(size, GATHER_TERMS)
    rels = [0]
    for step in steps:
        rels = rels + [rel ^ mask for mask in step for rel in rels]
    orbs = owner_map.shape[0]
    spots = seats(keep, orbs, local_rows, tuple(rels))
    other, spots = lax.optimization_barrier((other, spots))
    other_energy, other = core_weights(True, other, levels, vir, half)
    terms, energy = gradient_terms(own_energy, own, other_energy, other, slabs)
    buf, done, ours, theirs = terms[None], 0, None, None
    for k, step in enumerate(steps):
        far = [swap(buf, mask) for mask in step]
        piece = buf[done:]
        theirs = place_terms(done, True, piece, spots, theirs, orbs, local_rows)
        ours = place_terms(done, False, piece, spots, ours, orbs, local_rows)
        done = buf.shape[0]
        if k + 1 < len(steps):
            buf = jnp.concatenate([buf] + far, axis=0)
            buf, ours, theirs = lax.optimization_barrier((buf, ours, theirs))
    pair_energy = pair_slots(owner_map, energy)
    ours, theirs, pair_energy = lax.optimization_barrier((ours, theirs, pair_energy))
    for k, piece in enumerate(far):
        theirs = place_terms(done + k * piece.shape[0], True, piece, spots, theirs, orbs, local_rows)
    last = swap(theirs, 1)
    ours = place_terms(done, False, jnp.concatenate(far, axis=0), spots, ours, orbs, local_rows)
    grad_coef = (ours + last).T
    return (grad_coef, pair_energy)


def solution(mesh):
    return jax.shard_map(
        body,
        mesh=mesh,
        in_specs=(
            P(("groups", "aux"), None, None),
            P(("groups", "aux"), None),
            P(("groups", "aux")),
            P(("groups", "aux"), None),
            P("groups"),
            P("groups"),
            P("groups"),
            P("groups"),
        ),
        out_specs=(P(("groups", "aux"), None), P(("groups", "aux"))),
        check_vma=False,
    )
```

```python
import functools

import jax
import jax.numpy as jnp
from jax import lax
from jax.experimental import pallas as pl
from jax.experimental.pallas import tpu as pltpu
from jax.sharding import PartitionSpec as P

BW = 64
S = 5
CAP = 2
LANES = 128
HALVES = LANES // BW
TILES = BW * BW // LANES
ROWS = S * TILES
PARTS = 3
GATHER_COEF = (1, 2, 0)
SUM_INTS = (2, 0, 1)
GATHER_TERMS = (2, 0, 1)
SEAT = 8
SEATS = LANES // SEAT
TERM_TILES = -(-S * BW // LANES)
F32 = jnp.float32
BF16 = jnp.bfloat16
VMEM = pl.BlockSpec(memory_space=pltpu.VMEM)
SMEM = pl.BlockSpec(memory_space=pltpu.SMEM)


def limit(orbs):
    return max(8, orbs // 4) * 2**20


def iota(shape, dim):
    return lax.broadcasted_iota(jnp.int32, shape, dim)


def split_rows(count):
    unit = count // 16
    return (unit, 13 * unit, count - 14 * unit), (2 * unit, unit, 0)


def retile_rows(x, at, out, to):
    for s in range(S):
        out[to : to + 16, s * TILES : (s + 1) * TILES, :] = x[s, at : at + 16, :].reshape(16, TILES, LANES)


def fetch(start, x, slab, sems, first):
    copies = []
    for c in range(slab.shape[1] // 16):
        src = x.at[:, pl.ds(start + c * 16, 16), :]
        copies.append(pltpu.make_async_copy(src, slab.at[:, pl.ds(c * 16, 16), :], sems.at[first + c]))
        copies[-1].start()
    return copies


def retile_part(start, x, raw, out, ahead, slab, sems):
    have = 0 if raw is None else raw.shape[1]
    copies = fetch(start + have, x, slab, sems, 0)
    later = [] if ahead is None else fetch(start + out.shape[0], x, ahead, sems, len(copies))
    for c in range(have // 16):
        retile_rows(raw, c * 16, out, c * 16)
    for c, copy in enumerate(copies):
        copy.wait()
        retile_rows(slab, c * 16, out, have + c * 16)
    return later


def retile_kernel(start, x, raw, out, *refs):
    ahead = refs[0] if len(refs) == 3 else None
    slab, sems = refs[-2:]
    for copy in retile_part(start, x, raw, out, ahead, slab, sems):
        copy.wait()


def retile_shapes(count, part):
    sizes, ahead = split_rows(count)
    width = TILES * LANES
    have = ahead[part - 1] if part else 0
    out = [jax.ShapeDtypeStruct((sizes[part], ROWS, LANES), BF16)]
    if ahead[part]:
        out.append(jax.ShapeDtypeStruct((S, ahead[part], width), BF16))
    scratch = [
        pltpu.VMEM((S, sizes[part] - have, width), BF16),
        pltpu.SemaphoreType.DMA(((sizes[part] - have + ahead[part]) // 16,)),
    ]
    return sum(sizes[:part]), out, scratch


def retile(x, part, raw):
    start, out, scratch = retile_shapes(x.shape[1], part)
    return pl.pallas_call(
        functools.partial(retile_kernel, start),
        in_specs=[pl.BlockSpec(memory_space=pltpu.HBM), VMEM],
        out_specs=[VMEM] * len(out),
        out_shape=out,
        scratch_shapes=scratch,
        compiler_params=pltpu.CompilerParams(vmem_limit_bytes=10 * 2**20),
        cost_estimate=pl.CostEstimate(flops=0, bytes_accessed=4 * out[0].size, transcendentals=0),
    )(in_hbm(x), raw)


def prepare_kernel(blocks, counts, coef, x, ids, held, out, ahead, sems, own_blocks, slab, slab_sems):
    pairs = (blocks, own_blocks), (coef, held)
    copies = [pltpu.make_async_copy(src, dst, sems.at[k]) for k, (src, dst) in enumerate(pairs)]
    for copy in copies:
        copy.start()
    later = retile_part(0, x, None, out, ahead, slab, slab_sems)
    for copy in copies:
        copy.wait()
    lane = iota((1, LANES), 1)
    total = jnp.full(ids.shape, -1, jnp.int32)
    for s in range(S):
        total = jnp.where((lane == s) & (s < counts[...]), own_blocks[0, s], total)
    ids[...] = total
    for copy in later:
        copy.wait()


def in_hbm(x):
    return pltpu.with_memory_space_constraint(x, pltpu.HBM)


def prepare(blocks, counts, coef, x):
    far = pl.BlockSpec(memory_space=pltpu.HBM)
    _, out, scratch = retile_shapes(x.shape[1], 0)
    return pl.pallas_call(
        prepare_kernel,
        in_specs=[far, VMEM, far, far],
        out_specs=[VMEM] * 4,
        out_shape=[
            jax.ShapeDtypeStruct((1, LANES), jnp.int32),
            jax.ShapeDtypeStruct(coef.shape, coef.dtype),
        ]
        + out,
        scratch_shapes=[pltpu.SemaphoreType.DMA((2,)), pltpu.SMEM(blocks.shape, blocks.dtype)] + scratch,
        compiler_params=pltpu.CompilerParams(vmem_limit_bytes=8 * 2**20),
        cost_estimate=pl.CostEstimate(flops=0, bytes_accessed=4 * out[0].size, transcendentals=0),
    )(in_hbm(blocks), counts, in_hbm(coef), in_hbm(x))


def level_kernel(index, levels, owner, rows, slots, own_index, own_levels, held, sems):
    pairs = (index, own_index), (levels, own_levels), (owner, held)
    copies = [pltpu.make_async_copy(src, dst, sems.at[k]) for k, (src, dst) in enumerate(pairs)]
    for copy in copies:
        copy.start()
    for copy in copies:
        copy.wait()
    me = lax.axis_index("aux")
    lane = iota((1, LANES), 1)

    def step(i, rank):
        at = own_index[i]
        row = own_levels[pl.ds(lax.div(at, LANES), 1), :]
        rows[pl.ds(i, 1), :] = jnp.where(lane == lax.rem(at, LANES), 2.0 * row, 0.0)
        mine = held[i] == me
        slots[pl.ds(i, 1), :] = jnp.broadcast_to(jnp.where(mine, rank, -1), (1, LANES))
        return rank + jnp.where(mine, 1, 0)

    lax.fori_loop(0, rows.shape[0], step, jnp.int32(0))
    rows[...] = jnp.broadcast_to(jnp.sum(rows[...], axis=1, keepdims=True), rows.shape)


def level_rows(index, levels, owner):
    far = pl.BlockSpec(memory_space=pltpu.HBM)
    shape = (index.shape[0], LANES)
    return pl.pallas_call(
        level_kernel,
        in_specs=[far] * 3,
        out_specs=[VMEM] * 2,
        out_shape=[jax.ShapeDtypeStruct(shape, F32), jax.ShapeDtypeStruct(shape, jnp.int32)],
        scratch_shapes=[
            pltpu.SMEM(index.shape, index.dtype),
            pltpu.VMEM(levels.shape, levels.dtype),
            pltpu.SMEM(owner.shape, owner.dtype),
            pltpu.SemaphoreType.DMA((3,)),
        ],
        compiler_params=pltpu.CompilerParams(vmem_limit_bytes=2**20),
        cost_estimate=pl.CostEstimate(flops=0, bytes_accessed=2**20, transcendentals=0),
    )(in_hbm(index), in_hbm(levels), in_hbm(owner))


def stages(size, order):
    bits = []
    while size > 2:
        size //= 2
        bits.append(size)
    steps = [(bits.pop(0),)] if len(bits) % 2 else []
    for high, low in zip(bits[::2], bits[1::2]):
        both = (low, high, high ^ low)
        steps.append(tuple(both[k] for k in order))
    return tuple(steps)


def gather_index(dev, me, steps):
    rel = lax.bitwise_xor(dev, me)
    place, count = 0, 1
    for step in steps:
        bits = lax.bitwise_and(rel, functools.reduce(int.__or__, step))
        for k, mask in enumerate(step):
            place = place + jnp.where(bits == mask, (k + 1) * count, 0)
        count *= len(step) + 1
    return place


def half_kernel(steps, id_row, coef_a, coef_b, *refs):
    slabs, (half, send) = refs[:PARTS], refs[PARTS:]
    me = lax.axis_index("aux")
    orbs, width = coef_a.shape[1], coef_a.shape[2]
    per_dev = width // BW
    near = coef_a.shape[0]
    src = iota((LANES, LANES), 0)
    dst = iota((LANES, LANES), 1)
    wanted = (dst & BW) // BW + (dst & (TILES - 1)) * 2 + (dst & TILES) // TILES * BW
    spread = jnp.where(src == wanted, 1.0, 0.0).astype(BF16)
    ids = [id_row[0, s] for s in range(S)]
    picked = []
    for s in range(S):
        block = jnp.maximum(ids[s], 0)
        dev = lax.div(block, per_dev)
        inner = lax.rem(block, per_dev)
        place = gather_index(dev, me, steps)
        col = pl.multiple_of(lax.div(inner, HALVES) * LANES, LANES)
        spot = lax.rem(place, near)
        ours = coef_a[spot, :, pl.ds(col, LANES)]
        theirs = coef_b[spot, :, pl.ds(col, LANES)]
        picked.append(jnp.where(place < near, ours, theirs))
    apart = jnp.dot(jnp.concatenate(picked, axis=0), spread, preferred_element_type=F32)
    group = iota((orbs, LANES), 1) // TILES
    coef = [[jnp.zeros((orbs, LANES), F32) for _ in range(2)] for _ in range(HALVES)]
    for s in range(S):
        second = lax.rem(ids[s], HALVES) == 1
        value = apart[s * orbs : (s + 1) * orbs]
        value = jnp.where(second, pltpu.roll(value, LANES - TILES, 1), value)
        for h in range(HALVES):
            shift = (s * TILES - h * BW) % LANES
            there = pltpu.roll(value, shift, 1) if shift else value
            tile = s * TILES // LANES
            hit = (group == s % (LANES // TILES)) & (ids[s] >= 0)
            coef[h][tile] = jnp.where(hit, there, coef[h][tile])
    coef = jnp.concatenate([jnp.concatenate(coef[h], axis=1)[:, :ROWS] for h in range(HALVES)], axis=0).astype(BF16)
    low = iota((orbs, LANES), 1) < BW
    base = 0
    rows = []
    for slab in slabs:
        for p in range(slab.shape[0] // 2):
            both = jnp.concatenate([slab[2 * p], slab[2 * p + 1]], axis=1)
            r = jnp.dot(coef, both, preferred_element_type=F32)
            straight = jnp.where(low, r[:orbs, :LANES], r[orbs:, LANES:])
            crossed = jnp.where(low, r[:orbs, LANES:], r[orbs:, :LANES])
            rows.append(straight + pltpu.roll(crossed, BW, 1))
            if len(rows) == 16:
                half[:, base : base + 16, :] = jnp.swapaxes(jnp.stack(rows), 0, 1).astype(BF16)
                base, rows = base + 16, []
    pair_squares(half, 1 - lax.rem(me, 2), id_row, send)


def pair_squares(half, core, id_row, out):
    orbs, pairs = half.shape[0], half.shape[1]
    scale = 0.125 / (2 * pairs * lax.axis_size("aux"))
    lane = iota((BW, LANES), 1)
    left = lane < BW
    upper = iota((BW, LANES), 0) <= lax.rem(lane, BW)
    eye = iota((BW, LANES), 0) == lax.rem(lane, BW)
    quads = orbs // 8
    diags = []
    for k in range(quads):
        t = []
        for j in range(4):
            h = half[core * (orbs // 2) + 4 * k + j]
            t.append(lax.dot_general(h, h, (((0,), (0,)), ((), ())), preferred_element_type=F32) * scale)
        lefts = [t[j][:BW] + pltpu.roll(t[j][BW:], BW, 1) for j in (0, 1)]
        rights = [pltpu.roll(t[j][:BW], BW, 1) + t[j][BW:] for j in (2, 3)]
        a = jnp.where(left, lefts[0], rights[0])
        b = jnp.where(left, lefts[1], rights[1])
        out[k * BW : (k + 1) * BW, :] = jnp.where(upper, a, b)
        diags.append(jnp.sum(jnp.where(eye, b, 0.0), axis=0, keepdims=True))
    me = lax.axis_index("aux")
    spare = out.shape[0] - quads * BW - quads
    own = pltpu.roll((id_row[...] + 1).astype(F32), lax.rem(me, SEATS) * SEAT, 1)
    diags.append(jnp.where(iota((spare, LANES), 0) == lax.div(me, SEATS), own, 0.0))
    out[quads * BW :, :] = jnp.concatenate(diags, axis=0)


def own_kernel(half, id_row, out):
    pair_squares(half, lax.rem(lax.axis_index("aux"), 2), id_row, out)


def own_squares(half, ids, like):
    return pl.pallas_call(
        own_kernel,
        in_specs=[VMEM] * 2,
        out_specs=VMEM,
        out_shape=jax.ShapeDtypeStruct(like.shape, F32),
        compiler_params=pltpu.CompilerParams(vmem_limit_bytes=4 * 2**20),
        cost_estimate=pl.CostEstimate(flops=0, bytes_accessed=2 * 2**20, transcendentals=0),
    )(half, ids)


def half_transform(steps, ids, coef_a, coef_b, slabs):
    orbs = coef_a.shape[1]
    pairs = sum(s.shape[0] for s in slabs) // 2
    quads = orbs // 8
    rows = quads * BW + -(-(quads + -(-lax.axis_size("aux") // SEATS)) // 8) * 8
    packed = jax.ShapeDtypeStruct((rows, LANES), F32)
    return pl.pallas_call(
        functools.partial(half_kernel, steps),
        in_specs=[VMEM] * (3 + PARTS),
        out_specs=[VMEM] * 2,
        out_shape=[jax.ShapeDtypeStruct((orbs, pairs, LANES), BF16), packed],
        compiler_params=pltpu.CompilerParams(vmem_limit_bytes=limit(orbs)),
    )(ids, coef_a, coef_b, *slabs)


def weight_rows(packed, core, levels, vir, half, energy, weights):
    orbs, pairs = half.shape[0], half.shape[1]
    quads = orbs // 8
    lane = iota((BW, LANES), 1)
    row = iota((BW, LANES), 0)
    left = lane < BW
    inner = lax.rem(lane, BW)
    vir_b = jnp.concatenate([vir[...], vir[...]], axis=1)
    vir_a = jnp.sum(jnp.where((row == inner) & left, vir_b, 0.0), axis=1, keepdims=True)
    zero = jnp.zeros((BW, LANES), F32)
    scale = 0.5 / BW
    start = core * (orbs // 2)
    for k in range(0, quads, 2):
        squares = [packed[(k + j) * BW : (k + j + 1) * BW, :] for j in range(2)]
        turned = jnp.concatenate(squares, axis=0).T
        top, bottom = turned[:BW], turned[BW:]
        flips = [
            jnp.where(left, top, pltpu.roll(bottom, BW, 1)),
            jnp.where(left, pltpu.roll(top, BW, 1), bottom),
        ]
        for j in range(2):
            first = 4 * (k + j)
            diag = packed[quads * BW + k + j : quads * BW + k + j + 1, :]
            ints = [
                jnp.where(row <= inner, squares[j], flips[j]),
                jnp.where(row == inner, diag, jnp.where(row > inner, squares[j], flips[j])),
            ]
            for b in range(2):
                one, two = first + b, first + 2 + b
                level = jnp.where(left[:1], levels[pl.ds(start + one, 1), :], levels[pl.ds(start + two, 1), :])
                amps = ints[b] / ((level - vir_a) - vir_b)
                sums = jnp.sum(ints[b] * amps, axis=0, keepdims=True)
                energy[one : one + 1, :] = jnp.where(left[:1], sums, 0.0)
                energy[two : two + 1, :] = jnp.where(left[:1], 0.0, sums)
                turn = pltpu.roll(amps, BW, 1)
                for i, lows, highs in ((one, amps, turn), (two, turn, amps)):
                    square = jnp.concatenate([jnp.where(left, lows, zero), jnp.where(left, zero, highs)], axis=0)
                    w = jnp.dot(half[start + i], square.astype(BF16), preferred_element_type=F32) * scale
                    weights[i * pairs : (i + 1) * pairs, :] = w.astype(BF16).astype(F32)


def weight_kernel(other, packed, levels, vir, half, energy, weights):
    core = lax.rem(lax.axis_index("aux"), 2)
    weight_rows(packed, 1 - core if other else core, levels, vir, half, energy, weights)


def core_weights(other, packed, levels, vir, half):
    orbs, pairs = half.shape[0], half.shape[1]
    return pl.pallas_call(
        functools.partial(weight_kernel, other),
        in_specs=[VMEM] * 4,
        out_specs=[VMEM] * 2,
        out_shape=[
            jax.ShapeDtypeStruct((orbs // 2, LANES), F32),
            jax.ShapeDtypeStruct((orbs // 2 * pairs, LANES), F32),
        ],
        compiler_params=pltpu.CompilerParams(vmem_limit_bytes=4 * 2**20),
        cost_estimate=pl.CostEstimate(flops=0, bytes_accessed=3 * 2**20, transcendentals=0),
    )(packed, levels, vir, half)


def grad_kernel(own_energy, own, other_energy, other, *refs):
    slabs, (terms, energy, mixed) = refs[:PARTS], refs[PARTS:]
    core = lax.rem(lax.axis_index("aux"), 2)
    mid = own_energy.shape[0]
    orbs, pairs = 2 * mid, own.shape[0] // mid

    def ordered(ours, theirs):
        return jnp.concatenate([jnp.where(core == 0, ours, theirs), jnp.where(core == 0, theirs, ours)], axis=0)

    energy[...] = ordered(own_energy[...], other_energy[...])
    low = iota((orbs, LANES), 1) < BW
    blank = jnp.zeros((orbs, LANES), F32)
    total = jnp.zeros((ROWS, HALVES * orbs), F32)
    base = 0
    for slab in slabs:
        for start in range(0, slab.shape[0] // 2, 32):
            xs, ws = [], []
            for p in range(start, min(start + 32, slab.shape[0] // 2)):
                w = jnp.concatenate(
                    [
                        ref[pl.ds(g * 8 * pairs + base + p, 8, stride=pairs), :]
                        for ref in (own, other)
                        for g in range(mid // 8)
                    ],
                    axis=0,
                )
                turn = pltpu.roll(w, BW, 1)
                ws.append(jnp.concatenate([jnp.where(low, w, blank), jnp.where(low, blank, turn)], axis=0).astype(BF16))
                ws.append(jnp.concatenate([jnp.where(low, turn, blank), jnp.where(low, blank, w)], axis=0).astype(BF16))
                xs += [slab[2 * p], slab[2 * p + 1]]
            total = total + lax.dot_general(
                jnp.concatenate(xs, axis=1),
                jnp.concatenate(ws, axis=1),
                (((1,), (1,)), ((), ())),
                preferred_element_type=F32,
            )
        base += slab.shape[0] // 2
    width = mixed.shape[0]
    turn = total if HALVES * orbs > LANES else jnp.pad(total, ((0, 0), (0, LANES - HALVES * orbs)))
    for h in range(HALVES):
        rows = turn[:, h * orbs : h * orbs + LANES]
        if rows.shape[1] < LANES:
            rows = pltpu.roll(turn, LANES - h * orbs, 1)
        mixed[pl.ds(h, ROWS, stride=HALVES), :] = rows
    mixed[HALVES * ROWS :, :] = jnp.zeros((width - HALVES * ROWS, LANES), F32)
    for t in range(width // LANES):
        out = mixed[t * LANES : (t + 1) * LANES, :].T[:orbs]
        out = ordered(out[:mid], out[mid:])
        if (t + 1) * LANES > S * BW:
            out = jnp.where(low[:mid], out[:mid], pltpu.roll(out[mid:], BW, 1))
        terms[t * orbs : t * orbs + out.shape[0], :] = out


def gradient_terms(own_energy, own, other_energy, other, slabs):
    orbs = 2 * own_energy.shape[0]
    width = -(-S * BW // LANES) * LANES
    return pl.pallas_call(
        grad_kernel,
        in_specs=[VMEM] * (4 + PARTS),
        out_specs=[VMEM] * 2,
        out_shape=[jax.ShapeDtypeStruct((orbs * S * BW // LANES, LANES), F32), jax.ShapeDtypeStruct((orbs, LANES), F32)],
        scratch_shapes=[pltpu.VMEM((width, LANES), F32)],
        compiler_params=pltpu.CompilerParams(vmem_limit_bytes=limit(orbs)),
    )(own_energy, own, other_energy, other, *slabs)


def seat_kernel(start, per_dev, rels, packed, out):
    me = lax.axis_index("aux")
    side = jnp.where(iota((1, LANES), 1) < BW, 0, 1)
    for d, rel in enumerate(rels):
        dev = lax.bitwise_xor(me, rel)
        row = packed[pl.ds(start + lax.div(dev, SEATS), 1), :]
        row = pltpu.roll(row, lax.rem(SEATS - lax.rem(dev, SEATS), SEATS) * SEAT, 1)
        row = row.astype(jnp.int32) - (1 + me * per_dev)
        ids = [jnp.broadcast_to(row[:, s : s + 1], (1, LANES)) for s in range(2 * TERM_TILES)]
        for k in range(TERM_TILES):
            one, two = ids[2 * k], ids[2 * k + 1]
            out[d * SEAT + 2 * k : d * SEAT + 2 * k + 1, :] = jnp.where(side == 0, one, two) - side
            out[d * SEAT + 2 * k + 1 : d * SEAT + 2 * k + 2, :] = jnp.where(side == 0, two, one) - side


def seats(packed, orbs, rows, rels):
    start = orbs // 8 * (BW + 1)
    return pl.pallas_call(
        functools.partial(seat_kernel, start, rows // BW, rels),
        in_specs=[VMEM],
        out_specs=VMEM,
        out_shape=jax.ShapeDtypeStruct((len(rels) * SEAT, LANES), jnp.int32),
        compiler_params=pltpu.CompilerParams(vmem_limit_bytes=2 * 2**20),
        cost_estimate=pl.CostEstimate(flops=0, bytes_accessed=2**20, transcendentals=0),
    )(packed)


def place_kernel(base, other, piece, spots, *refs):
    out = refs[-1]
    orbs, width = out.shape
    shift = 0
    if other:
        shift = jnp.where(lax.rem(lax.axis_index("aux"), 2) == 0, 1, -1) * (width // BW)
    mid = orbs // 2
    step_tiles = range(width // LANES)
    for first in range(0, orbs, 16):
        parts = [slice(r, r + 8) for r in range(first, min(first + 16, orbs), 8)]
        if len(refs) == 2:
            total = [[refs[0][r, t * LANES : (t + 1) * LANES] for t in step_tiles] for r in parts]
        else:
            total = [[jnp.zeros((8, LANES), F32) for _ in step_tiles] for _ in parts]

        def step(d, total, parts=parts):
            total = [list(row) for row in total]
            for k in range(TERM_TILES):
                at = (base + d) * SEAT + 2 * k
                spot = jnp.broadcast_to(spots[pl.ds(at, 1), :] - shift, (8, LANES))
                turn_spot = jnp.broadcast_to(spots[pl.ds(at + 1, 1), :] - shift, (8, LANES))
                values, turns = [], []
                for r in parts:
                    half = (k + 1) * LANES > S * BW
                    swapped = half and r.start >= mid
                    start = k * orbs + r.start - (mid if swapped else 0)
                    value = piece[d, start : start + 8, :]
                    turn = pltpu.roll(value, BW, 1)
                    values.append(turn if swapped else value)
                    turns.append(value if swapped else turn)
                for t in step_tiles:
                    here, there = spot == HALVES * t, turn_spot == HALVES * t
                    for r in range(len(parts)):
                        added = jnp.where(here, values[r], 0.0) + jnp.where(there, turns[r], 0.0)
                        total[r][t] = total[r][t] + added
            return total

        if piece.shape[0] <= 8:
            for d in range(piece.shape[0]):
                total = step(d, total)
        else:
            total = lax.fori_loop(0, piece.shape[0], step, total)
        for r, part in enumerate(parts):
            for t in step_tiles:
                out[part, t * LANES : (t + 1) * LANES] = total[r][t]


def place_terms(base, other, piece, spots, total, orbs, rows):
    args = (piece, spots) if total is None else (piece, spots, total)
    return pl.pallas_call(
        functools.partial(place_kernel, base, other),
        in_specs=[VMEM] * len(args),
        out_specs=VMEM,
        out_shape=jax.ShapeDtypeStruct((orbs, rows), F32),
        compiler_params=pltpu.CompilerParams(vmem_limit_bytes=8 * 2**20),
        cost_estimate=pl.CostEstimate(flops=0, bytes_accessed=4 * piece.size, transcendentals=0),
    )(*args)


def pair_kernel(slots, energy, out):
    for k in range(CAP):
        out[k] = jnp.sum(jnp.where(slots[...] == k, energy[...], 0.0))


def pair_slots(slots, energy):
    return pl.pallas_call(
        pair_kernel,
        in_specs=[VMEM] * 2,
        out_specs=SMEM,
        out_shape=jax.ShapeDtypeStruct((CAP,), F32),
        compiler_params=pltpu.CompilerParams(vmem_limit_bytes=2**20),
        cost_estimate=pl.CostEstimate(flops=0, bytes_accessed=2**20, transcendentals=0),
    )(slots, energy)


def swap(x, mask):
    size = lax.axis_size("aux")
    return lax.ppermute(x, "aux", [(i, i ^ mask) for i in range(size)])


def body(
    integrals, block_list, slot_counts, coefficients, batch_index, occ_energy, vir_energy, owner_map
):
    local_rows = coefficients.shape[0]
    size = lax.axis_size("aux")
    steps = stages(size, GATHER_COEF)
    x = jnp.transpose(integrals, (1, 0, 2))
    buf = coefficients.T[None]
    slabs, raw = [], None
    for k, step in enumerate(steps):
        far = [swap(buf, mask) for mask in step]
        if k == 0:
            ids, buf, slab, raw = prepare(block_list, slot_counts.reshape(1, 1), buf, x)
            slabs.append(slab)
        if k + 1 == len(steps):
            slab, raw = retile(x, 1, raw)
            slabs.append(slab)
        buf = jnp.concatenate([buf] + far, axis=0)
        buf, _ = lax.optimization_barrier((buf, slabs[-1]))
        x, raw, _ = lax.optimization_barrier((x, raw, far[0]))
    far = swap(buf, 1)
    slabs += retile(x, 2, raw)
    half, send = half_transform(steps + ((1,),), ids, buf, far, slabs)
    keep = own_squares(half, ids, send) + swap(send, 1)
    for k, step in enumerate(reversed(stages(size, SUM_INTS))):
        far = [swap(keep, mask) for mask in step]
        if k == 0:
            levels, slots = level_rows(batch_index, occ_energy.reshape(-1, LANES), owner_map)
        keep = sum(far, keep)
        keep, levels, slots = lax.optimization_barrier((keep, levels, slots))
    other = swap(keep, 1)
    vir = vir_energy.reshape(1, -1)
    own_energy, own = core_weights(False, keep, levels, vir, half)
    steps = stages(size, GATHER_TERMS)
    rels = [0]
    for step in steps:
        rels = rels + [rel ^ mask for mask in step for rel in rels]
    orbs = owner_map.shape[0]
    spots = seats(keep, orbs, local_rows, tuple(rels))
    other, spots = lax.optimization_barrier((other, spots))
    other_energy, other = core_weights(True, other, levels, vir, half)
    terms, energy = gradient_terms(own_energy, own, other_energy, other, slabs)
    buf, done, ours, theirs = terms[None], 0, None, None
    for k, step in enumerate(steps):
        far = [swap(buf, mask) for mask in step]
        piece = buf[done:]
        theirs = place_terms(done, True, piece, spots, theirs, orbs, local_rows)
        ours = place_terms(done, False, piece, spots, ours, orbs, local_rows)
        if k == 0:
            pair_energy = pair_slots(slots, energy)
            ours, pair_energy = lax.optimization_barrier((ours, pair_energy))
        done = buf.shape[0]
        if k + 1 < len(steps):
            buf = jnp.concatenate([buf] + far, axis=0)
            buf, ours, theirs = lax.optimization_barrier((buf, ours, theirs))
    for k, piece in enumerate(far):
        theirs = place_terms(done + k * piece.shape[0], True, piece, spots, theirs, orbs, local_rows)
    last = swap(theirs, 1)
    ours = place_terms(done, False, jnp.concatenate(far, axis=0), spots, ours, orbs, local_rows)
    grad_coef = (ours + last).T
    return (grad_coef, pair_energy)


def solution(mesh):
    return jax.shard_map(
        body,
        mesh=mesh,
        in_specs=(
            P(("groups", "aux"), None, None),
            P(("groups", "aux"), None),
            P(("groups", "aux")),
            P(("groups", "aux"), None),
            P("groups"),
            P("groups"),
            P("groups"),
            P("groups"),
        ),
        out_specs=(P(("groups", "aux"), None), P(("groups", "aux"))),
        check_vma=False,
    )
```

```python
import functools

import jax
import jax.numpy as jnp
from jax import lax
from jax.experimental import pallas as pl
from jax.experimental.pallas import tpu as pltpu
from jax.sharding import PartitionSpec as P

BW = 64
S = 5
CAP = 2
LANES = 128
HALVES = LANES // BW
TILES = BW * BW // LANES
ROWS = S * TILES
PARTS = 3
GATHER_COEF = (1, 2, 0)
SUM_INTS = (1, 0, 2)
GATHER_TERMS = (2, 0, 1)
SEAT = 8
SEATS = LANES // SEAT
TERM_TILES = -(-S * BW // LANES)
F32 = jnp.float32
BF16 = jnp.bfloat16
VMEM = pl.BlockSpec(memory_space=pltpu.VMEM)
SMEM = pl.BlockSpec(memory_space=pltpu.SMEM)


def limit(orbs):
    return max(8, orbs // 4) * 2**20


def iota(shape, dim):
    return lax.broadcasted_iota(jnp.int32, shape, dim)


def split_rows(count):
    unit = count // 16
    return (unit, 13 * unit, count - 14 * unit), (2 * unit, unit, 0)


def retile_rows(x, at, out, to):
    for s in range(S):
        out[to : to + 16, s * TILES : (s + 1) * TILES, :] = x[s, at : at + 16, :].reshape(16, TILES, LANES)


def fetch(start, x, slab, sems, first):
    copies = []
    for c in range(slab.shape[1] // 16):
        src = x.at[:, pl.ds(start + c * 16, 16), :]
        copies.append(pltpu.make_async_copy(src, slab.at[:, pl.ds(c * 16, 16), :], sems.at[first + c]))
        copies[-1].start()
    return copies


def retile_part(start, x, raw, out, ahead, slab, sems):
    have = 0 if raw is None else raw.shape[1]
    copies = fetch(start + have, x, slab, sems, 0)
    later = [] if ahead is None else fetch(start + out.shape[0], x, ahead, sems, len(copies))
    for c in range(have // 16):
        retile_rows(raw, c * 16, out, c * 16)
    for c, copy in enumerate(copies):
        copy.wait()
        retile_rows(slab, c * 16, out, have + c * 16)
    return later


def retile_kernel(start, x, raw, out, *refs):
    ahead = refs[0] if len(refs) == 3 else None
    slab, sems = refs[-2:]
    for copy in retile_part(start, x, raw, out, ahead, slab, sems):
        copy.wait()


def retile_shapes(count, part):
    sizes, ahead = split_rows(count)
    width = TILES * LANES
    have = ahead[part - 1] if part else 0
    out = [jax.ShapeDtypeStruct((sizes[part], ROWS, LANES), BF16)]
    if ahead[part]:
        out.append(jax.ShapeDtypeStruct((S, ahead[part], width), BF16))
    scratch = [
        pltpu.VMEM((S, sizes[part] - have, width), BF16),
        pltpu.SemaphoreType.DMA(((sizes[part] - have + ahead[part]) // 16,)),
    ]
    return sum(sizes[:part]), out, scratch


def retile(x, part, raw):
    start, out, scratch = retile_shapes(x.shape[1], part)
    return pl.pallas_call(
        functools.partial(retile_kernel, start),
        in_specs=[pl.BlockSpec(memory_space=pltpu.HBM), VMEM],
        out_specs=[VMEM] * len(out),
        out_shape=out,
        scratch_shapes=scratch,
        compiler_params=pltpu.CompilerParams(vmem_limit_bytes=10 * 2**20),
        cost_estimate=pl.CostEstimate(flops=0, bytes_accessed=4 * out[0].size, transcendentals=0),
    )(in_hbm(x), raw)


def prepare_kernel(blocks, counts, coef, x, ids, held, out, ahead, sems, own_blocks, slab, slab_sems):
    pairs = (blocks, own_blocks), (coef, held)
    copies = [pltpu.make_async_copy(src, dst, sems.at[k]) for k, (src, dst) in enumerate(pairs)]
    for copy in copies:
        copy.start()
    later = retile_part(0, x, None, out, ahead, slab, slab_sems)
    for copy in copies:
        copy.wait()
    lane = iota((1, LANES), 1)
    total = jnp.full(ids.shape, -1, jnp.int32)
    for s in range(S):
        total = jnp.where((lane == s) & (s < counts[...]), own_blocks[0, s], total)
    ids[...] = total
    for copy in later:
        copy.wait()


def in_hbm(x):
    return pltpu.with_memory_space_constraint(x, pltpu.HBM)


def prepare(blocks, counts, coef, x):
    far = pl.BlockSpec(memory_space=pltpu.HBM)
    _, out, scratch = retile_shapes(x.shape[1], 0)
    return pl.pallas_call(
        prepare_kernel,
        in_specs=[far, VMEM, far, far],
        out_specs=[VMEM] * 4,
        out_shape=[
            jax.ShapeDtypeStruct((1, LANES), jnp.int32),
            jax.ShapeDtypeStruct(coef.shape, coef.dtype),
        ]
        + out,
        scratch_shapes=[pltpu.SemaphoreType.DMA((2,)), pltpu.SMEM(blocks.shape, blocks.dtype)] + scratch,
        compiler_params=pltpu.CompilerParams(vmem_limit_bytes=8 * 2**20),
        cost_estimate=pl.CostEstimate(flops=0, bytes_accessed=4 * out[0].size, transcendentals=0),
    )(in_hbm(blocks), counts, in_hbm(coef), in_hbm(x))


def level_kernel(index, levels, owner, rows, slots, own_index, own_levels, held, sems):
    pairs = (index, own_index), (levels, own_levels), (owner, held)
    copies = [pltpu.make_async_copy(src, dst, sems.at[k]) for k, (src, dst) in enumerate(pairs)]
    for copy in copies:
        copy.start()
    for copy in copies:
        copy.wait()
    me = lax.axis_index("aux")
    lane = iota((1, LANES), 1)

    def step(i, rank):
        at = own_index[i]
        row = own_levels[pl.ds(lax.div(at, LANES), 1), :]
        rows[pl.ds(i, 1), :] = jnp.where(lane == lax.rem(at, LANES), 2.0 * row, 0.0)
        mine = held[i] == me
        slots[pl.ds(i, 1), :] = jnp.broadcast_to(jnp.where(mine, rank, -1), (1, LANES))
        return rank + jnp.where(mine, 1, 0)

    lax.fori_loop(0, rows.shape[0], step, jnp.int32(0))
    rows[...] = jnp.broadcast_to(jnp.sum(rows[...], axis=1, keepdims=True), rows.shape)


def level_rows(index, levels, owner):
    far = pl.BlockSpec(memory_space=pltpu.HBM)
    shape = (index.shape[0], LANES)
    return pl.pallas_call(
        level_kernel,
        in_specs=[far] * 3,
        out_specs=[VMEM] * 2,
        out_shape=[jax.ShapeDtypeStruct(shape, F32), jax.ShapeDtypeStruct(shape, jnp.int32)],
        scratch_shapes=[
            pltpu.SMEM(index.shape, index.dtype),
            pltpu.VMEM(levels.shape, levels.dtype),
            pltpu.SMEM(owner.shape, owner.dtype),
            pltpu.SemaphoreType.DMA((3,)),
        ],
        compiler_params=pltpu.CompilerParams(vmem_limit_bytes=2**20),
        cost_estimate=pl.CostEstimate(flops=0, bytes_accessed=2**20, transcendentals=0),
    )(in_hbm(index), in_hbm(levels), in_hbm(owner))


def stages(size, order):
    bits = []
    while size > 2:
        size //= 2
        bits.append(size)
    steps = [(bits.pop(0),)] if len(bits) % 2 else []
    for high, low in zip(bits[::2], bits[1::2]):
        both = (low, high, high ^ low)
        steps.append(tuple(both[k] for k in order))
    return tuple(steps)


def gather_index(dev, me, steps):
    rel = lax.bitwise_xor(dev, me)
    place, count = 0, 1
    for step in steps:
        bits = lax.bitwise_and(rel, functools.reduce(int.__or__, step))
        for k, mask in enumerate(step):
            place = place + jnp.where(bits == mask, (k + 1) * count, 0)
        count *= len(step) + 1
    return place


def half_kernel(steps, id_row, coef_a, coef_b, *refs):
    slabs, (half, send) = refs[:PARTS], refs[PARTS:]
    me = lax.axis_index("aux")
    orbs, width = coef_a.shape[1], coef_a.shape[2]
    per_dev = width // BW
    near = coef_a.shape[0]
    src = iota((LANES, LANES), 0)
    dst = iota((LANES, LANES), 1)
    wanted = (dst & BW) // BW + (dst & (TILES - 1)) * 2 + (dst & TILES) // TILES * BW
    spread = jnp.where(src == wanted, 1.0, 0.0).astype(BF16)
    ids = [id_row[0, s] for s in range(S)]
    picked = []
    for s in range(S):
        block = jnp.maximum(ids[s], 0)
        dev = lax.div(block, per_dev)
        inner = lax.rem(block, per_dev)
        place = gather_index(dev, me, steps)
        col = pl.multiple_of(lax.div(inner, HALVES) * LANES, LANES)
        spot = lax.rem(place, near)
        ours = coef_a[spot, :, pl.ds(col, LANES)]
        theirs = coef_b[spot, :, pl.ds(col, LANES)]
        picked.append(jnp.where(place < near, ours, theirs))
    apart = jnp.dot(jnp.concatenate(picked, axis=0), spread, preferred_element_type=F32)
    group = iota((orbs, LANES), 1) // TILES
    coef = [[jnp.zeros((orbs, LANES), F32) for _ in range(2)] for _ in range(HALVES)]
    for s in range(S):
        second = lax.rem(ids[s], HALVES) == 1
        value = apart[s * orbs : (s + 1) * orbs]
        value = jnp.where(second, pltpu.roll(value, LANES - TILES, 1), value)
        for h in range(HALVES):
            shift = (s * TILES - h * BW) % LANES
            there = pltpu.roll(value, shift, 1) if shift else value
            tile = s * TILES // LANES
            hit = (group == s % (LANES // TILES)) & (ids[s] >= 0)
            coef[h][tile] = jnp.where(hit, there, coef[h][tile])
    coef = jnp.concatenate([jnp.concatenate(coef[h], axis=1)[:, :ROWS] for h in range(HALVES)], axis=0).astype(BF16)
    low = iota((orbs, LANES), 1) < BW
    base = 0
    rows = []
    for slab in slabs:
        for p in range(slab.shape[0] // 2):
            both = jnp.concatenate([slab[2 * p], slab[2 * p + 1]], axis=1)
            r = jnp.dot(coef, both, preferred_element_type=F32)
            straight = jnp.where(low, r[:orbs, :LANES], r[orbs:, LANES:])
            crossed = jnp.where(low, r[:orbs, LANES:], r[orbs:, :LANES])
            rows.append(straight + pltpu.roll(crossed, BW, 1))
            if len(rows) == 16:
                half[:, base : base + 16, :] = jnp.swapaxes(jnp.stack(rows), 0, 1).astype(BF16)
                base, rows = base + 16, []
    pair_squares(half, 1 - lax.rem(me, 2), id_row, send)


def pair_squares(half, core, id_row, out):
    orbs, pairs = half.shape[0], half.shape[1]
    scale = 0.125 / (2 * pairs * lax.axis_size("aux"))
    lane = iota((BW, LANES), 1)
    left = lane < BW
    upper = iota((BW, LANES), 0) <= lax.rem(lane, BW)
    eye = iota((BW, LANES), 0) == lax.rem(lane, BW)
    quads = orbs // 8
    diags = []
    for k in range(quads):
        t = []
        for j in range(4):
            h = half[core * (orbs // 2) + 4 * k + j]
            t.append(lax.dot_general(h, h, (((0,), (0,)), ((), ())), preferred_element_type=F32) * scale)
        lefts = [t[j][:BW] + pltpu.roll(t[j][BW:], BW, 1) for j in (0, 1)]
        rights = [pltpu.roll(t[j][:BW], BW, 1) + t[j][BW:] for j in (2, 3)]
        a = jnp.where(left, lefts[0], rights[0])
        b = jnp.where(left, lefts[1], rights[1])
        out[k * BW : (k + 1) * BW, :] = jnp.where(upper, a, b)
        diags.append(jnp.sum(jnp.where(eye, b, 0.0), axis=0, keepdims=True))
    me = lax.axis_index("aux")
    spare = out.shape[0] - quads * BW - quads
    own = pltpu.roll((id_row[...] + 1).astype(F32), lax.rem(me, SEATS) * SEAT, 1)
    diags.append(jnp.where(iota((spare, LANES), 0) == lax.div(me, SEATS), own, 0.0))
    out[quads * BW :, :] = jnp.concatenate(diags, axis=0)


def own_kernel(half, id_row, out):
    pair_squares(half, lax.rem(lax.axis_index("aux"), 2), id_row, out)


def own_squares(half, ids, like):
    return pl.pallas_call(
        own_kernel,
        in_specs=[VMEM] * 2,
        out_specs=VMEM,
        out_shape=jax.ShapeDtypeStruct(like.shape, F32),
        compiler_params=pltpu.CompilerParams(vmem_limit_bytes=4 * 2**20),
        cost_estimate=pl.CostEstimate(flops=0, bytes_accessed=2 * 2**20, transcendentals=0),
    )(half, ids)


def half_transform(steps, ids, coef_a, coef_b, slabs):
    orbs = coef_a.shape[1]
    pairs = sum(s.shape[0] for s in slabs) // 2
    quads = orbs // 8
    rows = quads * BW + -(-(quads + -(-lax.axis_size("aux") // SEATS)) // 8) * 8
    packed = jax.ShapeDtypeStruct((rows, LANES), F32)
    return pl.pallas_call(
        functools.partial(half_kernel, steps),
        in_specs=[VMEM] * (3 + PARTS),
        out_specs=[VMEM] * 2,
        out_shape=[jax.ShapeDtypeStruct((orbs, pairs, LANES), BF16), packed],
        compiler_params=pltpu.CompilerParams(vmem_limit_bytes=limit(orbs)),
    )(ids, coef_a, coef_b, *slabs)


def weight_rows(packed, core, levels, vir, half, energy, weights):
    orbs, pairs = half.shape[0], half.shape[1]
    quads = orbs // 8
    lane = iota((BW, LANES), 1)
    row = iota((BW, LANES), 0)
    left = lane < BW
    inner = lax.rem(lane, BW)
    vir_b = jnp.concatenate([vir[...], vir[...]], axis=1)
    vir_a = jnp.sum(jnp.where((row == inner) & left, vir_b, 0.0), axis=1, keepdims=True)
    zero = jnp.zeros((BW, LANES), F32)
    scale = 0.5 / BW
    start = core * (orbs // 2)
    for k in range(0, quads, 2):
        squares = [packed[(k + j) * BW : (k + j + 1) * BW, :] for j in range(2)]
        turned = jnp.concatenate(squares, axis=0).T
        top, bottom = turned[:BW], turned[BW:]
        flips = [
            jnp.where(left, top, pltpu.roll(bottom, BW, 1)),
            jnp.where(left, pltpu.roll(top, BW, 1), bottom),
        ]
        for j in range(2):
            first = 4 * (k + j)
            diag = packed[quads * BW + k + j : quads * BW + k + j + 1, :]
            ints = [
                jnp.where(row <= inner, squares[j], flips[j]),
                jnp.where(row == inner, diag, jnp.where(row > inner, squares[j], flips[j])),
            ]
            for b in range(2):
                one, two = first + b, first + 2 + b
                level = jnp.where(left[:1], levels[pl.ds(start + one, 1), :], levels[pl.ds(start + two, 1), :])
                amps = ints[b] / ((level - vir_a) - vir_b)
                sums = jnp.sum(ints[b] * amps, axis=0, keepdims=True)
                energy[one : one + 1, :] = jnp.where(left[:1], sums, 0.0)
                energy[two : two + 1, :] = jnp.where(left[:1], 0.0, sums)
                turn = pltpu.roll(amps, BW, 1)
                for i, lows, highs in ((one, amps, turn), (two, turn, amps)):
                    square = jnp.concatenate([jnp.where(left, lows, zero), jnp.where(left, zero, highs)], axis=0)
                    w = jnp.dot(half[start + i], square.astype(BF16), preferred_element_type=F32) * scale
                    weights[i * pairs : (i + 1) * pairs, :] = w.astype(BF16).astype(F32)


def weight_kernel(other, packed, levels, vir, half, energy, weights):
    core = lax.rem(lax.axis_index("aux"), 2)
    weight_rows(packed, 1 - core if other else core, levels, vir, half, energy, weights)


def core_weights(other, packed, levels, vir, half):
    orbs, pairs = half.shape[0], half.shape[1]
    return pl.pallas_call(
        functools.partial(weight_kernel, other),
        in_specs=[VMEM] * 4,
        out_specs=[VMEM] * 2,
        out_shape=[
            jax.ShapeDtypeStruct((orbs // 2, LANES), F32),
            jax.ShapeDtypeStruct((orbs // 2 * pairs, LANES), F32),
        ],
        compiler_params=pltpu.CompilerParams(vmem_limit_bytes=4 * 2**20),
        cost_estimate=pl.CostEstimate(flops=0, bytes_accessed=3 * 2**20, transcendentals=0),
    )(packed, levels, vir, half)


def grad_kernel(own_energy, own, other_energy, other, *refs):
    slabs, (terms, energy, mixed) = refs[:PARTS], refs[PARTS:]
    core = lax.rem(lax.axis_index("aux"), 2)
    mid = own_energy.shape[0]
    orbs, pairs = 2 * mid, own.shape[0] // mid

    def ordered(ours, theirs):
        return jnp.concatenate([jnp.where(core == 0, ours, theirs), jnp.where(core == 0, theirs, ours)], axis=0)

    energy[...] = ordered(own_energy[...], other_energy[...])
    low = iota((orbs, LANES), 1) < BW
    blank = jnp.zeros((orbs, LANES), F32)
    total = jnp.zeros((ROWS, HALVES * orbs), F32)
    base = 0
    for slab in slabs:
        for start in range(0, slab.shape[0] // 2, 32):
            xs, ws = [], []
            for p in range(start, min(start + 32, slab.shape[0] // 2)):
                w = jnp.concatenate(
                    [
                        ref[pl.ds(g * 8 * pairs + base + p, 8, stride=pairs), :]
                        for ref in (own, other)
                        for g in range(mid // 8)
                    ],
                    axis=0,
                )
                turn = pltpu.roll(w, BW, 1)
                ws.append(jnp.concatenate([jnp.where(low, w, blank), jnp.where(low, blank, turn)], axis=0).astype(BF16))
                ws.append(jnp.concatenate([jnp.where(low, turn, blank), jnp.where(low, blank, w)], axis=0).astype(BF16))
                xs += [slab[2 * p], slab[2 * p + 1]]
            total = total + lax.dot_general(
                jnp.concatenate(xs, axis=1),
                jnp.concatenate(ws, axis=1),
                (((1,), (1,)), ((), ())),
                preferred_element_type=F32,
            )
        base += slab.shape[0] // 2
    width = mixed.shape[0]
    turn = total if HALVES * orbs > LANES else jnp.pad(total, ((0, 0), (0, LANES - HALVES * orbs)))
    for h in range(HALVES):
        rows = turn[:, h * orbs : h * orbs + LANES]
        if rows.shape[1] < LANES:
            rows = pltpu.roll(turn, LANES - h * orbs, 1)
        mixed[pl.ds(h, ROWS, stride=HALVES), :] = rows
    mixed[HALVES * ROWS :, :] = jnp.zeros((width - HALVES * ROWS, LANES), F32)
    for t in range(width // LANES):
        out = mixed[t * LANES : (t + 1) * LANES, :].T[:orbs]
        out = ordered(out[:mid], out[mid:])
        if (t + 1) * LANES > S * BW:
            out = jnp.where(low[:mid], out[:mid], pltpu.roll(out[mid:], BW, 1))
        terms[t * orbs : t * orbs + out.shape[0], :] = out


def gradient_terms(own_energy, own, other_energy, other, slabs):
    orbs = 2 * own_energy.shape[0]
    width = -(-S * BW // LANES) * LANES
    return pl.pallas_call(
        grad_kernel,
        in_specs=[VMEM] * (4 + PARTS),
        out_specs=[VMEM] * 2,
        out_shape=[jax.ShapeDtypeStruct((orbs * S * BW // LANES, LANES), F32), jax.ShapeDtypeStruct((orbs, LANES), F32)],
        scratch_shapes=[pltpu.VMEM((width, LANES), F32)],
        compiler_params=pltpu.CompilerParams(vmem_limit_bytes=limit(orbs)),
    )(own_energy, own, other_energy, other, *slabs)


def seat_kernel(start, per_dev, rels, packed, out):
    me = lax.axis_index("aux")
    side = jnp.where(iota((1, LANES), 1) < BW, 0, 1)
    for d, rel in enumerate(rels):
        dev = lax.bitwise_xor(me, rel)
        row = packed[pl.ds(start + lax.div(dev, SEATS), 1), :]
        row = pltpu.roll(row, lax.rem(SEATS - lax.rem(dev, SEATS), SEATS) * SEAT, 1)
        row = row.astype(jnp.int32) - (1 + me * per_dev)
        ids = [jnp.broadcast_to(row[:, s : s + 1], (1, LANES)) for s in range(2 * TERM_TILES)]
        for k in range(TERM_TILES):
            one, two = ids[2 * k], ids[2 * k + 1]
            out[d * SEAT + 2 * k : d * SEAT + 2 * k + 1, :] = jnp.where(side == 0, one, two) - side
            out[d * SEAT + 2 * k + 1 : d * SEAT + 2 * k + 2, :] = jnp.where(side == 0, two, one) - side


def seats(packed, orbs, rows, rels):
    start = orbs // 8 * (BW + 1)
    return pl.pallas_call(
        functools.partial(seat_kernel, start, rows // BW, rels),
        in_specs=[VMEM],
        out_specs=VMEM,
        out_shape=jax.ShapeDtypeStruct((len(rels) * SEAT, LANES), jnp.int32),
        compiler_params=pltpu.CompilerParams(vmem_limit_bytes=2 * 2**20),
        cost_estimate=pl.CostEstimate(flops=0, bytes_accessed=2**20, transcendentals=0),
    )(packed)


def place_kernel(base, other, piece, spots, *refs):
    out = refs[-1]
    orbs, width = out.shape
    shift = 0
    if other:
        shift = jnp.where(lax.rem(lax.axis_index("aux"), 2) == 0, 1, -1) * (width // BW)
    mid = orbs // 2
    step_tiles = range(width // LANES)
    for first in range(0, orbs, 16):
        parts = [slice(r, r + 8) for r in range(first, min(first + 16, orbs), 8)]
        if len(refs) == 2:
            total = [[refs[0][r, t * LANES : (t + 1) * LANES] for t in step_tiles] for r in parts]
        else:
            total = [[jnp.zeros((8, LANES), F32) for _ in step_tiles] for _ in parts]

        def step(d, total, parts=parts):
            total = [list(row) for row in total]
            for k in range(TERM_TILES):
                at = (base + d) * SEAT + 2 * k
                spot = jnp.broadcast_to(spots[pl.ds(at, 1), :] - shift, (8, LANES))
                turn_spot = jnp.broadcast_to(spots[pl.ds(at + 1, 1), :] - shift, (8, LANES))
                values, turns = [], []
                for r in parts:
                    half = (k + 1) * LANES > S * BW
                    swapped = half and r.start >= mid
                    start = k * orbs + r.start - (mid if swapped else 0)
                    value = piece[d, start : start + 8, :]
                    turn = pltpu.roll(value, BW, 1)
                    values.append(turn if swapped else value)
                    turns.append(value if swapped else turn)
                for t in step_tiles:
                    here, there = spot == HALVES * t, turn_spot == HALVES * t
                    for r in range(len(parts)):
                        added = jnp.where(here, values[r], 0.0) + jnp.where(there, turns[r], 0.0)
                        total[r][t] = total[r][t] + added
            return total

        if piece.shape[0] <= 8:
            for d in range(piece.shape[0]):
                total = step(d, total)
        else:
            total = lax.fori_loop(0, piece.shape[0], step, total)
        for r, part in enumerate(parts):
            for t in step_tiles:
                out[part, t * LANES : (t + 1) * LANES] = total[r][t]


def place_terms(base, other, piece, spots, total, orbs, rows):
    args = (piece, spots) if total is None else (piece, spots, total)
    return pl.pallas_call(
        functools.partial(place_kernel, base, other),
        in_specs=[VMEM] * len(args),
        out_specs=VMEM,
        out_shape=jax.ShapeDtypeStruct((orbs, rows), F32),
        compiler_params=pltpu.CompilerParams(vmem_limit_bytes=8 * 2**20),
        cost_estimate=pl.CostEstimate(flops=0, bytes_accessed=4 * piece.size, transcendentals=0),
    )(*args)


def pair_kernel(slots, energy, out):
    for k in range(CAP):
        out[k] = jnp.sum(jnp.where(slots[...] == k, energy[...], 0.0))


def pair_slots(slots, energy):
    return pl.pallas_call(
        pair_kernel,
        in_specs=[VMEM] * 2,
        out_specs=SMEM,
        out_shape=jax.ShapeDtypeStruct((CAP,), F32),
        compiler_params=pltpu.CompilerParams(vmem_limit_bytes=2**20),
        cost_estimate=pl.CostEstimate(flops=0, bytes_accessed=2**20, transcendentals=0),
    )(slots, energy)


def swap(x, mask):
    size = lax.axis_size("aux")
    return lax.ppermute(x, "aux", [(i, i ^ mask) for i in range(size)])


def body(
    integrals, block_list, slot_counts, coefficients, batch_index, occ_energy, vir_energy, owner_map
):
    local_rows = coefficients.shape[0]
    size = lax.axis_size("aux")
    steps = stages(size, GATHER_COEF)
    x = jnp.transpose(integrals, (1, 0, 2))
    buf = coefficients.T[None]
    slabs, raw = [], None
    for k, step in enumerate(steps):
        far = [swap(buf, mask) for mask in step]
        if k == 0:
            ids, buf, slab, raw = prepare(block_list, slot_counts.reshape(1, 1), buf, x)
            slabs.append(slab)
        if k + 1 == len(steps):
            slab, raw = retile(x, 1, raw)
            slabs.append(slab)
        buf = jnp.concatenate([buf] + far, axis=0)
        buf, _ = lax.optimization_barrier((buf, slabs[-1]))
        x, raw, _ = lax.optimization_barrier((x, raw, far[0]))
    far = swap(buf, 1)
    slabs += retile(x, 2, raw)
    half, send = half_transform(steps + ((1,),), ids, buf, far, slabs)
    keep = own_squares(half, ids, send) + swap(send, 1)
    for k, step in enumerate(reversed(stages(size, SUM_INTS))):
        far = [swap(keep, mask) for mask in step]
        if k == 0:
            levels, slots = level_rows(batch_index, occ_energy.reshape(-1, LANES), owner_map)
        keep = sum(far, keep)
        keep, levels, slots = lax.optimization_barrier((keep, levels, slots))
    other = swap(keep, 1)
    vir = vir_energy.reshape(1, -1)
    own_energy, own = core_weights(False, keep, levels, vir, half)
    steps = stages(size, GATHER_TERMS)
    rels = [0]
    for step in steps:
        rels = rels + [rel ^ mask for mask in step for rel in rels]
    orbs = owner_map.shape[0]
    spots = seats(keep, orbs, local_rows, tuple(rels))
    other, spots = lax.optimization_barrier((other, spots))
    other_energy, other = core_weights(True, other, levels, vir, half)
    terms, energy = gradient_terms(own_energy, own, other_energy, other, slabs)
    buf, done, ours, theirs = terms[None], 0, None, None
    for k, step in enumerate(steps):
        far = [swap(buf, mask) for mask in step]
        piece = buf[done:]
        theirs = place_terms(done, True, piece, spots, theirs, orbs, local_rows)
        ours = place_terms(done, False, piece, spots, ours, orbs, local_rows)
        if k == 0:
            pair_energy = pair_slots(slots, energy)
            ours, pair_energy = lax.optimization_barrier((ours, pair_energy))
        done = buf.shape[0]
        if k + 1 < len(steps):
            buf = jnp.concatenate([buf] + far, axis=0)
            buf, ours, theirs = lax.optimization_barrier((buf, ours, theirs))
    for k, piece in enumerate(far):
        theirs = place_terms(done + k * piece.shape[0], True, piece, spots, theirs, orbs, local_rows)
    last = swap(theirs, 1)
    ours = place_terms(done, False, jnp.concatenate(far, axis=0), spots, ours, orbs, local_rows)
    grad_coef = (ours + last).T
    return (grad_coef, pair_energy)


def solution(mesh):
    return jax.shard_map(
        body,
        mesh=mesh,
        in_specs=(
            P(("groups", "aux"), None, None),
            P(("groups", "aux"), None),
            P(("groups", "aux")),
            P(("groups", "aux"), None),
            P("groups"),
            P("groups"),
            P("groups"),
            P("groups"),
        ),
        out_specs=(P(("groups", "aux"), None), P(("groups", "aux"))),
        check_vma=False,
    )
```
